32 devices in a mesh: img: 8 (over y, x, core), row: 4 (over z).
Axes of the slice: x: 2, y: 2, z: 4, core: 2. Of those that a mesh axis runs over, the one named last changes fastest.
Arguments:
- tokens: bfloat16 [16, 1536, 1152], P('img', 'row'), may hold values from -6 to 6
- cotangent: bfloat16 [16, 1536, 1152], P('img', 'row'), may hold values from -0.03125 to 0.03125
- targets: bfloat16 [16, 1536, 768], P('img', 'row'), may hold values from -6 to 6
- time_table: bfloat16 [64, 1152], P(None, 'img'), may hold values from -6 to 6
- ada_weight: bfloat16 [1152, 6912], P('img'), may hold values from -0.1875 to 0.1875
- ada_bias: bfloat16 [6912], P('img'), may hold values from -3 to 3
- qkv_weight: bfloat16 [1152, 3456], P('img'), may hold values from -0.1875 to 0.1875
- out_weight: bfloat16 [1152, 1152], P('img'), may hold values from -2 to 2
- up_weight: bfloat16 [1152, 4608], P('img'), may hold values from -0.1875 to 0.1875
- up_bias: bfloat16 [4608], P('img'), may hold values from -3 to 3
- down_weight: bfloat16 [4608, 1152], P('img'), may hold values from -0.09375 to 0.09375
- proj_first: bfloat16 [1152, 2048], P('img'), may hold values from -0.1875 to 0.1875
- proj_second: bfloat16 [2048, 2048], P('img'), may hold values from -0.125 to 0.125
- proj_third: bfloat16 [2048, 768], P('img'), may hold values from -0.125 to 0.125
- time_bins: int32 [16], replicated, may hold values from 0 to 63
- image_order: int32 [16], P('img'), may hold values from 0 to 15, each once
- counts: int32 [16, 4], P('img'), may hold values from 1 to 12, 32 in all within a row
Outputs:
- block_out: bfloat16 [16, 1536, 1152], P('img', 'row')
- grad_tokens: bfloat16 [16, 1536, 1152], P('img', 'row')
- grad_time_table: float32 [64, 1152], P(None, 'img')
- grad_ada_weight: float32 [1152, 6912], P('img')
- grad_ada_bias: float32 [6912], P('img')
- grad_qkv_weight: float32 [1152, 3456], P('img')
- grad_out_weight: float32 [1152, 1152], P('img')
- grad_up_weight: float32 [1152, 4608], P('img')
- grad_up_bias: float32 [4608], P('img')
- grad_down_weight: float32 [4608, 1152], P('img')
- grad_proj_first: float32 [1152, 2048], P('img')
- grad_proj_second: float32 [2048, 2048], P('img')
- grad_proj_third: float32 [2048, 768], P('img')
The draws below stay inside these ranges and needn't reach their ends.
Inputs may be any that keep to these rules, and one draw needn't show every extreme that they name: `counts`: each row sums to 32; entry [i, r] is the number of latent rows of image slot i on index r of row, and some entry of every row equals 12.
All inputs are finite; a program needn't handle non-finite values.
Results may differ from the reference program's by a relative error of at most 0.035.
Values may be sent and summed in bfloat16 or wider, within the bound.
A program may use at most 384 MiB of HBM per device.

```python
import math
import jax
import jax.numpy as jnp
import numpy as np
from jax import lax

D = 1152
HEADS = 16
HDIM = 72
FF = 4608
PW = 2048
TD = 768
NBINS = 64
LROWS = 32
RW = 32
CAPR = 12
SLOT = 384
IMAGES = 16
N_ROW = 4


def with_ends(values, own_key, smallest, top_value):
    spot = [jax.random.randint(jax.random.fold_in(own_key, axis), (), 0, length) for axis, length in enumerate(values.shape)]
    widest = values.shape.index(max(values.shape))
    neighbour = spot[:widest] + [(spot[widest] + 1) % values.shape[widest]] + spot[widest + 1:]
    return values.at[tuple(spot)].set(smallest).at[tuple(neighbour)].set(top_value)


def with_spikes(entries, rng, source, target, blocks, factor):
    owner, partner = [(jnp.arange(entries.shape[axis_at]) // (entries.shape[axis_at] // blocks)).reshape([-1 if axis == axis_at else 1 for axis in range(entries.ndim)]) for axis_at in (source, target)]
    chosen = jax.random.permutation(rng, blocks)[partner]
    strong = (owner == chosen) | (owner == (partner + blocks // 2) % blocks)
    return jnp.where(strong, factor * entries, entries)


def block_levels(own_key, extent, cuts, least, high):
    level = 1.0
    for axis_at, shards_of in cuts:
        heights = jax.random.uniform(jax.random.fold_in(jax.random.fold_in(own_key, 6), axis_at), (shards_of,), jnp.float32, least / len(cuts), high / len(cuts))
        level = level * jnp.repeat(jnp.exp(heights), extent[axis_at] // shards_of).reshape((-1,) + (1,) * (len(extent) - 1 - axis_at))
    return level


def rank_table(amount, lean):
    portions = [(1 << 20) // math.isqrt(rank ** lean) + 1 for rank in range(1, amount + 1)]
    spread = 1 + sum(portions) // (1 << 30)
    return np.cumsum(np.array([max(1, weight // spread) for weight in portions]))


def ranked_ids(own_key, dims, amount, skew):
    table = rank_table(amount, skew)
    lot = jax.random.randint(jax.random.fold_in(own_key, 1), dims, 0, int(table[amount - 1]))
    grade = jnp.searchsorted(jnp.asarray(table, jnp.int32), lot, side="right")
    return jax.random.permutation(jax.random.fold_in(own_key, 2), amount)[grade].astype(jnp.int32)


def profile(amount, total, reach, slope):
    portions = [(1 << 20) // math.isqrt(rank ** slope) + 1 for rank in range(2, amount + 1)]
    surplus, given = total - reach - (amount - 1), [1] * (amount - 1)
    while surplus > 0:
        free = [i for i in range(amount - 1) if given[i] < reach]
        whole, budget = sum([portions[i] for i in free]), surplus
        for i in free:
            more = min(reach - given[i], max(1, budget * portions[i] // whole), surplus)
            given[i] = given[i] + more
            surplus = surplus - more
    return np.array([reach] + given)


def uneven(key, count, total, limit, skew):
    if count == 2:
        one = jax.random.randint(key, (), max(1, total - limit), min(limit, total - 1) + 1)
        return jnp.stack([one, total - one])
    lengths = jnp.asarray(profile(count, total, limit, skew), jnp.int32)
    pairs = (count - 1) // 2
    giver, taker = lengths[1:1 + 2 * pairs:2], lengths[2:2 + 2 * pairs:2]
    slack = jnp.minimum(giver - 1, limit - taker)
    moved = jax.random.randint(jax.random.fold_in(key, 1), (pairs,), 0, 1 << 20) % (slack + 1)
    lengths = lengths.at[1:1 + 2 * pairs:2].set(giver - moved).at[2:2 + 2 * pairs:2].set(taker + moved)
    return lengths[jax.random.permutation(jax.random.fold_in(key, 2), count)]


def centred(key, shape, width, limit, cuts=(), held_as=jnp.bfloat16):
    gain = block_levels(key, shape, cuts, -0.22, 0.18) if cuts else 1.0
    values = jax.random.normal(key, shape, jnp.float32) * width * gain
    return jnp.minimum(jnp.maximum(values, -limit), limit).astype(held_as)


def gaussian_with(stream_key, dims, deviation, most, shards, heavy, kind=jnp.bfloat16):
    entries = deviation * jax.random.normal(stream_key, dims, jnp.float32)
    if shards:
        entries = entries * block_levels(stream_key, dims, shards, -0.22, 0.18)
    return jnp.clip(with_spikes(entries, jax.random.fold_in(stream_key, 3), *heavy), -most, most).astype(kind)


def setup_inputs(seed: int = 0) -> dict:
    streams_of = jax.random.split(jax.random.key(seed), 18)
    tokens = gaussian_with(streams_of[0], (IMAGES, N_ROW * SLOT, D), 1.0, 6.0, ((0, 8), (1, 4)), (0, 2, 8, 2.0))
    cotangent = centred(streams_of[1], (IMAGES, N_ROW * SLOT, D), 0.005, 0.03125, ((0, 8), (1, 4)))
    targets = centred(streams_of[2], (IMAGES, N_ROW * SLOT, TD), 1.0, 6.0, ((0, 8), (1, 4)))
    time_table = centred(streams_of[3], (NBINS, D), 1.0, 6.0, ((1, 8),))
    ada_weight = centred(streams_of[4], (D, 6 * D), D ** -0.5, 0.1875, ((0, 8),))
    ada_bias = centred(streams_of[5], (6 * D,), 0.5, 3.0, ((0, 8),))
    qkv_weight = centred(streams_of[6], (D, 3 * D), D ** -0.5, 0.1875, ((0, 8),))
    out_weight = centred(streams_of[7], (D, D), (max(D * 8 // (LROWS * RW), 1)) ** -0.5, 2.0, ((0, 8),))
    up_weight = centred(streams_of[8], (D, FF), D ** -0.5, 0.1875, ((0, 8),))
    up_bias = centred(streams_of[9], (FF,), 0.5, 3.0, ((0, 8),))
    down_weight = centred(streams_of[10], (FF, D), FF ** -0.5, 0.09375, ((0, 8),))
    proj_first = centred(streams_of[11], (D, PW), D ** -0.5, 0.1875, ((0, 8),))
    proj_second = centred(streams_of[12], (PW, PW), PW ** -0.5, 0.125, ((0, 8),))
    proj_third = centred(streams_of[13], (PW, TD), PW ** -0.5, 0.125, ((0, 8),))
    time_bins = with_ends(ranked_ids(streams_of[14], (IMAGES,), NBINS, 2), jax.random.fold_in(streams_of[14], 3), 0, NBINS - 1).astype(jnp.int32)
    image_order = jax.random.permutation(streams_of[15], IMAGES).astype(jnp.int32)
    counts = jax.vmap(lambda own: uneven(own, N_ROW, LROWS, CAPR, 2))(jax.random.split(streams_of[16], IMAGES)).reshape((IMAGES, N_ROW)).astype(jnp.int32)
    return {"tokens": tokens, "cotangent": cotangent, "targets": targets, "time_table": time_table, "ada_weight": ada_weight, "ada_bias": ada_bias, "qkv_weight": qkv_weight, "out_weight": out_weight, "up_weight": up_weight, "up_bias": up_bias, "down_weight": down_weight, "proj_first": proj_first, "proj_second": proj_second, "proj_third": proj_third, "time_bins": time_bins, "image_order": image_order, "counts": counts}


@jax.custom_vjp
def low(v):
    return lax.optimization_barrier(v.astype(jnp.bfloat16)).astype(jnp.float32)

@jax.custom_vjp
def low_back(v):
    return v

def low_keep(v):
    return (low(v), None)

def low_pass(kept, grad):
    return (grad,)

def back_keep(v):
    return (v, None)

def back_low(kept, grad):
    return (low(grad),)
low.defvjp(low_keep, low_pass)
low_back.defvjp(back_keep, back_low)
highest = lax.Precision.HIGHEST

def both_ways(operand):
    return low_back(low(operand))

def normalize(operand):
    centre = operand - lax.optimization_barrier(jnp.mean(operand, axis=-1, keepdims=True))
    return centre * lax.rsqrt(lax.optimization_barrier(jnp.mean(centre * centre, axis=-1, keepdims=True)) + 1e-06)

def alignment(projected, targets):
    unit_proj = projected * lax.rsqrt(lax.optimization_barrier(jnp.mean(projected * projected, axis=-1, keepdims=True)) + 1e-06)
    unit_target = targets * lax.rsqrt(lax.optimization_barrier(jnp.mean(targets * targets, axis=-1, keepdims=True)) + 1e-06)
    return lax.optimization_barrier(jnp.mean(unit_proj * unit_target, axis=-1))

def image_objective(tokens_img, weights_all, cotangent_img, targets_img, bin_image, slot_valid):
    table, ada_w, ada_b, qkv_w, out_w, up_w, up_b, down_w, first_w, second_w, third_w = weights_all
    select = (jnp.arange(NBINS) == bin_image).astype(table.dtype)
    condition = jnp.dot(select, table, precision=highest)
    silu_cond = low(jax.nn.silu(condition))
    modulation = low_back(jnp.dot(silu_cond, ada_w, precision=highest) + ada_b)
    shift_att, scale_att, gate_att, shift_mlp, scale_mlp, gate_mlp = jnp.split(modulation, 6)
    length = tokens_img.shape[0]
    h_att = low(normalize(tokens_img) * (1.0 + scale_att) + shift_att)
    qkv_rows = jnp.dot(h_att, qkv_w, precision=highest)
    queries = both_ways(qkv_rows[:, :D]).reshape(length, HEADS, HDIM)
    key_rows = both_ways(qkv_rows[:, D:2 * D]).reshape(length, HEADS, HDIM)
    value_rows = both_ways(qkv_rows[:, 2 * D:]).reshape(length, HEADS, HDIM)
    scores = low_back(jnp.einsum('qhd,khd->hqk', queries, key_rows, precision=highest) * HDIM ** (-0.5))
    scores = jnp.where(slot_valid[None, None, :] > 0, scores, -1e+30)
    attn_prob = jax.nn.softmax(scores, axis=-1)
    head_mix = both_ways(jnp.einsum('hqk,khd->qhd', low(attn_prob), value_rows, precision=highest).reshape(length, D))
    attn_out = low_back(jnp.dot(head_mix, out_w, precision=highest))
    residual = tokens_img + gate_att * attn_out
    h_mlp = low(normalize(residual) * (1.0 + scale_mlp) + shift_mlp)
    pre_act = low_back(jnp.dot(h_mlp, up_w, precision=highest) + up_b)
    gelu_out = low(jax.nn.gelu(pre_act, approximate=True))
    mlp_out = low_back(jnp.dot(gelu_out, down_w, precision=highest))
    block_full = slot_valid[:, None] * (residual + gate_mlp * mlp_out)
    lin_one = low_back(jnp.dot(low(block_full), first_w, precision=highest))
    hid_one = low(jax.nn.silu(lin_one))
    lin_two = low_back(jnp.dot(hid_one, second_w, precision=highest))
    hid_two = low(jax.nn.silu(lin_two))
    projected = low_back(jnp.dot(hid_two, third_w, precision=highest))
    cosine = alignment(projected, targets_img)
    result = jnp.sum(block_full * cotangent_img) - 0.5 * jnp.sum(slot_valid * cosine)
    return (result, block_full)

def reference(tokens, cotangent, targets, time_table, ada_weight, ada_bias, qkv_weight, out_weight, up_weight, up_bias, down_weight, proj_first, proj_second, proj_third, time_bins, image_order, counts):
    weights_all = (time_table.astype(jnp.float32), ada_weight.astype(jnp.float32), ada_bias.astype(jnp.float32), qkv_weight.astype(jnp.float32), out_weight.astype(jnp.float32), up_weight.astype(jnp.float32), up_bias.astype(jnp.float32), down_weight.astype(jnp.float32), proj_first.astype(jnp.float32), proj_second.astype(jnp.float32), proj_third.astype(jnp.float32))
    slot_bins = time_bins[image_order]
    position = jnp.arange(N_ROW * SLOT)
    slot_valid = ((position % SLOT)[None, :] < counts[:, position // SLOT] * RW).astype(jnp.float32)

    def image_step(totals, image_items):
        tokens_img, cotangent_img, targets_img, bin_image, valid_img = image_items

        def objective(tokens_float, weights_float):
            return image_objective(tokens_float, weights_float, cotangent_img, targets_img, bin_image, valid_img)
        result, pull_back, block_full = jax.vjp(objective, tokens_img.astype(jnp.float32), weights_all, has_aux=True)
        grad_input, grad_weights = pull_back(jnp.ones_like(result))
        return (jax.tree.map(jnp.add, totals, grad_weights), (block_full.astype(jnp.bfloat16), grad_input.astype(jnp.bfloat16)))
    start_totals = jax.tree.map(jnp.zeros_like, weights_all)
    totals, (block_out, grad_tokens) = lax.scan(image_step, start_totals, (tokens, cotangent.astype(jnp.float32), targets.astype(jnp.float32), slot_bins, slot_valid))
    return (block_out, grad_tokens, totals[0], totals[1], totals[2], totals[3], totals[4], totals[5], totals[6], totals[7], totals[8], totals[9], totals[10])
```

```python
import functools

import jax
import jax.numpy as jnp
from jax import lax
from jax.experimental import pallas as pl
from jax.experimental.pallas import tpu as pltpu
from jax.sharding import PartitionSpec as P

HEADS = 16
HDIM = 72
RW = 32
LROWS = 32
TOTAL = LROWS * RW
SCALE = HDIM ** (-0.5)
LAST = (((1,), (1,)), ((), ()))
FIRST = (((0,), (0,)), ((), ()))


def normalize(operand):
    centre = operand - jnp.mean(operand, axis=-1, keepdims=True)
    return centre * lax.rsqrt(jnp.mean(centre * centre, axis=-1, keepdims=True) + 1e-06)


def modulate(operand, shift_row, scale_row):
    return normalize(operand) * (1.0 + scale_row) + shift_row


def alignment(projected, targets):
    unit_proj = projected * lax.rsqrt(
        jnp.mean(projected * projected, axis=-1, keepdims=True) + 1e-06
    )
    unit_target = targets * lax.rsqrt(jnp.mean(targets * targets, axis=-1, keepdims=True) + 1e-06)
    return jnp.mean(unit_proj * unit_target, axis=-1)


def matmul(left_side, right_side):
    return jnp.dot(left_side, right_side, preferred_element_type=jnp.float32)


def transposed(left_side, right_side):
    return lax.dot_general(left_side, right_side, LAST, preferred_element_type=jnp.float32)


def weight_grad(left_side, right_side):
    return lax.dot_general(left_side, right_side, FIRST, preferred_element_type=jnp.float32)


def silu_back(operand, gradient):
    return jax.vjp(jax.nn.silu, operand)[1](gradient)[0]


def gelu_tanh(operand):
    return jax.nn.gelu(operand, approximate=True)


def gelu_back(operand, gradient):
    return jax.vjp(gelu_tanh, operand)[1](gradient)[0]


def attend_kernel(q_ref, k_ref, v_ref, o_ref, lse_ref):
    length = q_ref.shape[1]
    block = min(256, length)
    keys, values = k_ref[0], v_ref[0]
    for at in range(0, length, block):
        rows = pl.ds(at, block)
        scores = lax.dot_general(q_ref[0, rows, :], keys, LAST, preferred_element_type=jnp.float32)
        scores = scores * SCALE
        top = jnp.max(scores, axis=1, keepdims=True)
        weight = jnp.exp(scores - top)
        total = jnp.sum(weight, axis=1, keepdims=True)
        mixed = jnp.dot(weight.astype(jnp.bfloat16), values, preferred_element_type=jnp.float32)
        o_ref[0, rows, :] = (mixed / total).astype(o_ref.dtype)
        log_total = jnp.broadcast_to(top + jnp.log(total), (block, 128))
        lse_ref[0, :, rows] = log_total.T[:1, :]


def attend(queries, keys, values):
    heads, length, width = queries.shape
    span = keys.shape[1]
    return pl.pallas_call(
        attend_kernel,
        grid=(heads,),
        in_specs=[
            pl.BlockSpec((1, length, width), lambda h: (h, 0, 0)),
            pl.BlockSpec((1, span, width), lambda h: (h, 0, 0)),
            pl.BlockSpec((1, span, width), lambda h: (h, 0, 0)),
        ],
        out_specs=[
            pl.BlockSpec((1, length, width), lambda h: (h, 0, 0)),
            pl.BlockSpec((1, 1, length), lambda h: (h, 0, 0)),
        ],
        out_shape=[
            jax.ShapeDtypeStruct((heads, length, width), jnp.bfloat16),
            jax.ShapeDtypeStruct((heads, 1, length), jnp.float32),
        ],
        compiler_params=pltpu.CompilerParams(vmem_limit_bytes=48 * 1024 * 1024),
        cost_estimate=pl.CostEstimate(
            flops=4 * heads * length * span * 256,
            bytes_accessed=4 * heads * (length + span) * 128,
            transcendentals=heads * length * span,
        ),
        name="attend",
    )(queries, keys, values)


def attend_back_kernel(q_ref, k_ref, v_ref, o_ref, d_ref, lse_ref, dq_ref, dk_ref, dv_ref):
    length, width = q_ref.shape[1], q_ref.shape[2]
    span = k_ref.shape[1]
    block = 256
    queries, d_mix = q_ref[0], d_ref[0]
    product = d_mix.astype(jnp.float32) * o_ref[0].astype(jnp.float32)
    delta = lax.dot_general(
        jnp.ones((8, width), jnp.float32),
        product,
        LAST,
        precision=lax.Precision.HIGHEST,
        preferred_element_type=jnp.float32,
    )[:1, :]
    log_total = lse_ref[0]
    d_query = jnp.zeros((length, width), jnp.float32)
    for at in range(0, span, block):
        rows = pl.ds(at, block)
        keys, values = k_ref[0, rows, :], v_ref[0, rows, :]
        scores = lax.dot_general(keys, queries, LAST, preferred_element_type=jnp.float32) * SCALE
        prob = jnp.exp(scores - log_total)
        d_prob = lax.dot_general(values, d_mix, LAST, preferred_element_type=jnp.float32)
        d_score = (prob * (d_prob - delta)).astype(jnp.bfloat16)
        dv_ref[0, rows, :] = jnp.dot(
            prob.astype(jnp.bfloat16), d_mix, preferred_element_type=jnp.float32
        ).astype(dv_ref.dtype)
        dk_ref[0, rows, :] = (
            jnp.dot(d_score, queries, preferred_element_type=jnp.float32) * SCALE
        ).astype(dk_ref.dtype)
        d_query += lax.dot_general(d_score, keys, FIRST, preferred_element_type=jnp.float32)
    dq_ref[0] = (d_query * SCALE).astype(dq_ref.dtype)


def attend_back(queries, keys, values, mixed, d_mix, log_total):
    heads, length, width = queries.shape
    span = keys.shape[1]
    short = pl.BlockSpec((1, length, width), lambda h: (h, 0, 0))
    long = pl.BlockSpec((1, span, width), lambda h: (h, 0, 0))
    return pl.pallas_call(
        attend_back_kernel,
        grid=(heads,),
        in_specs=[
            short,
            long,
            long,
            short,
            short,
            pl.BlockSpec((1, 1, length), lambda h: (h, 0, 0)),
        ],
        out_specs=[short, long, long],
        out_shape=[
            jax.ShapeDtypeStruct((heads, length, width), jnp.bfloat16),
            jax.ShapeDtypeStruct((heads, span, width), jnp.bfloat16),
            jax.ShapeDtypeStruct((heads, span, width), jnp.bfloat16),
        ],
        compiler_params=pltpu.CompilerParams(vmem_limit_bytes=48 * 1024 * 1024),
        cost_estimate=pl.CostEstimate(
            flops=10 * heads * length * span * 256,
            bytes_accessed=10 * heads * (length + span) * 128,
            transcendentals=heads * length * span,
        ),
        name="attend_back",
    )(queries, keys, values, mixed, d_mix, log_total)


def split_heads(operand):
    return operand.reshape(operand.shape[0], HEADS, HDIM).transpose(1, 0, 2)


def join_heads(operand):
    return operand.transpose(1, 0, 2).reshape(operand.shape[1], HEADS * HDIM)


def local(
    n_img,
    n_row,
    tokens,
    cotangent,
    targets,
    time_table,
    ada_weight,
    ada_bias,
    qkv_weight,
    out_weight,
    up_weight,
    up_bias,
    down_weight,
    proj_first,
    proj_second,
    proj_third,
    time_bins,
    image_order,
    counts,
):
    f32, bf16 = jnp.float32, jnp.bfloat16
    per, slot_len, width = tokens.shape
    column = 2 * per
    group = n_row // column
    length = TOTAL // (2 * group)
    n_images = time_bins.shape[0]
    img_rank, row_rank = lax.axis_index("img"), lax.axis_index("row")
    core = img_rank % 2
    place = row_rank // group
    receives = place // per == core

    def swap(operand, axis, bit):
        size = n_img if axis == "img" else n_row
        return lax.ppermute(operand, axis, [(at, at ^ bit) for at in range(size)])

    def route(shift, back):
        pairs = [
            (img * n_row + (row + shift) % n_row, img * n_row + row)
            for img in range(n_img)
            for row in range(n_row)
            if (row // group) // per == img % 2
        ]
        return [(b, a) for a, b in pairs] if back else pairs

    own_counts = lax.dynamic_index_in_dim(counts, place % per, 0, keepdims=False)
    first_of = (jnp.cumsum(own_counts) - own_counts) * RW
    position = jnp.arange(slot_len)
    kept = (row_rank % group) * 2 * length + jnp.arange(2 * length)
    picks = []
    for shift in range(n_row):
        source_row = (row_rank + shift) % n_row
        begin = lax.dynamic_index_in_dim(first_of, source_row, 0, keepdims=False)
        limit = lax.dynamic_index_in_dim(own_counts, source_row, 0, keepdims=False) * RW
        hit = (kept[:, None] == begin + position[None, :]) & (position[None, :] < limit)
        picks.append(hit)
    pick = jnp.concatenate(picks, axis=1).astype(bf16)

    def image_of(shift):
        return (((row_rank - shift) % n_row) // group) % per

    def bring(operand):
        pieces = []
        for shift in range(n_row):
            piece = lax.dynamic_index_in_dim(operand, image_of(shift), 0, keepdims=False)
            if shift:
                piece = lax.ppermute(piece, ("img", "row"), route(shift, False))
            pieces.append(piece)
        packed = matmul(pick, jnp.concatenate(pieces, axis=0)).astype(bf16)
        own = lax.dynamic_slice_in_dim(packed, core * length, length, 0)
        other = lax.dynamic_slice_in_dim(packed, (1 - core) * length, length, 0)
        return jnp.where(receives, own, swap(other, "img", 1))

    def give(operand):
        other = swap(operand, "img", 1)
        both = jnp.where(
            core == 0,
            jnp.concatenate([operand, other], axis=0),
            jnp.concatenate([other, operand], axis=0),
        )
        spread = weight_grad(pick, both).astype(bf16)
        images = [jnp.zeros((slot_len, operand.shape[1]), bf16) for _ in range(per)]
        for shift in range(n_row):
            piece = spread[shift * slot_len : (shift + 1) * slot_len]
            if shift:
                piece = lax.ppermute(piece, ("img", "row"), route(shift, True))
            else:
                piece = jnp.where(receives, piece, jnp.zeros_like(piece))
            images = [
                image + jnp.where(image_of(shift) == at, piece, jnp.zeros_like(piece))
                for at, image in enumerate(images)
            ]
        return jnp.stack(images)

    def fetch(operand):
        return lax.all_gather(operand, "img", axis=0, tiled=True)

    order = lax.all_gather(image_order, "img", axis=0, tiled=True)
    chosen = jnp.sum(
        jnp.where(order[:, None] == jnp.arange(n_images)[None, :], time_bins[None, :], 0), axis=1
    )
    select = (chosen[:, None] == jnp.arange(time_table.shape[0])[None, :]).astype(f32)
    condition = jnp.dot(select, time_table.astype(f32), precision=lax.Precision.HIGHEST)
    silu_cond = jax.nn.silu(condition).astype(bf16)
    row_cond = lax.dynamic_index_in_dim(
        silu_cond.reshape(n_img // 2, column, -1), place, 1, keepdims=False
    )
    mod_width = ada_weight.shape[1]
    ff_width = up_weight.shape[1]
    bias_part = lax.dynamic_update_slice(
        jnp.zeros((mod_width,), f32), ada_bias.astype(f32), (img_rank * ada_bias.shape[0],)
    )
    up_bias_part = lax.dynamic_update_slice(
        jnp.zeros((ff_width,), f32), up_bias.astype(f32), (img_rank * up_bias.shape[0],)
    )
    mod_part = matmul(row_cond, ada_weight) + bias_part[None, :]
    summed_rows = lax.psum(jnp.concatenate([mod_part.reshape(-1), up_bias_part]), "img")
    modulation = lax.dynamic_index_in_dim(
        summed_rows[: (n_img // 2) * mod_width].reshape(n_img // 2, mod_width),
        img_rank // 2,
        0,
        keepdims=True,
    )
    up_bias_full = summed_rows[(n_img // 2) * mod_width :]
    shift_att, scale_att, gate_att, shift_mlp, scale_mlp, gate_mlp = jnp.split(
        modulation, 6, axis=1
    )

    qkv_full = fetch(qkv_weight)
    out_full = fetch(out_weight)
    up_full = fetch(up_weight)
    down_full = fetch(down_weight)
    first_full = fetch(proj_first)
    second_full = fetch(proj_second)
    third_full = fetch(proj_third)

    source = bring(tokens).astype(f32)
    outside = bring(jnp.concatenate([cotangent, targets], axis=2))
    own_cotangent = outside[:, :width].astype(f32)
    own_targets = outside[:, width:].astype(f32)

    h_att = modulate(source, shift_att, scale_att).astype(bf16)
    qkv_rows = matmul(h_att, qkv_full).astype(bf16)
    key_value = qkv_rows[:, width:]
    key_value = jnp.concatenate([key_value, swap(key_value, "img", 1)], axis=0)
    bits = [1 << at for at in range(group.bit_length() - 1)]
    for bit in bits:
        key_value = jnp.concatenate([key_value, swap(key_value, "row", bit)], axis=0)
    queries = split_heads(qkv_rows[:, :width])
    keys = split_heads(key_value[:, :width])
    values = split_heads(key_value[:, width:])
    mixed, log_total = attend(queries, keys, values)
    head_mix = join_heads(mixed)
    attn_out = matmul(head_mix, out_full)
    residual = source + gate_att * attn_out
    h_mlp = modulate(residual, shift_mlp, scale_mlp).astype(bf16)
    pre_act = matmul(h_mlp, up_full) + up_bias_full
    gelu_out = gelu_tanh(pre_act).astype(bf16)
    mlp_out = matmul(gelu_out, down_full)
    block_own = (residual + gate_mlp * mlp_out).astype(bf16)
    block_out = give(block_own)
    lin_one = matmul(block_own, first_full)
    hid_one = jax.nn.silu(lin_one).astype(bf16)
    lin_two = matmul(hid_one, second_full)
    hid_two = jax.nn.silu(lin_two).astype(bf16)
    projected = matmul(hid_two, third_full)

    def align_loss(operand):
        return -0.5 * jnp.sum(alignment(operand, own_targets))

    def scatter(grad):
        part = lax.psum_scatter(grad.astype(bf16), "img", scatter_dimension=0, tiled=True)
        part = part.astype(f32)
        for at in range(n_row.bit_length() - 1):
            part = part + swap(part.astype(bf16), "row", 1 << at).astype(f32)
        return part

    d_proj = jax.vjp(align_loss, projected)[1](jnp.ones((), f32))[0].astype(bf16)
    grad_third = scatter(weight_grad(hid_two, d_proj))
    d_lin_two = silu_back(lin_two, transposed(d_proj, third_full)).astype(bf16)
    grad_second = scatter(weight_grad(hid_one, d_lin_two))
    d_lin_one = silu_back(lin_one, transposed(d_lin_two, second_full)).astype(bf16)
    grad_first = scatter(weight_grad(block_own, d_lin_one))
    d_res = own_cotangent + transposed(d_lin_one, first_full)
    d_gate_mlp = jnp.sum(d_res * mlp_out, axis=0)
    d_mlp = (d_res * gate_mlp).astype(bf16)
    grad_down = scatter(weight_grad(gelu_out, d_mlp))
    d_pre = gelu_back(pre_act, transposed(d_mlp, down_full)).astype(bf16)
    bias_sum = jnp.sum(d_pre.astype(f32), axis=0)
    grad_up = scatter(weight_grad(h_mlp, d_pre))
    d_resid_norm, d_shift_mlp, d_scale_mlp = jax.vjp(modulate, residual, shift_mlp, scale_mlp)[1](
        transposed(d_pre, up_full)
    )
    d_residual = d_res + d_resid_norm
    d_gate_att = jnp.sum(d_residual * attn_out, axis=0)
    d_attn = (d_residual * gate_att).astype(bf16)
    grad_out = scatter(weight_grad(head_mix, d_attn))
    d_mixed = transposed(d_attn, out_full).astype(bf16)
    d_query, d_key, d_value = attend_back(
        queries, keys, values, mixed, split_heads(d_mixed), log_total
    )
    d_key_value = jnp.concatenate([join_heads(d_key), join_heads(d_value)], axis=1)
    for axis, bit in [("row", bit) for bit in reversed(bits)] + [("img", 1)]:
        half = d_key_value.shape[0] // 2
        arrived = swap(d_key_value[half:], axis, bit)
        d_key_value = (d_key_value[:half].astype(f32) + arrived.astype(f32)).astype(bf16)
    d_qkv = jnp.concatenate([join_heads(d_query), d_key_value], axis=1)
    grad_qkv = scatter(weight_grad(h_att, d_qkv))
    d_source, d_shift_att, d_scale_att = jax.vjp(modulate, source, shift_att, scale_att)[1](
        transposed(d_qkv, qkv_full)
    )
    grad_tokens = give((d_residual + d_source).astype(bf16))

    own_mod = jnp.concatenate(
        [d_shift_att[0], d_scale_att[0], d_gate_att, d_shift_mlp[0], d_scale_mlp[0], d_gate_mlp]
    )[None, :]
    own_mod = own_mod + swap(own_mod, "img", 1)
    for bit in bits:
        own_mod = own_mod + swap(own_mod, "row", bit)
    own_mod = own_mod.astype(bf16)
    column_mod = lax.all_gather(own_mod, "row", axis=0, tiled=True)[::group]
    same_core = [[2 * at + side for at in range(n_img // 2)] for side in range(2)]
    d_mod = lax.all_gather(
        column_mod, "img", axis=0, tiled=True, axis_index_groups=same_core
    )
    grad_ada = weight_grad(silu_cond, d_mod)
    grad_ada_bias = jnp.sum(
        lax.dynamic_slice_in_dim(d_mod, img_rank * ada_bias.shape[0], ada_bias.shape[0], 1).astype(
            f32
        ),
        axis=0,
    )
    d_cond = silu_back(condition, transposed(d_mod, ada_weight))
    grad_table = jnp.dot(select.T, d_cond, precision=lax.Precision.HIGHEST)
    grad_up_bias = lax.dynamic_slice_in_dim(
        lax.psum(bias_sum, ("img", "row")), img_rank * up_bias.shape[0], up_bias.shape[0], 0
    )
    return (
        block_out,
        grad_tokens,
        grad_table,
        grad_ada,
        grad_ada_bias,
        grad_qkv,
        grad_out,
        grad_up,
        grad_up_bias,
        grad_down,
        grad_first,
        grad_second,
        grad_third,
    )


def solution(mesh):
    return jax.shard_map(
        functools.partial(local, mesh.shape["img"], mesh.shape["row"]),
        mesh=mesh,
        in_specs=(
            P("img", "row", None),
            P("img", "row", None),
            P("img", "row", None),
            P(None, "img"),
            P("img", None),
            P("img"),
            P("img", None),
            P("img", None),
            P("img", None),
            P("img"),
            P("img", None),
            P("img", None),
            P("img", None),
            P("img", None),
            P(),
            P("img"),
            P("img", None),
        ),
        out_specs=(
            P("img", "row", None),
            P("img", "row", None),
            P(None, "img"),
            P("img", None),
            P("img"),
            P("img", None),
            P("img", None),
            P("img", None),
            P("img"),
            P("img", None),
            P("img", None),
            P("img", None),
            P("img", None),
        ),
        check_vma=False,
    )
```

```python
import functools

import jax
import jax.numpy as jnp
from jax import lax
from jax.experimental import pallas as pl
from jax.experimental.pallas import tpu as pltpu
from jax.sharding import PartitionSpec as P

HEADS = 16
HDIM = 72
RW = 32
LROWS = 32
TOTAL = LROWS * RW
SCALE = HDIM ** (-0.5)
LAST = (((1,), (1,)), ((), ()))
FIRST = (((0,), (0,)), ((), ()))


def normalize(operand):
    centre = operand - jnp.mean(operand, axis=-1, keepdims=True)
    return centre * lax.rsqrt(jnp.mean(centre * centre, axis=-1, keepdims=True) + 1e-06)


def modulate(operand, shift_row, scale_row):
    return normalize(operand) * (1.0 + scale_row) + shift_row


def alignment(projected, targets):
    unit_proj = projected * lax.rsqrt(
        jnp.mean(projected * projected, axis=-1, keepdims=True) + 1e-06
    )
    unit_target = targets * lax.rsqrt(jnp.mean(targets * targets, axis=-1, keepdims=True) + 1e-06)
    return jnp.mean(unit_proj * unit_target, axis=-1)


def matmul(left_side, right_side):
    return jnp.dot(left_side, right_side, preferred_element_type=jnp.float32)


def transposed(left_side, right_side):
    return lax.dot_general(left_side, right_side, LAST, preferred_element_type=jnp.float32)


def weight_grad(left_side, right_side):
    return lax.dot_general(left_side, right_side, FIRST, preferred_element_type=jnp.float32)


def silu_back(operand, gradient):
    return jax.vjp(jax.nn.silu, operand)[1](gradient)[0]


def gelu_tanh(operand):
    return jax.nn.gelu(operand, approximate=True)


def gelu_back(operand, gradient):
    return jax.vjp(gelu_tanh, operand)[1](gradient)[0]


def attend_kernel(q_ref, k_ref, v_ref, o_ref, lse_ref):
    length = q_ref.shape[1]
    block = min(256, length)
    keys, values = k_ref[0], v_ref[0]
    for at in range(0, length, block):
        rows = pl.ds(at, block)
        scores = lax.dot_general(q_ref[0, rows, :], keys, LAST, preferred_element_type=jnp.float32)
        scores = scores * SCALE
        top = jnp.max(scores, axis=1, keepdims=True)
        weight = jnp.exp(scores - top)
        total = jnp.sum(weight, axis=1, keepdims=True)
        mixed = jnp.dot(weight.astype(jnp.bfloat16), values, preferred_element_type=jnp.float32)
        o_ref[0, rows, :] = (mixed / total).astype(o_ref.dtype)
        log_total = jnp.broadcast_to(top + jnp.log(total), (block, 128))
        lse_ref[0, :, rows] = log_total.T[:1, :]


def attend(queries, keys, values):
    heads, length, width = queries.shape
    span = keys.shape[1]
    return pl.pallas_call(
        attend_kernel,
        grid=(heads,),
        in_specs=[
            pl.BlockSpec((1, length, width), lambda h: (h, 0, 0)),
            pl.BlockSpec((1, span, width), lambda h: (h, 0, 0)),
            pl.BlockSpec((1, span, width), lambda h: (h, 0, 0)),
        ],
        out_specs=[
            pl.BlockSpec((1, length, width), lambda h: (h, 0, 0)),
            pl.BlockSpec((1, 1, length), lambda h: (h, 0, 0)),
        ],
        out_shape=[
            jax.ShapeDtypeStruct((heads, length, width), jnp.bfloat16),
            jax.ShapeDtypeStruct((heads, 1, length), jnp.float32),
        ],
        compiler_params=pltpu.CompilerParams(vmem_limit_bytes=48 * 1024 * 1024),
        cost_estimate=pl.CostEstimate(
            flops=4 * heads * length * span * 256,
            bytes_accessed=4 * heads * (length + span) * 128,
            transcendentals=heads * length * span,
        ),
        name="attend",
    )(queries, keys, values)


def attend_back_kernel(q_ref, k_ref, v_ref, o_ref, d_ref, lse_ref, dq_ref, dk_ref, dv_ref):
    length, width = q_ref.shape[1], q_ref.shape[2]
    span = k_ref.shape[1]
    block = 256
    queries, d_mix = q_ref[0], d_ref[0]
    product = d_mix.astype(jnp.float32) * o_ref[0].astype(jnp.float32)
    delta = lax.dot_general(
        jnp.ones((8, width), jnp.float32),
        product,
        LAST,
        precision=lax.Precision.HIGHEST,
        preferred_element_type=jnp.float32,
    )[:1, :]
    log_total = lse_ref[0]
    d_query = jnp.zeros((length, width), jnp.float32)
    for at in range(0, span, block):
        rows = pl.ds(at, block)
        keys, values = k_ref[0, rows, :], v_ref[0, rows, :]
        scores = lax.dot_general(keys, queries, LAST, preferred_element_type=jnp.float32) * SCALE
        prob = jnp.exp(scores - log_total)
        d_prob = lax.dot_general(values, d_mix, LAST, preferred_element_type=jnp.float32)
        d_score = (prob * (d_prob - delta)).astype(jnp.bfloat16)
        dv_ref[0, rows, :] = jnp.dot(
            prob.astype(jnp.bfloat16), d_mix, preferred_element_type=jnp.float32
        ).astype(dv_ref.dtype)
        dk_ref[0, rows, :] = (
            jnp.dot(d_score, queries, preferred_element_type=jnp.float32) * SCALE
        ).astype(dk_ref.dtype)
        d_query += lax.dot_general(d_score, keys, FIRST, preferred_element_type=jnp.float32)
    dq_ref[0] = (d_query * SCALE).astype(dq_ref.dtype)


def attend_back(queries, keys, values, mixed, d_mix, log_total):
    heads, length, width = queries.shape
    span = keys.shape[1]
    short = pl.BlockSpec((1, length, width), lambda h: (h, 0, 0))
    long = pl.BlockSpec((1, span, width), lambda h: (h, 0, 0))
    return pl.pallas_call(
        attend_back_kernel,
        grid=(heads,),
        in_specs=[
            short,
            long,
            long,
            short,
            short,
            pl.BlockSpec((1, 1, length), lambda h: (h, 0, 0)),
        ],
        out_specs=[short, long, long],
        out_shape=[
            jax.ShapeDtypeStruct((heads, length, width), jnp.bfloat16),
            jax.ShapeDtypeStruct((heads, span, width), jnp.bfloat16),
            jax.ShapeDtypeStruct((heads, span, width), jnp.bfloat16),
        ],
        compiler_params=pltpu.CompilerParams(vmem_limit_bytes=48 * 1024 * 1024),
        cost_estimate=pl.CostEstimate(
            flops=10 * heads * length * span * 256,
            bytes_accessed=10 * heads * (length + span) * 128,
            transcendentals=heads * length * span,
        ),
        name="attend_back",
    )(queries, keys, values, mixed, d_mix, log_total)


MESH = pl.DeviceIdType.MESH
TILE_ROWS = 144
TILE_COLUMNS = 384
CUT = 80
SLOTS = 4
LINE_SLOTS = 8
LINE_TILE = 256
SIDE_PACE = 3
GIVE_ROWS = 16


def add(one, other):
    return (one.astype(jnp.float32) + other.astype(jnp.float32)).astype(jnp.bfloat16)


def mates():
    me = lax.axis_index("img")
    core, x, y = lax.rem(me, 2), lax.rem(me // 2, 2), me // 4
    return me, (core, x, y), (me + 1 - 2 * core, me + 2 - 4 * x, me + 4 - 8 * y)


def greet(where):
    barrier = pltpu.get_barrier_semaphore()
    pl.semaphore_signal(barrier, inc=1, device_id=where, device_id_type=MESH)


def gather_kernel(count, *refs):
    blocks, wholes = refs[:count], refs[count : 2 * count]
    send_sem, recv_sem, local_sem = refs[2 * count :]
    me, (core, x, y), (sibling, x_mate, y_mate) = mates()
    far = x_mate + 4 - 8 * y
    for mate in (sibling, x_mate, y_mate):
        greet({"img": mate})
    pl.semaphore_wait(pltpu.get_barrier_semaphore(), 3)

    def halves(at):
        rows = blocks[at].shape[0]
        cut = (rows // 2 + 15) // 16 * 16
        return pl.ds(0, cut), pl.ds(cut, rows - cut)

    def copy(at, kind, source, owner, rows, where):
        return pltpu.make_async_remote_copy(
            src_ref=source,
            dst_ref=wholes[at].at[owner, rows, :],
            send_sem=send_sem.at[at, kind],
            recv_sem=recv_sem.at[at, kind],
            device_id={"img": where},
            device_id_type=MESH,
        )

    def copies(at):
        upper, lower = halves(at)
        block, whole = blocks[at], wholes[at]
        found = [
            copy(at, 0, block.at[upper, :], me, upper, x_mate),
            copy(at, 1, block.at[lower, :], me, lower, y_mate),
            copy(at, 2, block.at[upper, :], me, upper, y_mate),
            copy(at, 3, block.at[lower, :], me, lower, x_mate),
            copy(at, 4, whole.at[x_mate, upper, :], x_mate, upper, y_mate),
            copy(at, 5, whole.at[y_mate, lower, :], y_mate, lower, x_mate),
            copy(at, 6, block.at[upper, :], me, upper, sibling),
            copy(at, 7, block.at[lower, :], me, lower, sibling),
        ]
        for kind, (owner, rows) in enumerate(
            [
                (x_mate, upper),
                (y_mate, lower),
                (y_mate, upper),
                (x_mate, lower),
                (far, upper),
                (far, lower),
            ]
        ):
            found.append(copy(at, 8 + kind, whole.at[owner, rows, :], owner, rows, sibling))
        return found

    every = [copies(at) for at in range(count)]
    locals_ = [
        pltpu.make_async_copy(blocks[at], wholes[at].at[me], local_sem.at[at])
        for at in range(count)
    ]
    for at in range(count):
        for kind in (0, 1, 6, 7):
            every[at][kind].start()
        locals_[at].start()
    for at in range(count):
        found = every[at]
        found[0].wait_recv()
        found[4].start()
        found[2].start()
        found[8].start()
        found[1].wait_recv()
        found[5].start()
        found[3].start()
        found[9].start()
    for at in range(count):
        found = every[at]
        for kind in (4, 5, 2, 3):
            found[kind].wait_recv()
            found[8 + kind].start()
    for at in range(count):
        for kind, one in enumerate(every[at]):
            if kind >= 6:
                one.wait_recv()
            one.wait_send()
        locals_[at].wait()


def gather_weights(blocks):
    count = len(blocks)
    results = pl.pallas_call(
        functools.partial(gather_kernel, count),
        in_specs=[pl.BlockSpec(memory_space=pl.ANY)] * count,
        out_specs=[pl.BlockSpec(memory_space=pl.ANY)] * count,
        out_shape=[jax.ShapeDtypeStruct((8, *block.shape), block.dtype) for block in blocks],
        scratch_shapes=[
            pltpu.SemaphoreType.DMA((count, 14)),
            pltpu.SemaphoreType.DMA((count, 14)),
            pltpu.SemaphoreType.DMA((count,)),
        ],
        compiler_params=pltpu.CompilerParams(collective_id=1, has_side_effects=True),
        cost_estimate=pl.CostEstimate(flops=0, bytes_accessed=200000000, transcendentals=0),
        name="gather_weights",
    )(*blocks)
    return [whole.reshape(-1, whole.shape[-1]) for whole in results]


class Line:
    def __init__(self, first_stage, buffers, sems):
        self.first_stage = first_stage
        self.shard, self.line_one, self.line_two, self.whole, self.line_three = buffers
        self.send_sem, self.recv_sem, self.store_sem, self.credit = sems
        row = lax.axis_index("row")
        self.is_end = (row == 0) | (row == 3)
        self.is_middle = (row == 1) | (row == 2)
        self.inner = {"row": jnp.where(row == 0, 1, 2)}
        self.outer = {"row": jnp.where(row == 1, 0, 3)}
        self.across = {"row": jnp.where(row == 1, 2, 1)}

    def remote(self, stage, slot, source, target, where):
        return pltpu.make_async_remote_copy(
            src_ref=source,
            dst_ref=target,
            send_sem=self.send_sem.at[self.first_stage + stage, slot],
            recv_sem=self.recv_sem.at[self.first_stage + stage, slot],
            device_id=where,
            device_id_type=MESH,
        )

    def inward(self, slot):
        return self.remote(0, slot, self.shard.at[slot], self.line_one.at[slot], self.inner)

    def crosswise(self, slot):
        return self.remote(1, slot, self.shard.at[slot], self.line_two.at[slot], self.across)

    def outward(self, slot):
        return self.remote(2, slot, self.whole.at[slot], self.line_three.at[slot], self.outer)

    def spend(self, stage, chunk):
        @pl.when(chunk >= LINE_SLOTS)
        def _():
            pl.semaphore_wait(self.credit.at[self.first_stage + stage], 1)

    def repay(self, stage, where):
        pl.semaphore_signal(
            self.credit.at[self.first_stage + stage],
            inc=1,
            device_id=where,
            device_id_type=MESH,
        )

    def load(self, chunk, slot, begin):
        def one(source):
            copy = pltpu.make_async_copy(source, self.shard.at[slot], self.load_sem.at[slot])
            copy.start() if begin else copy.wait()

        self.sources(chunk, one)

    def loaded(self, chunk, slot):
        self.load(chunk, slot, False)
        self.enter(chunk, slot)

    def enter(self, chunk, slot):
        @pl.when(self.is_end)
        def _():
            self.spend(0, chunk)
            self.inward(slot).start()

    def second(self, chunk, slot):
        @pl.when(self.is_middle)
        def _():
            self.inward(slot).wait_recv()
            self.shard[slot] = add(self.shard[slot], self.line_one[slot])
            self.repay(0, self.outer)
            self.spend(1, chunk)
            self.crosswise(slot).start()

    def third(self, chunk, slot):
        @pl.when(self.is_middle)
        def _():
            self.crosswise(slot).wait()
            self.whole[slot] = add(self.shard[slot], self.line_two[slot])
            self.repay(1, self.across)
            self.spend(2, chunk)
            self.outward(slot).start()
            self.store(chunk, slot, self.whole, True)

    def last(self, chunk, slot):
        @pl.when(self.is_end)
        def _():
            self.inward(slot).wait_send()
            self.outward(slot).wait_recv()
            self.store(chunk, slot, self.line_three, True)

    def end(self, chunk, slot):
        @pl.when(self.is_end)
        def _():
            self.store(chunk, slot, self.line_three, False)
            self.repay(2, self.inner)

        @pl.when(self.is_middle)
        def _():
            self.store(chunk, slot, self.whole, False)
            self.outward(slot).wait_send()

    def store(self, chunk, slot, origin, begin):
        def one(target):
            copy = pltpu.make_async_copy(origin.at[slot], target, self.store_sem.at[slot])
            copy.start() if begin else copy.wait()

        self.targets(chunk, one)

    def drain(self):
        @pl.when(self.is_end)
        def _():
            pl.semaphore_wait(self.credit.at[self.first_stage], LINE_SLOTS)

        @pl.when(self.is_middle)
        def _():
            pl.semaphore_wait(self.credit.at[self.first_stage + 1], LINE_SLOTS)
            pl.semaphore_wait(self.credit.at[self.first_stage + 2], LINE_SLOTS)


def pieces(lengths, chunk, body):
    low = 0
    for which, amount in enumerate(lengths):

        @pl.when((chunk >= low) & (chunk < low + amount))
        def _(low=low, which=which):
            body(which, chunk - low)

        low += amount


def tile_columns(at, width):
    return pl.ds(pl.multiple_of(at * width, width), width)


def sum_kernel(count, group, per, *refs):
    take = iter(refs)
    lefts = [next(take) for _ in range(count)]
    rights = [next(take) for _ in range(count)]
    image_part, bias_part, spread = next(take), next(take), next(take)
    parts = [next(take) for _ in range(3)]
    results = [next(take) for _ in range(count)]
    every_image, bias_total, given = next(take), next(take), next(take)
    part_results = [next(take) for _ in range(3)]
    grads, core_in, pair, upper_in, lower_in, upper_two, lower_two = [next(take) for _ in range(7)]
    main_buffers = [next(take) for _ in range(5)]
    tall_buffers = [next(take) for _ in range(5)]
    flat_buffers = [next(take) for _ in range(5)]
    image_in, bias_in, small_send, small_recv = [next(take) for _ in range(4)]
    send_sem, recv_sem, store_sem, load_sem, give_send, give_recv, credit = take
    row = lax.axis_index("row")
    near_row, far_row = row + 1 - 2 * lax.rem(row, 2), lax.rem(row + 2, 4)
    main = Line(5, main_buffers, (send_sem, recv_sem, store_sem.at[0], credit))
    tall = Line(8, tall_buffers, (send_sem, recv_sem, store_sem.at[1], credit))
    flat = Line(11, flat_buffers, (send_sem, recv_sem, store_sem.at[2], credit))
    tall.load_sem, flat.load_sem = load_sem.at[0], load_sem.at[1]
    lengths = [
        left.shape[1] * (right.shape[1] // TILE_COLUMNS) for left, right in zip(lefts, rights)
    ]
    chunks = sum(lengths)
    _, (core, x, y), (sibling, x_mate, y_mate) = mates()
    upper, lower = pl.ds(0, CUT), pl.ds(CUT, TILE_ROWS - CUT)

    def main_targets(chunk, body):
        def one(which, at):
            result = results[which]
            per_row = result.shape[2] // TILE_COLUMNS
            columns = tile_columns(lax.rem(at, per_row), TILE_COLUMNS)
            body(result.at[at // per_row, :, columns])

        pieces(lengths, chunk, one)

    main.targets = main_targets

    def side_tiles(line, origins, ends):
        amounts = [origin.shape[1] // LINE_TILE for origin in origins]

        def view(refs):
            def visit(chunk, body):
                def one(which, at):
                    body(refs[which].at[:, tile_columns(at, LINE_TILE)])

                pieces(amounts, chunk, one)

            return visit

        line.sources, line.targets = view(origins), view(ends)
        return sum(amounts)

    tall_tiles = side_tiles(tall, parts[1:], part_results[1:])
    flat_tiles = side_tiles(flat, parts[:1], part_results[:1])

    def remote(stage, slot, source, target, where):
        return pltpu.make_async_remote_copy(
            src_ref=source,
            dst_ref=target,
            send_sem=send_sem.at[stage, slot],
            recv_sem=recv_sem.at[stage, slot],
            device_id={"img": where},
            device_id_type=MESH,
        )

    def to_sibling(slot):
        return remote(0, slot, grads.at[slot, :, :, 1 - core], core_in.at[slot], sibling)

    def upper_first(slot):
        return remote(1, slot, pair.at[slot, :, 1 - x, upper, :], upper_in.at[slot], x_mate)

    def lower_first(slot):
        return remote(2, slot, pair.at[slot, 1 - y, :, lower, :], lower_in.at[slot], y_mate)

    def upper_second(slot):
        return remote(3, slot, pair.at[slot, 1 - y, x, upper, :], upper_two.at[slot], y_mate)

    def lower_second(slot):
        return remote(4, slot, pair.at[slot, y, 1 - x, lower, :], lower_two.at[slot], x_mate)

    def spend(stage, chunk):
        @pl.when(chunk >= SLOTS)
        def _():
            pl.semaphore_wait(credit.at[stage], 1)

    def repay(stage, where):
        pl.semaphore_signal(
            credit.at[stage], inc=1, device_id={"img": where}, device_id_type=MESH
        )

    for mate in (sibling, x_mate, y_mate):
        greet({"img": mate})
    for shift in range(1, 4):
        greet({"row": lax.rem(row + shift, 4)})
    pl.semaphore_wait(pltpu.get_barrier_semaphore(), 6)

    def small(kind, source, target, where):
        return pltpu.make_async_remote_copy(
            src_ref=source,
            dst_ref=target,
            send_sem=small_send.at[kind],
            recv_sem=small_recv.at[kind],
            device_id=where,
            device_id_type=MESH,
        )

    own_half = pl.ds(2 * (row // 2), 2)
    image_hops = [
        (image_part, image_in, {"img": sibling}),
        (every_image.at[row, y, x], every_image.at[row, y, x], {"img": y_mate}),
        (every_image.at[row, :, x], every_image.at[row, :, x], {"img": x_mate}),
        (every_image.at[row], every_image.at[row], {"row": near_row}),
        (every_image.at[own_half], every_image.at[own_half], {"row": far_row}),
    ]

    def small_hop(hop, begin):
        source, target, where = image_hops[hop]
        image = small(2 * hop, source, target, where)
        bias = small(2 * hop + 1, bias_total if hop else bias_part, bias_in.at[hop], where)
        if begin:
            image.start()
            bias.start()
            return
        image.wait()
        bias.wait()
        if hop == 0:
            summed = image_part[...] + image_in[...]
            every_image[row, y, x] = summed.astype(jnp.bfloat16)
        bias_total[...] = (bias_total if hop else bias_part)[...] + bias_in[hop]

    slot_len = given.shape[1]

    def giving(shift, rows):
        return pltpu.make_async_remote_copy(
            src_ref=spread.at[shift, rows, :],
            dst_ref=given.at[shift - 1, rows, :],
            send_sem=give_send.at[shift - 1],
            recv_sem=give_recv.at[shift - 1],
            device_id={"row": lax.rem(row + shift, 4)},
            device_id_type=MESH,
        )

    def owner_core(place):
        return (place // group) // per

    def give_some(at):
        @pl.when((at < slot_len // GIVE_ROWS) & (owner_core(row) == core))
        def _():
            for shift in range(1, 4):
                giving(shift, pl.ds(pl.multiple_of(at * GIVE_ROWS, GIVE_ROWS), GIVE_ROWS)).start()

    def give_wait():
        for shift in range(1, 4):
            whole = giving(shift, pl.ds(0, slot_len))

            @pl.when(owner_core(row) == core)
            def _(whole=whole):
                whole.wait_send()

            @pl.when(owner_core(lax.rem(row + 4 - shift, 4)) == core)
            def _(whole=whole):
                whole.wait_recv()

    def own_shard(chunk, slot):
        line_slot = lax.rem(chunk, LINE_SLOTS)
        upper_second(slot).wait()
        main.shard[line_slot, upper, :] = add(pair[slot, y, x, upper, :], upper_two[slot])
        repay(3, y_mate)
        lower_second(slot).wait()
        main.shard[line_slot, lower, :] = add(pair[slot, y, x, lower, :], lower_two[slot])
        repay(4, x_mate)
        main.enter(chunk, line_slot)

    def second_axis(chunk, slot):
        upper_first(slot).wait()
        for at in range(2):
            pair[slot, at, x, upper, :] = add(pair[slot, at, x, upper, :], upper_in[slot, at])
        repay(1, x_mate)
        spend(3, chunk)
        upper_second(slot).start()
        lower_first(slot).wait()
        for at in range(2):
            pair[slot, y, at, lower, :] = add(pair[slot, y, at, lower, :], lower_in[slot, at])
        repay(2, y_mate)
        spend(4, chunk)
        lower_second(slot).start()

    def first_axis(chunk, slot):
        to_sibling(slot).wait()
        for at_y in range(2):
            for at_x in range(2):
                pair[slot, at_y, at_x] = add(
                    grads[slot, at_y, at_x, core], core_in[slot, at_y, at_x]
                )
        repay(0, sibling)
        spend(1, chunk)
        upper_first(slot).start()
        spend(2, chunk)
        lower_first(slot).start()

    def multiply(chunk, slot):
        def one(which, at):
            left, right = lefts[which], rights[which]
            per_row = right.shape[1] // TILE_COLUMNS
            values = right[:, tile_columns(lax.rem(at, per_row), TILE_COLUMNS)]
            for half in range(2):
                rows = left[pl.ds(4 * half, 4), at // per_row]
                product = jnp.dot(
                    rows.reshape(4 * TILE_ROWS, -1), values, preferred_element_type=jnp.float32
                )
                grads[slot, half] = product.astype(jnp.bfloat16).reshape(
                    2, 2, TILE_ROWS, TILE_COLUMNS
                )

        pieces(lengths, chunk, one)
        spend(0, chunk)
        to_sibling(slot).start()

    stages = [
        (12, LINE_SLOTS, main.end),
        (11, LINE_SLOTS, main.last),
        (9, LINE_SLOTS, main.third),
        (7, LINE_SLOTS, main.second),
        (5, SLOTS, own_shard),
        (3, SLOTS, second_axis),
        (1, SLOTS, first_axis),
        (0, SLOTS, multiply),
    ]

    def step(at, carry):
        for hop in range(5):

            @pl.when(at == 4 * hop)
            def _(hop=hop):
                small_hop(hop, True)

            @pl.when(at == 4 * hop + 3)
            def _(hop=hop):
                small_hop(hop, False)

        give_some(at)
        for line, tiles in ((tall, tall_tiles), (flat, flat_tiles)):
            for lag, body in (
                (8, line.end),
                (7, line.last),
                (5, line.third),
                (3, line.second),
                (1, line.loaded),
                (0, functools.partial(line.load, begin=True)),
            ):
                tile = (at - lag) // SIDE_PACE
                due = lax.rem(at - lag, SIDE_PACE) == 0

                @pl.when((at >= lag) & due & (tile < tiles))
                def _(tile=tile, body=body):
                    body(tile, lax.rem(tile, LINE_SLOTS))

        for lag, slots, body in stages:
            chunk = at - lag

            @pl.when((chunk >= 0) & (chunk < chunks))
            def _(chunk=chunk, slots=slots, body=body):
                body(chunk, lax.rem(chunk, slots))

        return carry

    lax.fori_loop(0, chunks + 12, step, 0)
    for stage in range(5):
        pl.semaphore_wait(credit.at[stage], SLOTS)
    for line in (main, tall, flat):
        line.drain()
    give_wait()


def turn(operand):
    blocks = operand.shape[1] // (8 * TILE_ROWS)
    return operand.T.reshape(8, blocks, TILE_ROWS, operand.shape[0])


def sum_gradients(lefts, rights, image_part, bias_part, spread, parts, group, per):
    bf16 = jnp.bfloat16
    shapes = [
        jax.ShapeDtypeStruct((left.shape[1], TILE_ROWS, right.shape[1]), bf16)
        for left, right in zip(lefts, rights)
    ]
    image_rows, bias_rows = image_part.size // 128, bias_part.size // 128
    padded = -(-image_rows // 16) * 16
    image_part = jnp.pad(image_part.reshape(image_rows, 128), ((0, padded - image_rows), (0, 0)))
    bias_part = bias_part.reshape(bias_rows, 128)
    shapes += [
        jax.ShapeDtypeStruct((4, 2, 2, padded, 128), bf16),
        jax.ShapeDtypeStruct((bias_rows, 128), jnp.float32),
        jax.ShapeDtypeStruct((3, *spread.shape[1:]), bf16),
        *[jax.ShapeDtypeStruct(part.shape, bf16) for part in parts],
    ]
    tile = (TILE_ROWS, TILE_COLUMNS)
    vmem, hbm = pl.BlockSpec(memory_space=pltpu.VMEM), pl.BlockSpec(memory_space=pl.ANY)
    flops = 2 * sum(left.size * right.shape[1] for left, right in zip(lefts, rights))
    results = pl.pallas_call(
        functools.partial(sum_kernel, len(lefts), group, per),
        in_specs=[vmem] * (2 * len(lefts) + 2) + [hbm] * 4,
        out_specs=[hbm] * len(lefts) + [vmem] * 2 + [hbm] * 4,
        out_shape=shapes,
        scratch_shapes=[
            pltpu.VMEM((SLOTS, 2, 2, 2, *tile), bf16),
            pltpu.VMEM((SLOTS, 2, 2, *tile), bf16),
            pltpu.VMEM((SLOTS, 2, 2, *tile), bf16),
            pltpu.VMEM((SLOTS, 2, CUT, TILE_COLUMNS), bf16),
            pltpu.VMEM((SLOTS, 2, TILE_ROWS - CUT, TILE_COLUMNS), bf16),
            pltpu.VMEM((SLOTS, CUT, TILE_COLUMNS), bf16),
            pltpu.VMEM((SLOTS, TILE_ROWS - CUT, TILE_COLUMNS), bf16),
            *[pltpu.VMEM((LINE_SLOTS, *tile), bf16)] * 5,
            *[pltpu.VMEM((LINE_SLOTS, parts[1].shape[0], LINE_TILE), bf16)] * 5,
            *[pltpu.VMEM((LINE_SLOTS, parts[0].shape[0], LINE_TILE), bf16)] * 5,
            pltpu.VMEM((padded, 128), jnp.float32),
            pltpu.VMEM((5, bias_rows, 128), jnp.float32),
            pltpu.SemaphoreType.DMA((10,)),
            pltpu.SemaphoreType.DMA((10,)),
            pltpu.SemaphoreType.DMA((14, LINE_SLOTS)),
            pltpu.SemaphoreType.DMA((14, LINE_SLOTS)),
            pltpu.SemaphoreType.DMA((3, LINE_SLOTS)),
            pltpu.SemaphoreType.DMA((2, LINE_SLOTS)),
            pltpu.SemaphoreType.DMA((3,)),
            pltpu.SemaphoreType.DMA((3,)),
            pltpu.SemaphoreType.REGULAR((14,)),
        ],
        compiler_params=pltpu.CompilerParams(
            collective_id=0, has_side_effects=True, vmem_limit_bytes=56 * 1024 * 1024
        ),
        cost_estimate=pl.CostEstimate(
            flops=flops, bytes_accessed=600000000, transcendentals=0
        ),
        name="sum_gradients",
    )(*lefts, *rights, image_part, bias_part, spread, *parts)
    summed = [
        result.reshape(-1, result.shape[2]).astype(jnp.float32) for result in results[: len(lefts)]
    ]
    every_image, bias_total, given = results[len(lefts) : len(lefts) + 3]
    parts = [part.astype(jnp.float32) for part in results[len(lefts) + 3 :]]
    every_image = every_image[:, :, :, :image_rows].reshape(4, 4, -1).transpose(1, 0, 2)
    return summed, every_image.reshape(16, -1), bias_total.reshape(-1), given, parts


def split_heads(operand):
    return operand.reshape(operand.shape[0], HEADS, HDIM).transpose(1, 0, 2)


def join_heads(operand):
    return operand.transpose(1, 0, 2).reshape(operand.shape[1], HEADS * HDIM)


def local(
    n_img,
    n_row,
    tokens,
    cotangent,
    targets,
    time_table,
    ada_weight,
    ada_bias,
    qkv_weight,
    out_weight,
    up_weight,
    up_bias,
    down_weight,
    proj_first,
    proj_second,
    proj_third,
    time_bins,
    image_order,
    counts,
):
    f32, bf16 = jnp.float32, jnp.bfloat16
    per, slot_len, width = tokens.shape
    column = 2 * per
    group = n_row // column
    length = TOTAL // (2 * group)
    n_images = time_bins.shape[0]
    img_rank, row_rank = lax.axis_index("img"), lax.axis_index("row")
    core = img_rank % 2
    place = row_rank // group
    receives = place // per == core

    def swap(operand, axis, bit):
        size = n_img if axis == "img" else n_row
        return lax.ppermute(operand, axis, [(at, at ^ bit) for at in range(size)])

    def route(shift, back):
        pairs = [
            (img * n_row + (row + shift) % n_row, img * n_row + row)
            for img in range(n_img)
            for row in range(n_row)
            if (row // group) // per == img % 2
        ]
        return [(b, a) for a, b in pairs] if back else pairs

    own_counts = lax.dynamic_index_in_dim(counts, place % per, 0, keepdims=False)
    first_of = (jnp.cumsum(own_counts) - own_counts) * RW
    position = jnp.arange(slot_len)
    kept = (row_rank % group) * 2 * length + jnp.arange(2 * length)
    picks = []
    for shift in range(n_row):
        source_row = (row_rank + shift) % n_row
        begin = lax.dynamic_index_in_dim(first_of, source_row, 0, keepdims=False)
        limit = lax.dynamic_index_in_dim(own_counts, source_row, 0, keepdims=False) * RW
        hit = (kept[:, None] == begin + position[None, :]) & (position[None, :] < limit)
        picks.append(hit)
    pick = jnp.concatenate(picks, axis=1).astype(bf16)

    def image_of(shift):
        return (((row_rank - shift) % n_row) // group) % per

    def bring_start(operand):
        pieces = []
        for shift in range(n_row):
            piece = lax.dynamic_index_in_dim(operand, image_of(shift), 0, keepdims=False)
            if shift:
                piece = lax.ppermute(piece, ("img", "row"), route(shift, False))
            pieces.append(piece)
        return pieces

    def bring_end(pieces):
        packed = matmul(pick, jnp.concatenate(pieces, axis=0)).astype(bf16)
        own = lax.dynamic_slice_in_dim(packed, core * length, length, 0)
        other = lax.dynamic_slice_in_dim(packed, (1 - core) * length, length, 0)
        return jnp.where(receives, own, swap(other, "img", 1))

    def give_start(operand):
        other = swap(operand, "img", 1)
        both = jnp.where(
            core == 0,
            jnp.concatenate([operand, other], axis=0),
            jnp.concatenate([other, operand], axis=0),
        )
        return weight_grad(pick, both).astype(bf16)

    def give_end(spread, given=None):
        images = [jnp.zeros((slot_len, spread.shape[1]), bf16) for _ in range(per)]
        for shift in range(n_row):
            piece = spread[shift * slot_len : (shift + 1) * slot_len]
            if shift and given is not None:
                sender = ((row_rank - shift) % n_row) // group
                piece = jnp.where(sender // per == core, given[shift - 1], jnp.zeros_like(piece))
            elif shift:
                piece = lax.ppermute(piece, ("img", "row"), route(shift, True))
            else:
                piece = jnp.where(receives, piece, jnp.zeros_like(piece))
            images = [
                image + jnp.where(image_of(shift) == at, piece, jnp.zeros_like(piece))
                for at, image in enumerate(images)
            ]
        return jnp.stack(images)

    def fetch(operand):
        return lax.all_gather(operand, "img", axis=0, tiled=True)

    chip_bits = [1 << at for at in range(1, n_img.bit_length() - 1)]
    forth, back = chip_bits, chip_bits[-1:] + chip_bits[:-1]

    def side(bit):
        return (img_rank // bit) % 2

    def together(operand, bit, axis):
        blocks = jnp.stack([operand, swap(operand, "img", bit)], axis=axis)
        return jnp.where(side(bit) == 0, blocks, jnp.flip(blocks, axis=axis))

    def scattered(grad):
        return lax.psum_scatter(grad, "img", scatter_dimension=0, tiled=True)

    def offload_shards(left, right):
        return scattered(weight_grad(left, right).astype(bf16))

    def row_sum(part, turn_by):
        ranks = [(at + turn_by) % n_row for at in range(n_row)]
        return lax.psum(part, "row", axis_index_groups=[ranks]).astype(f32)

    fold = n_row // 4
    line_rank = row_rank // fold

    def over_row(part):
        def hop(operand, pairs):
            routes = [(a * fold + low, b * fold + low) for a, b in pairs for low in range(fold)]
            return lax.ppermute(operand, "row", routes)

        for at in range(fold.bit_length() - 1):
            part = (part.astype(f32) + swap(part, "row", 1 << at).astype(f32)).astype(bf16)
        part = (part.astype(f32) + hop(part, [(0, 1), (3, 2)]).astype(f32)).astype(bf16)
        part = (part.astype(f32) + hop(part, [(1, 2), (2, 1)]).astype(f32)).astype(bf16)
        outer = hop(part, [(1, 0), (2, 3)])
        return jnp.where((line_rank == 0) | (line_rank == 3), outer, part).astype(f32)

    order = image_order
    for bit in [1] + chip_bits:
        order = together(order, bit, 0).reshape(-1)
    chosen = jnp.sum(
        jnp.where(order[:, None] == jnp.arange(n_images)[None, :], time_bins[None, :], 0), axis=1
    )
    select = (chosen[:, None] == jnp.arange(time_table.shape[0])[None, :]).astype(f32)
    condition = jnp.dot(select, time_table.astype(f32), precision=lax.Precision.HIGHEST)
    silu_cond = jax.nn.silu(condition).astype(bf16)
    row_cond = lax.dynamic_index_in_dim(
        silu_cond.reshape(n_img // 2, column, -1), place, 1, keepdims=False
    )
    mod_width = ada_weight.shape[1]
    ff_width = up_weight.shape[1]
    bias_part = lax.dynamic_update_slice(
        jnp.zeros((mod_width,), f32), ada_bias.astype(f32), (img_rank * ada_bias.shape[0],)
    )
    up_bias_part = lax.dynamic_update_slice(
        jnp.zeros((ff_width,), f32), up_bias.astype(f32), (img_rank * up_bias.shape[0],)
    )
    mod_part = matmul(row_cond, ada_weight) + bias_part[None, :]
    summed_rows = jnp.concatenate([mod_part.reshape(-1), up_bias_part])
    for bit in [1] + chip_bits:
        summed_rows = summed_rows + swap(summed_rows, "img", bit)
    modulation = lax.dynamic_index_in_dim(
        summed_rows[: (n_img // 2) * mod_width].reshape(n_img // 2, mod_width),
        img_rank // 2,
        0,
        keepdims=True,
    )
    up_bias_full = summed_rows[(n_img // 2) * mod_width :]
    small_plane = n_img == 8 and n_row == 4
    early = [qkv_weight, out_weight, proj_third]
    if small_plane:
        early, modulation = lax.optimization_barrier((early, modulation))
        qkv_full, out_full, third_full = gather_weights(early)
    else:
        qkv_full, out_full, third_full = [fetch(one) for one in early]
    up_full = fetch(up_weight)
    down_full = fetch(down_weight)
    first_full = fetch(proj_first)
    second_full = fetch(proj_second)

    shift_att, scale_att, gate_att, shift_mlp, scale_mlp, gate_mlp = jnp.split(
        modulation, 6, axis=1
    )
    arriving, qkv_full = lax.optimization_barrier((bring_start(tokens), qkv_full))
    source = bring_end(arriving).astype(f32)
    later, source = lax.optimization_barrier(
        (jnp.concatenate([cotangent, targets], axis=2), source)
    )
    outside = bring_start(later)

    h_att = modulate(source, shift_att, scale_att).astype(bf16)
    qkv_rows = matmul(h_att, qkv_full).astype(bf16)
    key_value = qkv_rows[:, width:]
    key_value = jnp.concatenate([key_value, swap(key_value, "img", 1)], axis=0)
    bits = [1 << at for at in range(group.bit_length() - 1)]
    for bit in bits:
        key_value = jnp.concatenate([key_value, swap(key_value, "row", bit)], axis=0)
    queries = split_heads(qkv_rows[:, :width])
    keys = split_heads(key_value[:, :width])
    values = split_heads(key_value[:, width:])
    mixed, log_total = attend(queries, keys, values)
    head_mix = join_heads(mixed)
    attn_out = matmul(head_mix, out_full)
    residual = source + gate_att * attn_out
    h_mlp = modulate(residual, shift_mlp, scale_mlp).astype(bf16)
    outside, h_mlp = lax.optimization_barrier((outside, h_mlp))
    outside = bring_end(outside)
    own_cotangent = outside[:, :width].astype(f32)
    own_targets = outside[:, width:].astype(f32)
    pre_act = matmul(h_mlp, up_full) + up_bias_full
    gelu_out = gelu_tanh(pre_act).astype(bf16)
    mlp_out = matmul(gelu_out, down_full)
    lefts = [gelu_out, h_mlp, head_mix, h_att]
    if small_plane:
        lefts = [turn(left) for left in lefts]
        lefts, mlp_out = lax.optimization_barrier((lefts, mlp_out))
    block_own = (residual + gate_mlp * mlp_out).astype(bf16)
    lin_one = matmul(block_own, first_full)
    hid_one = jax.nn.silu(lin_one).astype(bf16)
    lin_two = matmul(hid_one, second_full)
    hid_two = jax.nn.silu(lin_two).astype(bf16)
    projected = matmul(hid_two, third_full)

    def align_loss(operand):
        return -0.5 * jnp.sum(alignment(operand, own_targets))

    d_proj = jax.vjp(align_loss, projected)[1](jnp.ones((), f32))[0].astype(bf16)
    third_sum = weight_grad(hid_two, d_proj).astype(bf16)
    third_sum, d_proj = lax.optimization_barrier((third_sum, d_proj))
    third_part = scattered(third_sum)
    d_lin_two = silu_back(lin_two, transposed(d_proj, third_full)).astype(bf16)
    second_sum = weight_grad(hid_one, d_lin_two).astype(bf16)
    second_sum, d_lin_two = lax.optimization_barrier((second_sum, d_lin_two))
    second_part = scattered(second_sum)
    d_lin_one = silu_back(lin_one, transposed(d_lin_two, second_full)).astype(bf16)
    first_sum = weight_grad(block_own, d_lin_one).astype(bf16)
    first_sum, d_lin_one = lax.optimization_barrier((first_sum, d_lin_one))
    first_part = scattered(first_sum)
    d_res = own_cotangent + transposed(d_lin_one, first_full)
    d_gate_mlp = jnp.sum(d_res * mlp_out, axis=0)
    d_mlp = (d_res * gate_mlp).astype(bf16)
    d_pre = gelu_back(pre_act, transposed(d_mlp, down_full)).astype(bf16)
    bias_sum = jnp.sum(d_pre.astype(f32), axis=0)
    d_resid_norm, d_shift_mlp, d_scale_mlp = jax.vjp(modulate, residual, shift_mlp, scale_mlp)[1](
        transposed(d_pre, up_full)
    )
    d_residual = d_res + d_resid_norm
    d_gate_att = jnp.sum(d_residual * attn_out, axis=0)
    d_attn = (d_residual * gate_att).astype(bf16)
    d_mixed = transposed(d_attn, out_full).astype(bf16)
    third_part, d_mixed = lax.optimization_barrier((third_part, d_mixed))
    d_query, d_key, d_value = attend_back(
        queries, keys, values, mixed, split_heads(d_mixed), log_total
    )
    second_part, d_key = lax.optimization_barrier((second_part, d_key))
    d_key_value = jnp.concatenate([join_heads(d_key), join_heads(d_value)], axis=1)
    for axis, bit in [("row", bit) for bit in reversed(bits)] + [("img", 1)]:
        half = d_key_value.shape[0] // 2
        arrived = swap(d_key_value[half:], axis, bit)
        d_key_value = (d_key_value[:half].astype(f32) + arrived.astype(f32)).astype(bf16)
    d_qkv = jnp.concatenate([join_heads(d_query), d_key_value], axis=1)
    d_source, d_shift_att, d_scale_att = jax.vjp(modulate, source, shift_att, scale_att)[1](
        transposed(d_qkv, qkv_full)
    )
    spread = give_start((d_residual + d_source).astype(bf16))
    block_out = give_end(give_start(block_own))
    own_mod = jnp.concatenate(
        [d_shift_att[0], d_scale_att[0], d_gate_att, d_shift_mlp[0], d_scale_mlp[0], d_gate_mlp]
    )
    rights = [d_mlp, d_pre, d_attn, d_qkv]
    proj_parts = [first_part, second_part, third_part]
    if small_plane:
        tied = (spread, proj_parts, rights, own_mod, bias_sum)
        spread, proj_parts, rights, own_mod, bias_sum = lax.optimization_barrier(tied)
        blocks = spread.reshape(n_row, slot_len, width)
        large, d_mod, bias_sum, given, proj_grads = sum_gradients(
            lefts, rights, own_mod, bias_sum, blocks, proj_parts, group, per
        )
        grad_tokens = give_end(spread, given)
    else:
        grad_tokens = give_end(spread)
        proj_grads = [row_sum(part, at) for at, part in enumerate(proj_parts)]
        large = [over_row(offload_shards(*pair)) for pair in zip(lefts, rights)]
        slot_id = column * (img_rank // 2) + place
        placed = jnp.zeros((n_images, mod_width), f32)
        placed = lax.dynamic_update_slice(placed, own_mod[None, :], (slot_id, 0))
        d_mod, bias_sum = lax.psum((placed, bias_sum), ("img", "row"))
        d_mod = d_mod.astype(bf16)
    grad_first, grad_second, grad_third = proj_grads
    grad_down, grad_up, grad_out, grad_qkv = large

    grad_ada = weight_grad(silu_cond, d_mod)
    grad_ada_bias = jnp.sum(
        lax.dynamic_slice_in_dim(d_mod, img_rank * ada_bias.shape[0], ada_bias.shape[0], 1).astype(
            f32
        ),
        axis=0,
    )
    d_cond = silu_back(condition, transposed(d_mod, ada_weight))
    grad_table = jnp.dot(select.T, d_cond, precision=lax.Precision.HIGHEST)
    grad_up_bias = lax.dynamic_slice_in_dim(
        bias_sum, img_rank * up_bias.shape[0], up_bias.shape[0], 0
    )
    return (
        block_out,
        grad_tokens,
        grad_table,
        grad_ada,
        grad_ada_bias,
        grad_qkv,
        grad_out,
        grad_up,
        grad_up_bias,
        grad_down,
        grad_first,
        grad_second,
        grad_third,
    )


def solution(mesh):
    return jax.shard_map(
        functools.partial(local, mesh.shape["img"], mesh.shape["row"]),
        mesh=mesh,
        in_specs=(
            P("img", "row", None),
            P("img", "row", None),
            P("img", "row", None),
            P(None, "img"),
            P("img", None),
            P("img"),
            P("img", None),
            P("img", None),
            P("img", None),
            P("img"),
            P("img", None),
            P("img", None),
            P("img", None),
            P("img", None),
            P(),
            P("img"),
            P("img", None),
        ),
        out_specs=(
            P("img", "row", None),
            P("img", "row", None),
            P(None, "img"),
            P("img", None),
            P("img"),
            P("img", None),
            P("img", None),
            P("img", None),
            P("img"),
            P("img", None),
            P("img", None),
            P("img", None),
            P("img", None),
        ),
        check_vma=False,
    )
```

```python
import functools

import jax
import jax.numpy as jnp
from jax import lax
from jax.experimental import pallas as pl
from jax.experimental.pallas import tpu as pltpu
from jax.sharding import PartitionSpec as P

HEADS = 16
HDIM = 72
RW = 32
LROWS = 32
TOTAL = LROWS * RW
SCALE = HDIM ** (-0.5)
LOG2E = 1.4426950408889634
LAST = (((1,), (1,)), ((), ()))
FIRST = (((0,), (0,)), ((), ()))


def normalize(operand):
    centre = operand - jnp.mean(operand, axis=-1, keepdims=True)
    return centre * lax.rsqrt(jnp.mean(centre * centre, axis=-1, keepdims=True) + 1e-06)


def modulate(operand, shift_row, scale_row):
    return normalize(operand) * (1.0 + scale_row) + shift_row


def alignment(projected, targets):
    unit_proj = projected * lax.rsqrt(
        jnp.mean(projected * projected, axis=-1, keepdims=True) + 1e-06
    )
    unit_target = targets * lax.rsqrt(jnp.mean(targets * targets, axis=-1, keepdims=True) + 1e-06)
    return jnp.mean(unit_proj * unit_target, axis=-1)


def matmul(left_side, right_side):
    return jnp.dot(left_side, right_side, preferred_element_type=jnp.float32)


def transposed(left_side, right_side):
    return lax.dot_general(left_side, right_side, LAST, preferred_element_type=jnp.float32)


def weight_grad(left_side, right_side):
    return lax.dot_general(left_side, right_side, FIRST, preferred_element_type=jnp.float32)


def silu_back(operand, gradient):
    return jax.vjp(jax.nn.silu, operand)[1](gradient)[0]


def gelu_tanh(operand):
    return jax.nn.gelu(operand, approximate=True)


def gelu_back(operand, gradient):
    return jax.vjp(gelu_tanh, operand)[1](gradient)[0]


MESH = pl.DeviceIdType.MESH
WINDOW = 256


def head_window(head, width):
    first = jnp.minimum(head * HDIM // 128, (width - WINDOW) // 128) * 128
    lane = lax.broadcasted_iota(jnp.int32, (1, WINDOW), 1) + first - head * HDIM
    return first, (lane >= 0) & (lane < HDIM)


def columns_at(first, part, width):
    return pl.ds(pl.multiple_of(first + part * width, 128), WINDOW)


def attend_kernel(own_ref, rest_ref, mix_ref, lse_ref):
    length, width = mix_ref.shape
    block = min(256, length)

    def one_head(head, carry):
        first, mine = head_window(head, width)
        mix_columns = columns_at(first, 0, width)
        key_refs = [own_ref.at[:, columns_at(first, 1, width)]]
        key_refs.append(rest_ref.at[:, columns_at(first, 0, width)])
        value_refs = [own_ref.at[:, columns_at(first, 2, width)]]
        value_refs.append(rest_ref.at[:, columns_at(first, 1, width)])
        keys, values = [ref[...] for ref in key_refs], [ref[...] for ref in value_refs]
        for at in range(0, length, block):
            rows = pl.ds(at, block)
            queries = jnp.where(mine, own_ref[rows, mix_columns], jnp.bfloat16(0))
            scores = [
                lax.dot_general(queries, part, LAST, preferred_element_type=jnp.float32)
                for part in keys
            ]
            tops = [jnp.max(part, axis=1, keepdims=True) for part in scores]
            top = jnp.maximum(tops[0], tops[1])
            top = top * (SCALE * LOG2E)
            weights = [jnp.exp2(part * (SCALE * LOG2E) - top) for part in scores]
            total = sum(jnp.sum(part, axis=1, keepdims=True) for part in weights)
            mixed = sum(
                jnp.dot(part.astype(jnp.bfloat16), value, preferred_element_type=jnp.float32)
                for part, value in zip(weights, values)
            )
            mixed = (mixed / total).astype(mix_ref.dtype)
            mix_ref[rows, mix_columns] = jnp.where(mine, mixed, mix_ref[rows, mix_columns])
            log_total = jnp.broadcast_to(top + jnp.log(total) * LOG2E, (block, 128))
            lse_ref[head, :, rows] = log_total.T[:1, :]
        return carry

    mix_ref[...] = jnp.zeros_like(mix_ref)
    lax.fori_loop(0, HEADS, one_head, 0)


def attend(own, rest, width):
    length, span = own.shape[0], own.shape[0] + rest.shape[0]
    vmem, bf16 = pl.BlockSpec(memory_space=pltpu.VMEM), jnp.bfloat16
    return pl.pallas_call(
        attend_kernel,
        in_specs=[vmem] * 2,
        out_specs=[vmem] * 2,
        out_shape=[
            jax.ShapeDtypeStruct((length, width), bf16),
            jax.ShapeDtypeStruct((HEADS, 1, length), jnp.float32),
        ],
        compiler_params=pltpu.CompilerParams(vmem_limit_bytes=56 * 1024 * 1024),
        cost_estimate=pl.CostEstimate(
            flops=4 * HEADS * length * span * 256,
            bytes_accessed=4 * (length + span) * width * 2,
            transcendentals=HEADS * length * span,
        ),
        name="attend",
    )(own, rest)


def greet(where):
    barrier = pltpu.get_barrier_semaphore()
    pl.semaphore_signal(barrier, inc=1, device_id=where, device_id_type=MESH)


class Give:
    def __init__(self, group, per, spread, given, send_sem, recv_sem):
        self.group, self.per = group, per
        self.spread, self.given, self.send_sem, self.recv_sem = spread, given, send_sem, recv_sem
        self.row = lax.axis_index("row")
        self.slots = given.shape[1]

    def greet(self):
        for shift in range(1, 4):
            greet({"row": lax.rem(self.row + shift, 4)})

    def copy(self, shift, rows):
        return pltpu.make_async_remote_copy(
            src_ref=self.spread.at[shift, rows, :],
            dst_ref=self.given.at[shift - 1, rows, :],
            send_sem=self.send_sem.at[shift - 1],
            recv_sem=self.recv_sem.at[shift - 1],
            device_id={"row": lax.rem(self.row + shift, 4)},
            device_id_type=MESH,
        )

    def from_here(self, row):
        return (row // self.group) // self.per == lax.rem(lax.axis_index("img"), 2)

    def start(self, at, amount):
        @pl.when((at < self.slots // amount) & self.from_here(self.row))
        def _():
            for shift in range(1, 4):
                rows = pl.ds(pl.multiple_of(at * amount, amount), amount)
                self.copy(shift, rows).start()

    def wait(self):
        for shift in range(1, 4):
            whole = self.copy(shift, pl.ds(0, self.slots))

            @pl.when(self.from_here(self.row))
            def _(whole=whole):
                whole.wait_send()

            @pl.when(self.from_here(lax.rem(self.row + 4 - shift, 4)))
            def _(whole=whole):
                whole.wait_recv()


def attend_back_kernel(
    give, own_ref, rest_ref, mix_ref, d_ref, lse_ref, spread, dq_ref, own_out, rest_out, given, *sems
):
    length, width = mix_ref.shape
    block = 256
    if give:
        sender = Give(*give, spread, given, *sems)
        sender.greet()
        pl.semaphore_wait(pltpu.get_barrier_semaphore(), 3)
        sender.start(0, given.shape[1])
    for ref in (dq_ref, own_out, rest_out):
        ref[...] = jnp.zeros_like(ref)

    def one_head(head, carry):
        first, mine = head_window(head, width)
        here, next_part = columns_at(first, 0, width), columns_at(first, 1, width)
        queries = jnp.where(mine, own_ref[:, here], jnp.bfloat16(0))
        d_mix = jnp.where(mine, d_ref[:, here], jnp.bfloat16(0))
        product = d_mix.astype(jnp.float32) * mix_ref[:, here].astype(jnp.float32)
        delta = lax.dot_general(
            jnp.ones((8, WINDOW), jnp.float32),
            product,
            LAST,
            precision=lax.Precision.HIGHEST,
            preferred_element_type=jnp.float32,
        )[:1, :]
        log_total = lse_ref[head]
        d_query = jnp.zeros((length, WINDOW), jnp.float32)
        runs = [(own_ref, 1, own_out, at) for at in range(0, length, block)]
        runs += [(rest_ref, 0, rest_out, at) for at in range(0, rest_ref.shape[0], block)]
        for source, part, target, at in runs:
            rows = pl.ds(at, block)
            keys = source[rows, columns_at(first, part, width)]
            values = source[rows, columns_at(first, part + 1, width)]
            scores = lax.dot_general(keys, queries, LAST, preferred_element_type=jnp.float32)
            prob = jnp.exp2(scores * (SCALE * LOG2E) - log_total)
            d_prob = lax.dot_general(values, d_mix, LAST, preferred_element_type=jnp.float32)
            d_score = (prob * (d_prob - delta)).astype(jnp.bfloat16)
            d_key = jnp.dot(d_score, queries, preferred_element_type=jnp.float32) * SCALE
            d_value = jnp.dot(
                prob.astype(jnp.bfloat16), d_mix, preferred_element_type=jnp.float32
            )
            target[rows, here] += d_key.astype(target.dtype)
            target[rows, next_part] += d_value.astype(target.dtype)
            d_query += lax.dot_general(d_score, keys, FIRST, preferred_element_type=jnp.float32)
        d_query = jnp.where(mine, d_query * SCALE, 0.0)
        dq_ref[:, here] += d_query.astype(dq_ref.dtype)
        return carry

    lax.fori_loop(0, HEADS, one_head, 0)
    if give:
        sender.wait()


def attend_back(own, rest, mixed, d_mix, log_total, spread, give):
    length, width = mixed.shape
    span = length + rest.shape[0]
    vmem, bf16 = pl.BlockSpec(memory_space=pltpu.VMEM), jnp.bfloat16
    hbm = pl.BlockSpec(memory_space=pl.ANY)
    remote = dict(collective_id=2, has_side_effects=True) if give else {}
    return pl.pallas_call(
        functools.partial(attend_back_kernel, give),
        in_specs=[vmem] * 5 + [hbm],
        out_specs=[vmem] * 3 + [hbm],
        out_shape=[
            jax.ShapeDtypeStruct((length, width), bf16),
            jax.ShapeDtypeStruct((length, 2 * width), bf16),
            jax.ShapeDtypeStruct((span - length, 2 * width), bf16),
            jax.ShapeDtypeStruct((spread.shape[0] - 1, *spread.shape[1:]), bf16),
        ],
        scratch_shapes=[pltpu.SemaphoreType.DMA((3,))] * 2 if give else [],
        compiler_params=pltpu.CompilerParams(vmem_limit_bytes=56 * 1024 * 1024, **remote),
        cost_estimate=pl.CostEstimate(
            flops=10 * HEADS * length * span * 256,
            bytes_accessed=8 * (length + span) * width * 2,
            transcendentals=HEADS * length * span,
        ),
        name="attend_back",
    )(own, rest, mixed, d_mix, log_total, spread)


TILE_ROWS = 144
TILE_COLUMNS = 384
CUT = 80
SLOTS = 4
LINE_SLOTS = 8
LINE_TILE = 256
SIDE_PACE = 4
GIVE_ROWS = 16


def add(one, other):
    return one + other


def mates():
    me = lax.axis_index("img")
    core, x, y = lax.rem(me, 2), lax.rem(me // 2, 2), me // 4
    return me, (core, x, y), (me + 1 - 2 * core, me + 2 - 4 * x, me + 4 - 8 * y)


def gather_kernel(count, group, per, *refs):
    take = iter(refs)
    blocks = [next(take) for _ in range(count)]
    slots = [next(take) for _ in range(3)]
    part = next(take)
    wholes = [next(take) for _ in range(count)]
    arrivals = [next(take) for _ in range(3)]
    total = next(take)
    part_in, part_sum, send_sem, recv_sem, local_sem, slot_send, slot_recv, slot_local = [
        next(take) for _ in range(8)
    ]
    part_send, part_recv = take
    row = lax.axis_index("row")
    me, (core, x, y), (sibling, x_mate, y_mate) = mates()
    far = x_mate + 4 - 8 * y
    for mate in (sibling, x_mate, y_mate):
        greet({"img": mate})
    for shift in range(1, 4):
        greet({"row": lax.rem(row + shift, 4)})
    pl.semaphore_wait(pltpu.get_barrier_semaphore(), 6)

    def place_of(place):
        return (place // group) // per, lax.rem(place // group, per)

    takes_in = place_of(row)[0] == core

    def by_row(which, shift):
        where = lax.rem(row + 4 - shift, 4)
        return pltpu.make_async_remote_copy(
            src_ref=slots[which].at[place_of(where)[1]],
            dst_ref=arrivals[which].at[row],
            send_sem=slot_send.at[which, shift - 1],
            recv_sem=slot_recv.at[which, shift - 1],
            device_id={"row": where},
            device_id_type=MESH,
        )

    def own_slots(which):
        source = slots[which].at[place_of(row)[1]]
        return pltpu.make_async_copy(source, arrivals[which].at[row], slot_local.at[which])

    def by_core(which, shift):
        origin = lax.rem(row + shift, 4)
        source = arrivals[which].at[origin] if shift else slots[which].at[place_of(row)[1]]
        return pltpu.make_async_remote_copy(
            src_ref=source,
            dst_ref=arrivals[which].at[origin],
            send_sem=slot_send.at[which, 3 + shift],
            recv_sem=slot_recv.at[which, 3 + shift],
            device_id={"img": sibling},
            device_id_type=MESH,
        )

    def start_slots(which):
        for shift in range(1, 4):

            @pl.when(place_of(lax.rem(row + 4 - shift, 4))[0] == core)
            def _(shift=shift):
                by_row(which, shift).start()

        @pl.when(takes_in)
        def _():
            own_slots(which).start()
            by_core(which, 0).start()

    def pass_slots(which):
        for shift in range(1, 4):

            @pl.when(takes_in)
            def _(shift=shift):
                by_row(which, shift).wait_recv()
                by_core(which, shift).start()

    def end_slots(which):
        for shift in range(1, 4):

            @pl.when(place_of(lax.rem(row + 4 - shift, 4))[0] == core)
            def _(shift=shift):
                by_row(which, shift).wait_send()

        @pl.when(takes_in)
        def _():
            own_slots(which).wait()
            for shift in range(4):
                by_core(which, shift).wait_send()

        @pl.when(jnp.logical_not(takes_in))
        def _():
            for shift in range(4):
                by_core(which, shift).wait_recv()

    part_mates = [sibling, x_mate, y_mate]

    def part_hop(hop):
        return pltpu.make_async_remote_copy(
            src_ref=part_sum.at[hop - 1] if hop else part,
            dst_ref=part_in.at[hop],
            send_sem=part_send.at[hop],
            recv_sem=part_recv.at[hop],
            device_id={"img": part_mates[hop]},
            device_id_type=MESH,
        )

    def take_part(hop):
        part_hop(hop).wait()
        summed = (part_sum[hop - 1] if hop else part[...]) + part_in[hop]
        if hop == 2:
            total[...] = summed
        else:
            part_sum[hop] = summed
            part_hop(hop + 1).start()

    def halves(at):
        rows = blocks[at].shape[0]
        cut = (rows // 2 + 15) // 16 * 16
        return pl.ds(0, cut), pl.ds(cut, rows - cut)

    def copy(at, kind, source, owner, rows, where):
        return pltpu.make_async_remote_copy(
            src_ref=source,
            dst_ref=wholes[at].at[owner, rows, :],
            send_sem=send_sem.at[at, kind],
            recv_sem=recv_sem.at[at, kind],
            device_id={"img": where},
            device_id_type=MESH,
        )

    def copies(at):
        upper, lower = halves(at)
        block, whole = blocks[at], wholes[at]
        found = [
            copy(at, 0, block.at[upper, :], me, upper, x_mate),
            copy(at, 1, block.at[lower, :], me, lower, y_mate),
            copy(at, 2, block.at[upper, :], me, upper, y_mate),
            copy(at, 3, block.at[lower, :], me, lower, x_mate),
            copy(at, 4, whole.at[x_mate, upper, :], x_mate, upper, y_mate),
            copy(at, 5, whole.at[y_mate, lower, :], y_mate, lower, x_mate),
            copy(at, 6, block.at[upper, :], me, upper, sibling),
            copy(at, 7, block.at[lower, :], me, lower, sibling),
        ]
        for kind, (owner, rows) in enumerate(
            [
                (x_mate, upper),
                (y_mate, lower),
                (y_mate, upper),
                (x_mate, lower),
                (far, upper),
                (far, lower),
            ]
        ):
            found.append(copy(at, 8 + kind, whole.at[owner, rows, :], owner, rows, sibling))
        return found

    every = [copies(at) for at in range(count)]
    locals_ = [
        pltpu.make_async_copy(blocks[at], wholes[at].at[me], local_sem.at[at])
        for at in range(count)
    ]
    part_hop(0).start()
    start_slots(0)
    for at in range(count):
        for kind in (0, 1, 6, 7):
            every[at][kind].start()
        locals_[at].start()
    take_part(0)
    start_slots(1)
    start_slots(2)
    for at in range(count):
        found = every[at]
        found[0].wait_recv()
        found[4].start()
        found[2].start()
        found[8].start()
        found[1].wait_recv()
        found[5].start()
        found[3].start()
        found[9].start()
    take_part(1)
    pass_slots(0)
    for at in range(count):
        found = every[at]
        for kind in (4, 5, 2, 3):
            found[kind].wait_recv()
            found[8 + kind].start()
    take_part(2)
    pass_slots(1)
    pass_slots(2)
    for at in range(count):
        for kind, one in enumerate(every[at]):
            if kind >= 6:
                one.wait_recv()
            one.wait_send()
        locals_[at].wait()
    for which in range(3):
        end_slots(which)


def gather_weights(blocks, slots, part, group, per):
    count = len(blocks)
    vmem, hbm = pl.BlockSpec(memory_space=pltpu.VMEM), pl.BlockSpec(memory_space=pl.ANY)
    part_rows = part.size // 128
    results = pl.pallas_call(
        functools.partial(gather_kernel, count, group, per),
        in_specs=[hbm] * (count + 3) + [vmem],
        out_specs=[hbm] * (count + 3) + [vmem],
        out_shape=[
            *[jax.ShapeDtypeStruct((8, *block.shape), block.dtype) for block in blocks],
            *[jax.ShapeDtypeStruct((4, *one.shape[1:]), one.dtype) for one in slots],
            jax.ShapeDtypeStruct((part_rows, 128), jnp.float32),
        ],
        scratch_shapes=[
            pltpu.VMEM((3, part_rows, 128), jnp.float32),
            pltpu.VMEM((2, part_rows, 128), jnp.float32),
            pltpu.SemaphoreType.DMA((count, 14)),
            pltpu.SemaphoreType.DMA((count, 14)),
            pltpu.SemaphoreType.DMA((count,)),
            pltpu.SemaphoreType.DMA((3, 7)),
            pltpu.SemaphoreType.DMA((3, 7)),
            pltpu.SemaphoreType.DMA((3,)),
            pltpu.SemaphoreType.DMA((3,)),
            pltpu.SemaphoreType.DMA((3,)),
        ],
        compiler_params=pltpu.CompilerParams(collective_id=1, has_side_effects=True),
        cost_estimate=pl.CostEstimate(flops=0, bytes_accessed=200000000, transcendentals=0),
        name="gather_weights",
    )(*blocks, *slots, part.reshape(part_rows, 128))
    wholes = [whole.reshape(-1, whole.shape[-1]) for whole in results[:count]]
    return wholes, results[count : count + 3], results[-1].reshape(-1)


def compact_kernel(places, *refs):
    sources, (shift, scale), targets, (h_att, sems) = refs[:3], refs[3:5], refs[5:8], refs[8:]
    amount = targets[0].shape[0] // RW

    def one(at, carry):
        begin = pl.multiple_of(places[at], RW)
        rows = pl.ds(pl.multiple_of(at * RW, RW), RW)
        for which in range(3):
            source = sources[which].at[pl.ds(begin, RW), :]
            pltpu.make_async_copy(source, targets[which].at[rows, :], sems.at[which]).start()
        return carry

    lax.fori_loop(0, amount, one, 0)

    def wait(which):
        rows = pl.ds(0, targets[which].shape[0])
        source = sources[which].at[rows, :]
        pltpu.make_async_copy(source, targets[which], sems.at[which]).wait()

    wait(0)

    def norm(at, carry):
        rows = pl.ds(pl.multiple_of(at * 64, 64), 64)
        block = targets[0][rows, :].astype(jnp.float32)
        block = modulate(block, shift[...], scale[...])
        h_att[rows, :] = block.astype(jnp.bfloat16)
        return carry

    lax.fori_loop(0, targets[0].shape[0] // 64, norm, 0)
    wait(1)
    wait(2)


def compact(places, slots, shift, scale):
    length = places.shape[0] * RW
    flat = [one.reshape(-1, one.shape[-1]) for one in slots]
    vmem, hbm = pl.BlockSpec(memory_space=pltpu.VMEM), pl.BlockSpec(memory_space=pl.ANY)
    shapes = [jax.ShapeDtypeStruct((length, one.shape[1]), one.dtype) for one in flat]
    return pl.pallas_call(
        compact_kernel,
        in_specs=[pl.BlockSpec(memory_space=pltpu.SMEM), *[hbm] * 3, vmem, vmem],
        out_specs=[vmem] * 4,
        out_shape=[*shapes, shapes[0]],
        scratch_shapes=[pltpu.SemaphoreType.DMA((3,))],
        compiler_params=pltpu.CompilerParams(vmem_limit_bytes=32 * 1024 * 1024),
        cost_estimate=pl.CostEstimate(flops=0, bytes_accessed=8000000, transcendentals=0),
        name="compact",
    )(places, *flat, shift, scale)


class Line:
    def __init__(self, first_stage, buffers, sems):
        self.first_stage = first_stage
        self.shard, self.line_one, self.line_two, self.whole, self.line_three = buffers
        self.send_sem, self.recv_sem, self.store_sem, self.credit = sems
        row = lax.axis_index("row")
        self.is_end = (row == 0) | (row == 3)
        self.is_middle = (row == 1) | (row == 2)
        self.inner = {"row": jnp.where(row == 0, 1, 2)}
        self.outer = {"row": jnp.where(row == 1, 0, 3)}
        self.across = {"row": jnp.where(row == 1, 2, 1)}

    def remote(self, stage, slot, source, target, where):
        return pltpu.make_async_remote_copy(
            src_ref=source,
            dst_ref=target,
            send_sem=self.send_sem.at[self.first_stage + stage, slot],
            recv_sem=self.recv_sem.at[self.first_stage + stage, slot],
            device_id=where,
            device_id_type=MESH,
        )

    def inward(self, slot):
        return self.remote(0, slot, self.shard.at[slot], self.line_one.at[slot], self.inner)

    def crosswise(self, slot):
        return self.remote(1, slot, self.shard.at[slot], self.line_two.at[slot], self.across)

    def outward(self, slot):
        return self.remote(2, slot, self.whole.at[slot], self.line_three.at[slot], self.outer)

    def spend(self, stage, chunk):
        @pl.when(chunk >= LINE_SLOTS)
        def _():
            pl.semaphore_wait(self.credit.at[self.first_stage + stage], 1)

    def repay(self, stage, where):
        pl.semaphore_signal(
            self.credit.at[self.first_stage + stage],
            inc=1,
            device_id=where,
            device_id_type=MESH,
        )

    def load(self, chunk, slot, begin):
        def one(source):
            copy = pltpu.make_async_copy(source, self.shard.at[slot], self.load_sem.at[slot])
            copy.start() if begin else copy.wait()

        self.sources(chunk, one)

    def loaded(self, chunk, slot):
        self.load(chunk, slot, False)
        self.enter(chunk, slot)

    def enter(self, chunk, slot):
        @pl.when(self.is_end)
        def _():
            self.spend(0, chunk)
            self.inward(slot).start()

    def second(self, chunk, slot):
        @pl.when(self.is_middle)
        def _():
            self.inward(slot).wait_recv()
            self.shard[slot] = add(self.shard[slot], self.line_one[slot])
            self.repay(0, self.outer)
            self.spend(1, chunk)
            self.crosswise(slot).start()

    def third(self, chunk, slot):
        @pl.when(self.is_middle)
        def _():
            self.crosswise(slot).wait()
            self.whole[slot] = add(self.shard[slot], self.line_two[slot])
            self.repay(1, self.across)
            self.spend(2, chunk)
            self.outward(slot).start()
            self.store(chunk, slot, self.whole, True)

    def last(self, chunk, slot):
        @pl.when(self.is_end)
        def _():
            self.inward(slot).wait_send()
            self.outward(slot).wait_recv()
            self.store(chunk, slot, self.line_three, True)

    def end(self, chunk, slot):
        @pl.when(self.is_end)
        def _():
            self.store(chunk, slot, self.line_three, False)
            self.repay(2, self.inner)

        @pl.when(self.is_middle)
        def _():
            self.store(chunk, slot, self.whole, False)
            self.outward(slot).wait_send()

    def store(self, chunk, slot, origin, begin):
        def one(target):
            copy = pltpu.make_async_copy(origin.at[slot], target, self.store_sem.at[slot])
            copy.start() if begin else copy.wait()

        self.targets(chunk, one)

    def drain(self):
        @pl.when(self.is_end)
        def _():
            pl.semaphore_wait(self.credit.at[self.first_stage], LINE_SLOTS)

        @pl.when(self.is_middle)
        def _():
            pl.semaphore_wait(self.credit.at[self.first_stage + 1], LINE_SLOTS)
            pl.semaphore_wait(self.credit.at[self.first_stage + 2], LINE_SLOTS)


def pieces(lengths, chunk, body):
    low = 0
    for which, amount in enumerate(lengths):

        @pl.when((chunk >= low) & (chunk < low + amount))
        def _(low=low, which=which):
            body(which, chunk - low)

        low += amount


def tile_columns(at, width):
    return pl.ds(pl.multiple_of(at * width, width), width)


def sum_kernel(count, group, per, *refs):
    take = iter(refs)
    lefts = [next(take) for _ in range(count)]
    rights = [next(take) for _ in range(count)]
    image_part, bias_part, spread = next(take), next(take), next(take)
    parts = [next(take) for _ in range(2)]
    results = [next(take) for _ in range(count)]
    every_image, bias_total, given = next(take), next(take), next(take)
    part_results = [next(take) for _ in range(2)]
    grads, core_in, pair, upper_in, lower_in, upper_two, lower_two = [next(take) for _ in range(7)]
    main_buffers = [next(take) for _ in range(5)]
    tall_buffers = [next(take) for _ in range(5)]
    image_in, bias_in, small_send, small_recv = [next(take) for _ in range(4)]
    send_sem, recv_sem, store_sem, load_sem, give_send, give_recv, credit = take
    row = lax.axis_index("row")
    near_row, far_row = row + 1 - 2 * lax.rem(row, 2), lax.rem(row + 2, 4)
    main = Line(5, main_buffers, (send_sem, recv_sem, store_sem.at[0], credit))
    tall = Line(8, tall_buffers, (send_sem, recv_sem, store_sem.at[1], credit))
    tall.load_sem = load_sem
    across = [-(-right.shape[1] // TILE_COLUMNS) for right in rights]
    lengths = [left.shape[1] * amount for left, amount in zip(lefts, across)]
    chunks = sum(lengths)
    _, (core, x, y), (sibling, x_mate, y_mate) = mates()
    upper, lower = pl.ds(0, CUT), pl.ds(CUT, TILE_ROWS - CUT)

    def main_targets(chunk, body):
        def one(which, at):
            result = results[which]
            columns = tile_columns(lax.rem(at, across[which]), TILE_COLUMNS)
            body(result.at[at // across[which], :, columns])

        pieces(lengths, chunk, one)

    main.targets = main_targets

    def side_tiles(line, origins, ends):
        amounts = [origin.shape[1] // LINE_TILE for origin in origins]

        def view(refs):
            def visit(chunk, body):
                def one(which, at):
                    body(refs[which].at[:, tile_columns(at, LINE_TILE)])

                pieces(amounts, chunk, one)

            return visit

        line.sources, line.targets = view(origins), view(ends)
        return sum(amounts)

    tall_tiles = side_tiles(tall, parts, part_results)

    def remote(stage, slot, source, target, where):
        return pltpu.make_async_remote_copy(
            src_ref=source,
            dst_ref=target,
            send_sem=send_sem.at[stage, slot],
            recv_sem=recv_sem.at[stage, slot],
            device_id={"img": where},
            device_id_type=MESH,
        )

    def to_sibling(slot):
        return remote(0, slot, grads.at[slot, :, :, 1 - core], core_in.at[slot], sibling)

    def upper_first(slot):
        return remote(1, slot, pair.at[slot, :, 1 - x, upper, :], upper_in.at[slot], x_mate)

    def lower_first(slot):
        return remote(2, slot, pair.at[slot, 1 - y, :, lower, :], lower_in.at[slot], y_mate)

    def upper_second(slot):
        return remote(3, slot, pair.at[slot, 1 - y, x, upper, :], upper_two.at[slot], y_mate)

    def lower_second(slot):
        return remote(4, slot, pair.at[slot, y, 1 - x, lower, :], lower_two.at[slot], x_mate)

    def spend(stage, chunk):
        @pl.when(chunk >= SLOTS)
        def _():
            pl.semaphore_wait(credit.at[stage], 1)

    def repay(stage, where):
        pl.semaphore_signal(
            credit.at[stage], inc=1, device_id={"img": where}, device_id_type=MESH
        )

    for mate in (sibling, x_mate, y_mate):
        greet({"img": mate})
    sender = Give(group, per, spread, given, give_send, give_recv)
    sender.greet()
    pl.semaphore_wait(pltpu.get_barrier_semaphore(), 6)

    def small(kind, source, target, where):
        return pltpu.make_async_remote_copy(
            src_ref=source,
            dst_ref=target,
            send_sem=small_send.at[kind],
            recv_sem=small_recv.at[kind],
            device_id=where,
            device_id_type=MESH,
        )

    own_half = pl.ds(2 * (row // 2), 2)
    image_hops = [
        (image_part, image_in, {"img": sibling}),
        (every_image.at[row, y, x], every_image.at[row, y, x], {"img": y_mate}),
        (every_image.at[row, :, x], every_image.at[row, :, x], {"img": x_mate}),
        (every_image.at[row], every_image.at[row], {"row": near_row}),
        (every_image.at[own_half], every_image.at[own_half], {"row": far_row}),
    ]

    def small_hop(hop, begin):
        source, target, where = image_hops[hop]
        image = small(2 * hop, source, target, where)
        bias = small(2 * hop + 1, bias_total if hop else bias_part, bias_in.at[hop], where)
        if begin:
            image.start()
            bias.start()
            return
        image.wait()
        bias.wait()
        if hop == 0:
            summed = image_part[...] + image_in[...]
            every_image[row, y, x] = summed.astype(jnp.bfloat16)
        bias_total[...] = (bias_total if hop else bias_part)[...] + bias_in[hop]

    def own_shard(chunk, slot):
        line_slot = lax.rem(chunk, LINE_SLOTS)
        upper_second(slot).wait()
        main.shard[line_slot, upper, :] = add(pair[slot, y, x, upper, :], upper_two[slot])
        repay(3, y_mate)
        lower_second(slot).wait()
        main.shard[line_slot, lower, :] = add(pair[slot, y, x, lower, :], lower_two[slot])
        repay(4, x_mate)
        main.enter(chunk, line_slot)

    def second_axis(chunk, slot):
        upper_first(slot).wait()
        for at in range(2):
            pair[slot, at, x, upper, :] = add(pair[slot, at, x, upper, :], upper_in[slot, at])
        repay(1, x_mate)
        spend(3, chunk)
        upper_second(slot).start()
        lower_first(slot).wait()
        for at in range(2):
            pair[slot, y, at, lower, :] = add(pair[slot, y, at, lower, :], lower_in[slot, at])
        repay(2, y_mate)
        spend(4, chunk)
        lower_second(slot).start()

    def first_axis(chunk, slot):
        to_sibling(slot).wait()
        for at_y in range(2):
            for at_x in range(2):
                pair[slot, at_y, at_x] = add(
                    grads[slot, at_y, at_x, core], core_in[slot, at_y, at_x]
                )
        repay(0, sibling)
        spend(1, chunk)
        upper_first(slot).start()
        spend(2, chunk)
        lower_first(slot).start()

    def multiply(chunk, slot):
        def one(which, at):
            left, right = lefts[which], rights[which]
            column, whole_tiles = lax.rem(at, across[which]), right.shape[1] // TILE_COLUMNS

            def times(values):
                for half in range(2):
                    rows = left[pl.ds(4 * half, 4), at // across[which]]
                    rows = rows.reshape(4 * TILE_ROWS, -1)
                    product = jnp.dot(rows, values, preferred_element_type=jnp.float32)
                    grads[slot, half] = product.astype(jnp.bfloat16).reshape(
                        2, 2, TILE_ROWS, TILE_COLUMNS
                    )

            if whole_tiles == across[which]:
                times(right[:, tile_columns(column, TILE_COLUMNS)])
                return

            @pl.when(column < whole_tiles)
            def _():
                times(right[:, tile_columns(column, TILE_COLUMNS)])

            @pl.when(column == whole_tiles)
            def _():
                rest = right[:, whole_tiles * TILE_COLUMNS :]
                gap = jnp.zeros((rest.shape[0], TILE_COLUMNS - rest.shape[1]), rest.dtype)
                times(jnp.concatenate([rest, gap], axis=1))

        pieces(lengths, chunk, one)
        spend(0, chunk)
        to_sibling(slot).start()

    stages = [
        (12, LINE_SLOTS, main.end),
        (11, LINE_SLOTS, main.last),
        (9, LINE_SLOTS, main.third),
        (7, LINE_SLOTS, main.second),
        (5, SLOTS, own_shard),
        (3, SLOTS, second_axis),
        (1, SLOTS, first_axis),
        (0, SLOTS, multiply),
    ]

    def step(at, carry):
        for hop in range(5):

            @pl.when(at == 4 * hop)
            def _(hop=hop):
                small_hop(hop, True)

            @pl.when(at == 4 * hop + 3)
            def _(hop=hop):
                small_hop(hop, False)


        @pl.when(lax.rem(at, 3) < 2)
        def _():
            sender.start(2 * (at // 3) + lax.rem(at, 3), GIVE_ROWS)

        for line, tiles in ((tall, tall_tiles),):
            for lag, body in (
                (8, line.end),
                (7, line.last),
                (5, line.third),
                (3, line.second),
                (1, line.loaded),
                (0, functools.partial(line.load, begin=True)),
            ):
                tile = (at - lag) // SIDE_PACE
                due = lax.rem(at - lag, SIDE_PACE) == 0

                @pl.when((at >= lag) & due & (tile < tiles))
                def _(tile=tile, body=body):
                    body(tile, lax.rem(tile, LINE_SLOTS))

        for lag, slots, body in stages:
            chunk = at - lag

            @pl.when((chunk >= 0) & (chunk < chunks))
            def _(chunk=chunk, slots=slots, body=body):
                body(chunk, lax.rem(chunk, slots))

        return carry

    lax.fori_loop(0, chunks + 12, step, 0)
    for stage in range(5):
        pl.semaphore_wait(credit.at[stage], SLOTS)
    for line in (main, tall):
        line.drain()
    sender.wait()


def turn(operand):
    blocks = operand.shape[1] // (8 * TILE_ROWS)
    return operand.T.reshape(8, blocks, TILE_ROWS, operand.shape[0])


def sum_gradients(lefts, rights, image_part, bias_part, spread, parts, group, per):
    bf16 = jnp.bfloat16
    shapes = [
        jax.ShapeDtypeStruct(
            (left.shape[1], TILE_ROWS, -(-right.shape[1] // TILE_COLUMNS) * TILE_COLUMNS), bf16
        )
        for left, right in zip(lefts, rights)
    ]
    image_rows, bias_rows = image_part.size // 128, bias_part.size // 128
    padded = -(-image_rows // 16) * 16
    image_part = jnp.pad(image_part.reshape(image_rows, 128), ((0, padded - image_rows), (0, 0)))
    bias_part = bias_part.reshape(bias_rows, 128)
    shapes += [
        jax.ShapeDtypeStruct((4, 2, 2, padded, 128), bf16),
        jax.ShapeDtypeStruct((bias_rows, 128), jnp.float32),
        jax.ShapeDtypeStruct((3, *spread.shape[1:]), bf16),
        *[jax.ShapeDtypeStruct(part.shape, bf16) for part in parts],
    ]
    tile = (TILE_ROWS, TILE_COLUMNS)
    vmem, hbm = pl.BlockSpec(memory_space=pltpu.VMEM), pl.BlockSpec(memory_space=pl.ANY)
    flops = 2 * sum(left.size * right.shape[1] for left, right in zip(lefts, rights))
    results = pl.pallas_call(
        functools.partial(sum_kernel, len(lefts), group, per),
        in_specs=[vmem] * (2 * len(lefts) + 2) + [hbm] * 3,
        out_specs=[hbm] * len(lefts) + [vmem] * 2 + [hbm] * 3,
        out_shape=shapes,
        scratch_shapes=[
            pltpu.VMEM((SLOTS, 2, 2, 2, *tile), bf16),
            pltpu.VMEM((SLOTS, 2, 2, *tile), bf16),
            pltpu.VMEM((SLOTS, 2, 2, *tile), bf16),
            pltpu.VMEM((SLOTS, 2, CUT, TILE_COLUMNS), bf16),
            pltpu.VMEM((SLOTS, 2, TILE_ROWS - CUT, TILE_COLUMNS), bf16),
            pltpu.VMEM((SLOTS, CUT, TILE_COLUMNS), bf16),
            pltpu.VMEM((SLOTS, TILE_ROWS - CUT, TILE_COLUMNS), bf16),
            *[pltpu.VMEM((LINE_SLOTS, *tile), bf16)] * 5,
            *[pltpu.VMEM((LINE_SLOTS, parts[0].shape[0], LINE_TILE), bf16)] * 5,
            pltpu.VMEM((padded, 128), jnp.float32),
            pltpu.VMEM((5, bias_rows, 128), jnp.float32),
            pltpu.SemaphoreType.DMA((10,)),
            pltpu.SemaphoreType.DMA((10,)),
            pltpu.SemaphoreType.DMA((11, LINE_SLOTS)),
            pltpu.SemaphoreType.DMA((11, LINE_SLOTS)),
            pltpu.SemaphoreType.DMA((2, LINE_SLOTS)),
            pltpu.SemaphoreType.DMA((LINE_SLOTS,)),
            pltpu.SemaphoreType.DMA((3,)),
            pltpu.SemaphoreType.DMA((3,)),
            pltpu.SemaphoreType.REGULAR((11,)),
        ],
        compiler_params=pltpu.CompilerParams(
            collective_id=0, has_side_effects=True, vmem_limit_bytes=56 * 1024 * 1024
        ),
        cost_estimate=pl.CostEstimate(
            flops=flops, bytes_accessed=600000000, transcendentals=0
        ),
        name="sum_gradients",
    )(*lefts, *rights, image_part, bias_part, spread, *parts)
    summed = [
        result.reshape(-1, result.shape[2])[:, : right.shape[1]].astype(jnp.float32)
        for result, right in zip(results, rights)
    ]
    every_image, bias_total, given = results[len(lefts) : len(lefts) + 3]
    parts = [part.astype(jnp.float32) for part in results[len(lefts) + 3 :]]
    every_image = every_image[:, :, :, :image_rows].reshape(4, 4, -1).transpose(1, 0, 2)
    return summed, every_image.reshape(16, -1), bias_total.reshape(-1), given, parts


def local(
    n_img,
    n_row,
    tokens,
    cotangent,
    targets,
    time_table,
    ada_weight,
    ada_bias,
    qkv_weight,
    out_weight,
    up_weight,
    up_bias,
    down_weight,
    proj_first,
    proj_second,
    proj_third,
    time_bins,
    image_order,
    counts,
):
    f32, bf16 = jnp.float32, jnp.bfloat16
    per, slot_len, width = tokens.shape
    column = 2 * per
    group = n_row // column
    length = TOTAL // (2 * group)
    n_images = time_bins.shape[0]
    img_rank, row_rank = lax.axis_index("img"), lax.axis_index("row")
    core = img_rank % 2
    place = row_rank // group
    receives = place // per == core

    def swap(operand, axis, bit):
        size = n_img if axis == "img" else n_row
        return lax.ppermute(operand, axis, [(at, at ^ bit) for at in range(size)])

    def route(shift, back):
        pairs = [
            (img * n_row + (row + shift) % n_row, img * n_row + row)
            for img in range(n_img)
            for row in range(n_row)
            if (row // group) // per == img % 2
        ]
        return [(b, a) for a, b in pairs] if back else pairs

    own_counts = lax.dynamic_index_in_dim(counts, place % per, 0, keepdims=False)
    first_of = (jnp.cumsum(own_counts) - own_counts) * RW
    position = jnp.arange(slot_len)
    kept = (row_rank % group) * 2 * length + jnp.arange(2 * length)
    picks = []
    for shift in range(n_row):
        source_row = (row_rank + shift) % n_row
        begin = lax.dynamic_index_in_dim(first_of, source_row, 0, keepdims=False)
        limit = lax.dynamic_index_in_dim(own_counts, source_row, 0, keepdims=False) * RW
        hit = (kept[:, None] == begin + position[None, :]) & (position[None, :] < limit)
        picks.append(hit)
    pick = jnp.concatenate(picks, axis=1).astype(bf16)

    def image_of(shift):
        return (((row_rank - shift) % n_row) // group) % per

    def bring(operand):
        pieces = []
        for shift in range(n_row):
            piece = lax.dynamic_index_in_dim(operand, image_of(shift), 0, keepdims=False)
            if shift:
                piece = lax.ppermute(piece, ("img", "row"), route(shift, False))
            pieces.append(piece)
        packed = matmul(pick, jnp.concatenate(pieces, axis=0)).astype(bf16)
        own = lax.dynamic_slice_in_dim(packed, core * length, length, 0)
        other = lax.dynamic_slice_in_dim(packed, (1 - core) * length, length, 0)
        return jnp.where(receives, own, swap(other, "img", 1))

    def give_start(operand, other):
        both = jnp.where(
            core == 0,
            jnp.concatenate([operand, other], axis=0),
            jnp.concatenate([other, operand], axis=0),
        )
        return weight_grad(pick, both).astype(bf16).reshape(n_row, slot_len, -1)

    def give_send(spread):
        sent = [
            lax.ppermute(spread[shift], ("img", "row"), route(shift, True))
            for shift in range(1, n_row)
        ]
        return [spread[0], *sent]

    def give_merge(blocks):
        images = [jnp.zeros_like(blocks[0]) for _ in range(per)]
        for shift, block in enumerate(blocks):
            sender = ((row_rank - shift) % n_row) // group
            for at in range(per):
                wanted = (sender // per == core) & (sender % per == at)
                if group > 1:
                    images[at] = images[at] + jnp.where(wanted, block, jnp.zeros_like(block))
                else:
                    images[at] = jnp.where(wanted, block, images[at])
        return jnp.stack(images)

    def fetch(operand):
        return lax.all_gather(operand, "img", axis=0, tiled=True)

    chip_bits = [1 << at for at in range(1, n_img.bit_length() - 1)]
    forth, back = chip_bits, chip_bits[-1:] + chip_bits[:-1]

    def side(bit):
        return (img_rank // bit) % 2

    def together(operand, bit, axis):
        blocks = jnp.stack([operand, swap(operand, "img", bit)], axis=axis)
        return jnp.where(side(bit) == 0, blocks, jnp.flip(blocks, axis=axis))

    def scattered(grad):
        return lax.psum_scatter(grad, "img", scatter_dimension=0, tiled=True)

    def offload_shards(left, right):
        return scattered(weight_grad(left, right).astype(bf16))

    def row_sum(part, turn_by):
        ranks = [(at + turn_by) % n_row for at in range(n_row)]
        return lax.psum(part, "row", axis_index_groups=[ranks]).astype(f32)

    fold = n_row // 4
    line_rank = row_rank // fold

    def over_row(part):
        def hop(operand, pairs):
            routes = [(a * fold + low, b * fold + low) for a, b in pairs for low in range(fold)]
            return lax.ppermute(operand, "row", routes)

        for at in range(fold.bit_length() - 1):
            part = (part.astype(f32) + swap(part, "row", 1 << at).astype(f32)).astype(bf16)
        part = (part.astype(f32) + hop(part, [(0, 1), (3, 2)]).astype(f32)).astype(bf16)
        part = (part.astype(f32) + hop(part, [(1, 2), (2, 1)]).astype(f32)).astype(bf16)
        outer = hop(part, [(1, 0), (2, 3)])
        return jnp.where((line_rank == 0) | (line_rank == 3), outer, part).astype(f32)

    order = image_order
    for bit in [1] + chip_bits:
        order = together(order, bit, 0).reshape(-1)
    chosen = jnp.sum(
        jnp.where(order[:, None] == jnp.arange(n_images)[None, :], time_bins[None, :], 0), axis=1
    )
    select = (chosen[:, None] == jnp.arange(time_table.shape[0])[None, :]).astype(f32)
    condition = jnp.dot(select, time_table.astype(f32), precision=lax.Precision.HIGHEST)
    silu_cond = jax.nn.silu(condition).astype(bf16)
    row_cond = lax.dynamic_index_in_dim(
        silu_cond.reshape(n_img // 2, column, -1), place, 1, keepdims=False
    )
    mod_width = ada_weight.shape[1]
    ff_width = up_weight.shape[1]
    bias_part = lax.dynamic_update_slice(
        jnp.zeros((mod_width,), f32), ada_bias.astype(f32), (img_rank * ada_bias.shape[0],)
    )
    up_bias_part = lax.dynamic_update_slice(
        jnp.zeros((ff_width,), f32), up_bias.astype(f32), (img_rank * up_bias.shape[0],)
    )
    mod_part = matmul(row_cond, ada_weight) + bias_part[None, :]
    small_plane = n_img == 8 and n_row == 4
    early = [qkv_weight, out_weight, proj_third]
    summed_rows = jnp.concatenate([mod_part.reshape(-1), up_bias_part])
    if small_plane:
        early, arrived, summed_rows = gather_weights(
            early, [tokens, cotangent, targets], summed_rows, group, per
        )
    else:
        early = [fetch(one) for one in early]
        for bit in [1] + chip_bits:
            summed_rows = summed_rows + swap(summed_rows, "img", bit)
    qkv_full, out_full, third_full = early
    modulation = lax.dynamic_index_in_dim(
        summed_rows[: (n_img // 2) * mod_width].reshape(n_img // 2, mod_width),
        img_rank // 2,
        0,
        keepdims=True,
    )
    up_bias_full = summed_rows[(n_img // 2) * mod_width :]
    up_full = fetch(up_weight)
    down_full = fetch(down_weight)
    first_full = fetch(proj_first)
    second_full = fetch(proj_second)

    shift_att, scale_att, gate_att, shift_mlp, scale_mlp, gate_mlp = jnp.split(
        modulation, 6, axis=1
    )
    if small_plane:
        image_counts = lax.dynamic_index_in_dim(together(counts, 1, 0).reshape(column, n_row), place, 0)
        ends = jnp.cumsum(image_counts[0])
        units = core * (length // RW) + jnp.arange(length // RW)
        origin = jnp.sum((units[:, None] >= ends[None, :]).astype(jnp.int32), axis=1)
        before = jnp.sum(
            jnp.where(origin[:, None] == jnp.arange(n_row), ends - image_counts[0], 0), axis=1
        )
        places = origin * slot_len + (units - before) * RW
        source, own_cotangent, own_targets, h_att = compact(
            places.astype(jnp.int32), arrived, shift_att, scale_att
        )
        source = source.astype(f32)
        own_cotangent, own_targets = own_cotangent.astype(f32), own_targets.astype(f32)
    else:
        source = bring(tokens).astype(f32)
        own_cotangent, own_targets = bring(cotangent).astype(f32), bring(targets).astype(f32)
        h_att = modulate(source, shift_att, scale_att).astype(bf16)
    qkv_rows = matmul(h_att, qkv_full).astype(bf16)
    rest = swap(qkv_rows[:, width:], "img", 1)
    bits = [1 << at for at in range(group.bit_length() - 1)]
    for bit in bits:
        near = jnp.concatenate([qkv_rows[:, width:], rest], axis=0)
        rest = jnp.concatenate([rest, swap(near, "row", bit)], axis=0)
    head_mix, log_total = attend(qkv_rows, rest, width)
    attn_out = matmul(head_mix, out_full)
    residual = source + gate_att * attn_out
    h_mlp = modulate(residual, shift_mlp, scale_mlp).astype(bf16)
    pre_act = matmul(h_mlp, up_full) + up_bias_full
    gelu_out = gelu_tanh(pre_act).astype(bf16)
    mlp_out = matmul(gelu_out, down_full)
    lefts = [gelu_out, h_mlp, head_mix, h_att]
    if small_plane:
        lefts = [turn(left) for left in lefts]
        lefts, mlp_out = lax.optimization_barrier((lefts, mlp_out))
    block_own = (residual + gate_mlp * mlp_out).astype(bf16)
    lin_one = matmul(block_own, first_full)
    hid_one = jax.nn.silu(lin_one).astype(bf16)
    left_first = turn(block_own) if small_plane else block_own
    block_spread = give_start(block_own, swap(block_own, "img", 1))
    tied = lax.optimization_barrier((block_spread, left_first, hid_one))
    block_spread, left_first, hid_one = tied
    lin_two = matmul(hid_one, second_full)
    hid_two = jax.nn.silu(lin_two).astype(bf16)
    projected = matmul(hid_two, third_full)

    def align_loss(operand):
        return -0.5 * jnp.sum(alignment(operand, own_targets))

    d_proj = jax.vjp(align_loss, projected)[1](jnp.ones((), f32))[0].astype(bf16)
    third_sum = weight_grad(hid_two, d_proj).astype(bf16)
    third_sum, d_proj = lax.optimization_barrier((third_sum, d_proj))
    third_part = scattered(third_sum)
    d_lin_two = silu_back(lin_two, transposed(d_proj, third_full)).astype(bf16)
    second_sum = weight_grad(hid_one, d_lin_two).astype(bf16)
    second_sum, d_lin_two = lax.optimization_barrier((second_sum, d_lin_two))
    second_part = scattered(second_sum)
    d_lin_one = silu_back(lin_one, transposed(d_lin_two, second_full)).astype(bf16)
    d_res = own_cotangent + transposed(d_lin_one, first_full)
    d_gate_mlp = jnp.sum(d_res * mlp_out, axis=0)
    d_mlp = (d_res * gate_mlp).astype(bf16)
    d_pre = gelu_back(pre_act, transposed(d_mlp, down_full)).astype(bf16)
    bias_sum = jnp.sum(d_pre.astype(f32), axis=0)
    d_resid_norm, d_shift_mlp, d_scale_mlp = jax.vjp(modulate, residual, shift_mlp, scale_mlp)[1](
        transposed(d_pre, up_full)
    )
    d_residual = d_res + d_resid_norm
    d_gate_att = jnp.sum(d_residual * attn_out, axis=0)
    d_attn = (d_residual * gate_att).astype(bf16)
    d_mixed = transposed(d_attn, out_full).astype(bf16)
    third_part, d_mixed = lax.optimization_barrier((third_part, d_mixed))
    d_query, d_own, d_rest, block_given = attend_back(
        qkv_rows,
        rest,
        head_mix,
        d_mixed,
        log_total,
        block_spread,
        (group, per) if small_plane else None,
    )
    if small_plane:
        block_out = give_merge([block_spread[0], *block_given])
    else:
        block_out = give_merge(give_send(block_spread))
    second_part, d_query = lax.optimization_barrier((second_part, d_query))
    d_own = d_own.astype(f32)
    for bit in reversed(bits):
        full = jnp.concatenate([d_own, d_rest.astype(f32)], axis=0)
        half = full.shape[0] // 2
        full = full[:half] + swap(full[half:].astype(bf16), "row", bit).astype(f32)
        d_own, d_rest = full[:length], full[length:].astype(bf16)
    d_own = d_own + swap(d_rest, "img", 1).astype(f32)
    d_qkv = jnp.concatenate([d_query, d_own.astype(bf16)], axis=1)
    d_source, d_shift_att, d_scale_att = jax.vjp(modulate, source, shift_att, scale_att)[1](
        transposed(d_qkv, qkv_full)
    )
    tokens_own = (d_residual + d_source).astype(bf16)
    spread = give_start(tokens_own, swap(tokens_own, "img", 1))
    own_mod = jnp.concatenate(
        [d_shift_att[0], d_scale_att[0], d_gate_att, d_shift_mlp[0], d_scale_mlp[0], d_gate_mlp]
    )
    lefts.append(left_first)
    rights = [d_mlp, d_pre, d_attn, d_qkv, d_lin_one]
    proj_parts = [second_part, third_part]
    if small_plane:
        tied = (spread, proj_parts, rights, own_mod, bias_sum)
        spread, proj_parts, rights, own_mod, bias_sum = lax.optimization_barrier(tied)
        large, d_mod, bias_sum, given, proj_grads = sum_gradients(
            lefts, rights, own_mod, bias_sum, spread, proj_parts, group, per
        )
        grad_tokens = give_merge([spread[0], *given])
    else:
        grad_tokens = give_merge(give_send(spread))
        proj_grads = [row_sum(part, at) for at, part in enumerate(proj_parts)]
        large = [over_row(offload_shards(*pair)) for pair in zip(lefts, rights)]
        slot_id = column * (img_rank // 2) + place
        placed = jnp.zeros((n_images, mod_width), f32)
        placed = lax.dynamic_update_slice(placed, own_mod[None, :], (slot_id, 0))
        d_mod, bias_sum = lax.psum((placed, bias_sum), ("img", "row"))
        d_mod = d_mod.astype(bf16)
    grad_second, grad_third = proj_grads
    grad_down, grad_up, grad_out, grad_qkv, grad_first = large

    grad_ada = weight_grad(silu_cond, d_mod)
    grad_ada_bias = jnp.sum(
        lax.dynamic_slice_in_dim(d_mod, img_rank * ada_bias.shape[0], ada_bias.shape[0], 1).astype(
            f32
        ),
        axis=0,
    )
    d_cond = silu_back(condition, transposed(d_mod, ada_weight))
    grad_table = jnp.dot(select.T, d_cond, precision=lax.Precision.HIGHEST)
    grad_up_bias = lax.dynamic_slice_in_dim(
        bias_sum, img_rank * up_bias.shape[0], up_bias.shape[0], 0
    )
    return (
        block_out,
        grad_tokens,
        grad_table,
        grad_ada,
        grad_ada_bias,
        grad_qkv,
        grad_out,
        grad_up,
        grad_up_bias,
        grad_down,
        grad_first,
        grad_second,
        grad_third,
    )


def solution(mesh):
    return jax.shard_map(
        functools.partial(local, mesh.shape["img"], mesh.shape["row"]),
        mesh=mesh,
        in_specs=(
            P("img", "row", None),
            P("img", "row", None),
            P("img", "row", None),
            P(None, "img"),
            P("img", None),
            P("img"),
            P("img", None),
            P("img", None),
            P("img", None),
            P("img"),
            P("img", None),
            P("img", None),
            P("img", None),
            P("img", None),
            P(),
            P("img"),
            P("img", None),
        ),
        out_specs=(
            P("img", "row", None),
            P("img", "row", None),
            P(None, "img"),
            P("img", None),
            P("img"),
            P("img", None),
            P("img", None),
            P("img", None),
            P("img"),
            P("img", None),
            P("img", None),
            P("img", None),
            P("img", None),
        ),
        check_vma=False,
    )
```

```python
import functools

import jax
import jax.numpy as jnp
from jax import lax
from jax.experimental import pallas as pl
from jax.experimental.pallas import tpu as pltpu
from jax.sharding import PartitionSpec as P

HEADS = 16
HDIM = 72
RW = 32
LROWS = 32
TOTAL = LROWS * RW
SCALE = HDIM ** (-0.5)
LOG2E = 1.4426950408889634
LAST = (((1,), (1,)), ((), ()))
FIRST = (((0,), (0,)), ((), ()))


def normalize(operand):
    centre = operand - jnp.mean(operand, axis=-1, keepdims=True)
    return centre * lax.rsqrt(jnp.mean(centre * centre, axis=-1, keepdims=True) + 1e-06)


def modulate(operand, shift_row, scale_row):
    return normalize(operand) * (1.0 + scale_row) + shift_row


def alignment(projected, targets):
    unit_proj = projected * lax.rsqrt(
        jnp.mean(projected * projected, axis=-1, keepdims=True) + 1e-06
    )
    unit_target = targets * lax.rsqrt(jnp.mean(targets * targets, axis=-1, keepdims=True) + 1e-06)
    return jnp.mean(unit_proj * unit_target, axis=-1)


def matmul(left_side, right_side):
    return jnp.dot(left_side, right_side, preferred_element_type=jnp.float32)


def transposed(left_side, right_side):
    return lax.dot_general(left_side, right_side, LAST, preferred_element_type=jnp.float32)


def weight_grad(left_side, right_side):
    return lax.dot_general(left_side, right_side, FIRST, preferred_element_type=jnp.float32)


def silu_back(operand, gradient):
    return jax.vjp(jax.nn.silu, operand)[1](gradient)[0]


def gelu_tanh(operand):
    return jax.nn.gelu(operand, approximate=True)


def gelu_back(operand, gradient):
    return jax.vjp(gelu_tanh, operand)[1](gradient)[0]


MESH = pl.DeviceIdType.MESH
HALF = HEADS // 2


def head_window(head, width, window):
    first = jnp.minimum(head * HDIM // 128, (width - window) // 128) * 128
    lane = lax.broadcasted_iota(jnp.int32, (1, window), 1) + first - head * HDIM
    return first, (lane >= 0) & (lane < HDIM)


def each_head(body):
    def narrow(at, carry):
        body(2 * at + at // (HALF // 2), 128)
        return carry

    def wide(at, carry):
        body(2 * at + 1 - at // (HALF // 2), 256)
        return carry

    lax.fori_loop(0, HALF, narrow, 0)
    lax.fori_loop(0, HALF, wide, 0)


def columns_at(first, part, width, window):
    return pl.ds(pl.multiple_of(first + part * width, 128), window)


def attend_kernel(own_ref, rest_ref, mix_ref, lse_ref):
    length, width = mix_ref.shape
    block = min(256, length)

    def one_head(head, window):
        first, mine = head_window(head, width, window)
        mix_columns = columns_at(first, 0, width, window)
        key_refs = [own_ref.at[:, columns_at(first, 1, width, window)]]
        key_refs.append(rest_ref.at[:, columns_at(first, 0, width, window)])
        value_refs = [own_ref.at[:, columns_at(first, 2, width, window)]]
        value_refs.append(rest_ref.at[:, columns_at(first, 1, width, window)])
        keys, values = [ref[...] for ref in key_refs], [ref[...] for ref in value_refs]
        for at in range(0, length, block):
            rows = pl.ds(at, block)
            queries = jnp.where(mine, own_ref[rows, mix_columns], jnp.bfloat16(0))
            scores = [
                lax.dot_general(queries, part, LAST, preferred_element_type=jnp.float32)
                for part in keys
            ]
            tops = [jnp.max(part, axis=1, keepdims=True) for part in scores]
            top = jnp.maximum(tops[0], tops[1])
            top = top * (SCALE * LOG2E)
            weights = [jnp.exp2(part * (SCALE * LOG2E) - top) for part in scores]
            total = sum(jnp.sum(part, axis=1, keepdims=True) for part in weights)
            mixed = sum(
                jnp.dot(part.astype(jnp.bfloat16), value, preferred_element_type=jnp.float32)
                for part, value in zip(weights, values)
            )
            mixed = (mixed / total).astype(mix_ref.dtype)
            mix_ref[rows, mix_columns] = jnp.where(mine, mixed, mix_ref[rows, mix_columns])
            log_total = jnp.broadcast_to(top + jnp.log(total) * LOG2E, (block, 128))
            lse_ref[head, :, rows] = log_total.T[:1, :]

    mix_ref[...] = jnp.zeros_like(mix_ref)
    each_head(one_head)


def attend(own, rest, width):
    length, span = own.shape[0], own.shape[0] + rest.shape[0]
    vmem, bf16 = pl.BlockSpec(memory_space=pltpu.VMEM), jnp.bfloat16
    return pl.pallas_call(
        attend_kernel,
        in_specs=[vmem] * 2,
        out_specs=[vmem] * 2,
        out_shape=[
            jax.ShapeDtypeStruct((length, width), bf16),
            jax.ShapeDtypeStruct((HEADS, 1, length), jnp.float32),
        ],
        compiler_params=pltpu.CompilerParams(vmem_limit_bytes=60 * 1024 * 1024),
        cost_estimate=pl.CostEstimate(
            flops=4 * HEADS * length * span * 256,
            bytes_accessed=4 * (length + span) * width * 2,
            transcendentals=HEADS * length * span,
        ),
        name="attend",
    )(own, rest)


def greet(where):
    barrier = pltpu.get_barrier_semaphore()
    pl.semaphore_signal(barrier, inc=1, device_id=where, device_id_type=MESH)


class Give:
    def __init__(self, group, per, spread, given, send_sem, recv_sem):
        self.group, self.per = group, per
        self.spread, self.given, self.send_sem, self.recv_sem = spread, given, send_sem, recv_sem
        self.row = lax.axis_index("row")
        self.slots = given.shape[1]

    def greet(self):
        for shift in range(1, 4):
            greet({"row": lax.rem(self.row + shift, 4)})

    def copy(self, shift, rows):
        return pltpu.make_async_remote_copy(
            src_ref=self.spread.at[shift, rows, :],
            dst_ref=self.given.at[shift - 1, rows, :],
            send_sem=self.send_sem.at[shift - 1],
            recv_sem=self.recv_sem.at[shift - 1],
            device_id={"row": lax.rem(self.row + shift, 4)},
            device_id_type=MESH,
        )

    def from_here(self, row):
        return (row // self.group) // self.per == lax.rem(lax.axis_index("img"), 2)

    def start(self, at, amount):
        @pl.when((at < self.slots // amount) & self.from_here(self.row))
        def _():
            for shift in range(1, 4):
                rows = pl.ds(pl.multiple_of(at * amount, amount), amount)
                self.copy(shift, rows).start()

    def trickle(self, at, amount):
        block = at // 2

        @pl.when((block < self.slots // amount) & self.from_here(self.row))
        def _():
            rows = pl.ds(pl.multiple_of(block * amount, amount), amount)

            @pl.when(lax.rem(at, 2) == 0)
            def _():
                self.copy(1, rows).start()
                self.copy(3, rows).start()

            @pl.when(lax.rem(at, 2) == 1)
            def _():
                self.copy(2, rows).start()

    def wait(self):
        for shift in range(1, 4):
            whole = self.copy(shift, pl.ds(0, self.slots))

            @pl.when(self.from_here(self.row))
            def _(whole=whole):
                whole.wait_send()

            @pl.when(self.from_here(lax.rem(self.row + 4 - shift, 4)))
            def _(whole=whole):
                whole.wait_recv()


def attend_back_kernel(give, own_ref, rest_ref, mix_ref, d_ref, lse_ref, spread, *refs):
    length, width = mix_ref.shape
    block = 256
    if give:
        d_own, given, d_rest, arrived, core_send, core_recv, *sems = refs
        me = lax.axis_index("img")
        sibling = {"img": me + 1 - 2 * lax.rem(me, 2)}
        sender = Give(*give, spread, given, *sems)
        sender.greet()
        greet(sibling)
        pl.semaphore_wait(pltpu.get_barrier_semaphore(), 4)
        sender.start(0, given.shape[1])
    else:
        d_own, d_rest = refs
    for ref in (d_own, d_rest):
        ref[...] = jnp.zeros_like(ref)

    def one_head(head, window):
        first, mine = head_window(head, width, window)
        here = columns_at(first, 0, width, window)
        queries = jnp.where(mine, own_ref[:, here], jnp.bfloat16(0))
        d_mix = jnp.where(mine, d_ref[:, here], jnp.bfloat16(0))
        product = d_mix.astype(jnp.float32) * mix_ref[:, here].astype(jnp.float32)
        delta = lax.dot_general(
            jnp.ones((8, window), jnp.float32),
            product,
            LAST,
            precision=lax.Precision.HIGHEST,
            preferred_element_type=jnp.float32,
        )[:1, :]
        log_total = lse_ref[head]
        d_query = jnp.zeros((length, window), jnp.float32)
        runs = [(own_ref, 1, d_own, at) for at in range(0, length, block)]
        runs += [(rest_ref, 0, d_rest, at) for at in range(0, rest_ref.shape[0], block)]
        for source, part, target, at in runs:
            rows = pl.ds(at, block)
            key_columns = columns_at(first, part, width, window)
            value_columns = columns_at(first, part + 1, width, window)
            keys, values = source[rows, key_columns], source[rows, value_columns]
            scores = lax.dot_general(keys, queries, LAST, preferred_element_type=jnp.float32)
            prob = jnp.exp2(scores * (SCALE * LOG2E) - log_total)
            d_prob = lax.dot_general(values, d_mix, LAST, preferred_element_type=jnp.float32)
            d_score = (prob * (d_prob - delta)).astype(jnp.bfloat16)
            d_key = jnp.dot(d_score, queries, preferred_element_type=jnp.float32) * SCALE
            d_value = jnp.dot(
                prob.astype(jnp.bfloat16), d_mix, preferred_element_type=jnp.float32
            )
            target[rows, key_columns] += d_key.astype(target.dtype)
            target[rows, value_columns] += d_value.astype(target.dtype)
            d_query += lax.dot_general(d_score, keys, FIRST, preferred_element_type=jnp.float32)
        d_query = jnp.where(mine, d_query * SCALE, 0.0)
        d_own[:, here] += d_query.astype(d_own.dtype)

    each_head(one_head)
    if give:
        swap = pltpu.make_async_remote_copy(
            src_ref=d_rest,
            dst_ref=arrived,
            send_sem=core_send,
            recv_sem=core_recv,
            device_id=sibling,
            device_id_type=MESH,
        )
        swap.start()
        swap.wait()
        d_own[:, pl.ds(width, 2 * width)] += arrived[...]
        sender.wait()


def attend_back(own, rest, mixed, d_mix, log_total, spread, give):
    length, width = mixed.shape
    span = length + rest.shape[0]
    vmem, bf16 = pl.BlockSpec(memory_space=pltpu.VMEM), jnp.bfloat16
    hbm = pl.BlockSpec(memory_space=pl.ANY)
    shapes = [jax.ShapeDtypeStruct(own.shape, bf16)]
    specs, scratch, remote = [vmem, vmem], [], {}
    if give:
        shapes.append(jax.ShapeDtypeStruct((spread.shape[0] - 1, *spread.shape[1:]), bf16))
        specs = [vmem, hbm]
        scratch = [pltpu.VMEM(rest.shape, bf16)] * 2
        scratch += [pltpu.SemaphoreType.DMA] * 2 + [pltpu.SemaphoreType.DMA((3,))] * 2
        remote = dict(collective_id=2, has_side_effects=True)
    else:
        shapes.append(jax.ShapeDtypeStruct(rest.shape, bf16))
    return pl.pallas_call(
        functools.partial(attend_back_kernel, give),
        in_specs=[vmem] * 5 + [hbm],
        out_specs=specs,
        out_shape=shapes,
        scratch_shapes=scratch,
        compiler_params=pltpu.CompilerParams(vmem_limit_bytes=60 * 1024 * 1024, **remote),
        cost_estimate=pl.CostEstimate(
            flops=10 * HEADS * length * span * 256,
            bytes_accessed=8 * (length + span) * width * 2,
            transcendentals=HEADS * length * span,
        ),
        name="attend_back",
    )(own, rest, mixed, d_mix, log_total, spread)


TILE_ROWS = 144
TILE_COLUMNS = 384
CUTS = (80, 64)
SLOTS = 4
LINE_SLOTS = 10
LAST_LAG = 15
LINE_TILE = 256
AT_ONCE = 2
GIVE_ROWS = 16
TOKEN_ROWS = 128


def add(one, other):
    return one + other


def mates():
    me = lax.axis_index("img")
    core, x, y = lax.rem(me, 2), lax.rem(me // 2, 2), me // 4
    return me, (core, x, y), (me + 1 - 2 * core, me + 2 - 4 * x, me + 4 - 8 * y)


def gather_kernel(count, group, per, *refs):
    take = iter(refs)
    blocks = [next(take) for _ in range(count)]
    slots = [next(take) for _ in range(3)]
    part = next(take)
    wholes = [next(take) for _ in range(count)]
    arrivals = [next(take) for _ in range(3)]
    total = next(take)
    part_in, part_sum, send_sem, recv_sem, local_sem, slot_send, slot_recv, slot_local = [
        next(take) for _ in range(8)
    ]
    part_send, part_recv, *staged = take
    row = lax.axis_index("row")
    me, (core, x, y), (sibling, x_mate, y_mate) = mates()
    far = x_mate + 4 - 8 * y
    for mate in (sibling, x_mate, y_mate):
        greet({"img": mate})
    for shift in range(1, 4):
        greet({"row": lax.rem(row + shift, 4)})
    pl.semaphore_wait(pltpu.get_barrier_semaphore(), 6)

    def place_of(place):
        return (place // group) // per, lax.rem(place // group, per)

    takes_in = place_of(row)[0] == core

    def by_row(which, shift):
        where = lax.rem(row + 4 - shift, 4)
        return pltpu.make_async_remote_copy(
            src_ref=slots[which].at[place_of(where)[1]],
            dst_ref=arrivals[which].at[row],
            send_sem=slot_send.at[which, shift - 1],
            recv_sem=slot_recv.at[which, shift - 1],
            device_id={"row": where},
            device_id_type=MESH,
        )

    def own_slots(which, leaving):
        source = slots[which].at[place_of(row)[1]]
        stage = staged[count + which]
        if leaving:
            return pltpu.make_async_copy(stage, arrivals[which].at[row], slot_local.at[which])
        return pltpu.make_async_copy(source, stage, slot_local.at[which])

    def by_core(which, shift):
        origin = lax.rem(row + shift, 4)
        source = arrivals[which].at[origin] if shift else slots[which].at[place_of(row)[1]]
        return pltpu.make_async_remote_copy(
            src_ref=source,
            dst_ref=arrivals[which].at[origin],
            send_sem=slot_send.at[which, 3 + shift],
            recv_sem=slot_recv.at[which, 3 + shift],
            device_id={"img": sibling},
            device_id_type=MESH,
        )

    def start_slots(which):
        for shift in range(1, 4):

            @pl.when(place_of(lax.rem(row + 4 - shift, 4))[0] == core)
            def _(shift=shift):
                by_row(which, shift).start()

        @pl.when(takes_in)
        def _():
            own_slots(which, False).start()
            by_core(which, 0).start()

    def stage_slots(which):
        @pl.when(takes_in)
        def _():
            own_slots(which, False).wait()
            own_slots(which, True).start()

    def pass_slots(which):
        for shift in range(1, 4):

            @pl.when(takes_in)
            def _(shift=shift):
                by_row(which, shift).wait_recv()
                by_core(which, shift).start()

    def end_slots(which):
        for shift in range(1, 4):

            @pl.when(place_of(lax.rem(row + 4 - shift, 4))[0] == core)
            def _(shift=shift):
                by_row(which, shift).wait_send()

        @pl.when(takes_in)
        def _():
            own_slots(which, True).wait()
            for shift in range(4):
                by_core(which, shift).wait_send()

        @pl.when(jnp.logical_not(takes_in))
        def _():
            for shift in range(4):
                by_core(which, shift).wait_recv()

    part_mates = [sibling, x_mate, y_mate]

    def part_hop(hop):
        return pltpu.make_async_remote_copy(
            src_ref=part_sum.at[hop - 1] if hop else part,
            dst_ref=part_in.at[hop],
            send_sem=part_send.at[hop],
            recv_sem=part_recv.at[hop],
            device_id={"img": part_mates[hop]},
            device_id_type=MESH,
        )

    def take_part(hop):
        part_hop(hop).wait()
        summed = (part_sum[hop - 1] if hop else part[...]) + part_in[hop]
        if hop == 2:
            total[...] = summed
        else:
            part_sum[hop] = summed
            part_hop(hop + 1).start()

    def halves(at):
        rows = blocks[at].shape[0]
        cut = (rows // 2 + 15) // 16 * 16
        return pl.ds(0, cut), pl.ds(cut, rows - cut)

    def copy(at, kind, source, owner, rows, where):
        return pltpu.make_async_remote_copy(
            src_ref=source,
            dst_ref=wholes[at].at[owner, rows, :],
            send_sem=send_sem.at[at, kind],
            recv_sem=recv_sem.at[at, kind],
            device_id={"img": where},
            device_id_type=MESH,
        )

    def copies(at):
        upper, lower = halves(at)
        block, whole = blocks[at], wholes[at]
        found = [
            copy(at, 0, block.at[upper, :], me, upper, x_mate),
            copy(at, 1, block.at[lower, :], me, lower, y_mate),
            copy(at, 2, block.at[upper, :], me, upper, y_mate),
            copy(at, 3, block.at[lower, :], me, lower, x_mate),
            copy(at, 4, whole.at[x_mate, upper, :], x_mate, upper, y_mate),
            copy(at, 5, whole.at[y_mate, lower, :], y_mate, lower, x_mate),
            copy(at, 6, block.at[upper, :], me, upper, sibling),
            copy(at, 7, block.at[lower, :], me, lower, sibling),
        ]
        for kind, (owner, rows) in enumerate(
            [
                (x_mate, upper),
                (y_mate, lower),
                (y_mate, upper),
                (x_mate, lower),
                (far, upper),
                (far, lower),
            ]
        ):
            found.append(copy(at, 8 + kind, whole.at[owner, rows, :], owner, rows, sibling))
        return found

    every = [copies(at) for at in range(count)]
    locals_ = [
        pltpu.make_async_copy(blocks[at], staged[at], local_sem.at[at]) for at in range(count)
    ]
    moved = [
        pltpu.make_async_copy(staged[at], wholes[at].at[me], local_sem.at[at])
        for at in range(count)
    ]
    part_hop(0).start()
    start_slots(0)
    for at in range(count):
        for kind in (0, 1, 6, 7):
            every[at][kind].start()
        locals_[at].start()
    take_part(0)
    start_slots(1)
    start_slots(2)
    for at in range(count):
        found = every[at]
        found[0].wait_recv()
        found[4].start()
        found[2].start()
        found[8].start()
        found[1].wait_recv()
        found[5].start()
        found[3].start()
        found[9].start()
    take_part(1)
    for at in range(count):
        locals_[at].wait()
        moved[at].start()
    for which in range(3):
        stage_slots(which)
    pass_slots(0)
    for at in range(count):
        found = every[at]
        for kind in (4, 5, 2, 3):
            found[kind].wait_recv()
            found[8 + kind].start()
    take_part(2)
    pass_slots(1)
    pass_slots(2)
    for at in range(count):
        for kind, one in enumerate(every[at]):
            if kind >= 6:
                one.wait_recv()
            one.wait_send()
        moved[at].wait()
    for which in range(3):
        end_slots(which)


def gather_weights(blocks, slots, part, group, per):
    count = len(blocks)
    vmem, hbm = pl.BlockSpec(memory_space=pltpu.VMEM), pl.BlockSpec(memory_space=pl.ANY)
    part_rows = part.size // 128
    results = pl.pallas_call(
        functools.partial(gather_kernel, count, group, per),
        in_specs=[hbm] * (count + 3) + [vmem],
        out_specs=[hbm] * (count + 3) + [vmem],
        out_shape=[
            *[jax.ShapeDtypeStruct((8, *block.shape), block.dtype) for block in blocks],
            *[jax.ShapeDtypeStruct((4, *one.shape[1:]), one.dtype) for one in slots],
            jax.ShapeDtypeStruct((part_rows, 128), jnp.float32),
        ],
        scratch_shapes=[
            pltpu.VMEM((3, part_rows, 128), jnp.float32),
            pltpu.VMEM((2, part_rows, 128), jnp.float32),
            pltpu.SemaphoreType.DMA((count, 14)),
            pltpu.SemaphoreType.DMA((count, 14)),
            pltpu.SemaphoreType.DMA((count,)),
            pltpu.SemaphoreType.DMA((3, 7)),
            pltpu.SemaphoreType.DMA((3, 7)),
            pltpu.SemaphoreType.DMA((3,)),
            pltpu.SemaphoreType.DMA((3,)),
            pltpu.SemaphoreType.DMA((3,)),
            *[pltpu.VMEM(block.shape, block.dtype) for block in blocks],
            *[pltpu.VMEM(one.shape[1:], one.dtype) for one in slots],
        ],
        compiler_params=pltpu.CompilerParams(
            collective_id=1, has_side_effects=True, vmem_limit_bytes=60 * 1024 * 1024
        ),
        cost_estimate=pl.CostEstimate(flops=0, bytes_accessed=200000000, transcendentals=0),
        name="gather_weights",
    )(*blocks, *slots, part.reshape(part_rows, 128))
    wholes = [whole.reshape(-1, whole.shape[-1]) for whole in results[:count]]
    return wholes, results[count : count + 3], results[-1].reshape(-1)


def compact_kernel(places, *refs):
    sources, (shift, scale), targets, (h_att, sems) = refs[:3], refs[3:5], refs[5:8], refs[8:]
    amount = targets[0].shape[0] // RW

    def one(at, carry):
        begin = pl.multiple_of(places[at], RW)
        rows = pl.ds(pl.multiple_of(at * RW, RW), RW)
        for which in range(3):
            source = sources[which].at[pl.ds(begin, RW), :]
            pltpu.make_async_copy(source, targets[which].at[rows, :], sems.at[which]).start()
        return carry

    lax.fori_loop(0, amount, one, 0)

    def wait(which):
        rows = pl.ds(0, targets[which].shape[0])
        source = sources[which].at[rows, :]
        pltpu.make_async_copy(source, targets[which], sems.at[which]).wait()

    wait(0)

    def norm(at, carry):
        rows = pl.ds(pl.multiple_of(at * 64, 64), 64)
        block = targets[0][rows, :].astype(jnp.float32)
        block = modulate(block, shift[...], scale[...])
        h_att[rows, :] = block.astype(jnp.bfloat16)
        return carry

    lax.fori_loop(0, targets[0].shape[0] // 64, norm, 0)
    wait(1)
    wait(2)


def compact(places, slots, shift, scale):
    length = places.shape[0] * RW
    flat = [one.reshape(-1, one.shape[-1]) for one in slots]
    vmem, hbm = pl.BlockSpec(memory_space=pltpu.VMEM), pl.BlockSpec(memory_space=pl.ANY)
    shapes = [jax.ShapeDtypeStruct((length, one.shape[1]), one.dtype) for one in flat]
    return pl.pallas_call(
        compact_kernel,
        in_specs=[pl.BlockSpec(memory_space=pltpu.SMEM), *[hbm] * 3, vmem, vmem],
        out_specs=[vmem] * 4,
        out_shape=[*shapes, shapes[0]],
        scratch_shapes=[pltpu.SemaphoreType.DMA((3,))],
        compiler_params=pltpu.CompilerParams(vmem_limit_bytes=60 * 1024 * 1024),
        cost_estimate=pl.CostEstimate(flops=0, bytes_accessed=8000000, transcendentals=0),
        name="compact",
    )(places, *flat, shift, scale)


class Line:
    def __init__(self, first_stage, slots, buffers, sems):
        self.first_stage, self.slots = first_stage, slots
        self.shard, self.line_one, self.line_two, self.whole, self.line_three = buffers
        self.send_sem, self.recv_sem, self.store_sem, self.credit = sems
        row = lax.axis_index("row")
        self.is_end = (row == 0) | (row == 3)
        self.is_middle = (row == 1) | (row == 2)
        self.inner = {"row": jnp.where(row == 0, 1, 2)}
        self.outer = {"row": jnp.where(row == 1, 0, 3)}
        self.across = {"row": jnp.where(row == 1, 2, 1)}

    def remote(self, stage, slot, source, target, where):
        return pltpu.make_async_remote_copy(
            src_ref=source,
            dst_ref=target,
            send_sem=self.send_sem.at[self.first_stage + stage, slot],
            recv_sem=self.recv_sem.at[self.first_stage + stage, slot],
            device_id=where,
            device_id_type=MESH,
        )

    def inward(self, slot):
        return self.remote(0, slot, self.shard.at[slot], self.line_one.at[slot], self.inner)

    def crosswise(self, slot):
        return self.remote(1, slot, self.shard.at[slot], self.line_two.at[slot], self.across)

    def outward(self, slot):
        return self.remote(2, slot, self.whole.at[slot], self.line_three.at[slot], self.outer)

    def spend(self, stage, chunk):
        @pl.when(chunk >= self.slots)
        def _():
            pl.semaphore_wait(self.credit.at[self.first_stage + stage], 1)

    def repay(self, stage, where):
        pl.semaphore_signal(
            self.credit.at[self.first_stage + stage],
            inc=1,
            device_id=where,
            device_id_type=MESH,
        )

    def load(self, chunk, slot, begin):
        def one(source):
            copy = pltpu.make_async_copy(source, self.shard.at[slot], self.load_sem.at[slot])
            copy.start() if begin else copy.wait()

        self.sources(chunk, one)

    def loaded(self, chunk, slot):
        self.load(chunk, slot, False)
        self.enter(chunk, slot)

    def enter(self, chunk, slot):
        @pl.when(self.is_end)
        def _():
            self.spend(0, chunk)
            self.inward(slot).start()

    def second(self, chunk, slot):
        @pl.when(self.is_middle)
        def _():
            self.inward(slot).wait_recv()
            self.shard[slot] = add(self.shard[slot], self.line_one[slot])
            self.repay(0, self.outer)
            self.spend(1, chunk)
            self.crosswise(slot).start()

    def third(self, chunk, slot):
        @pl.when(self.is_middle)
        def _():
            self.crosswise(slot).wait()
            self.whole[slot] = add(self.shard[slot], self.line_two[slot])
            self.repay(1, self.across)
            self.spend(2, chunk)
            self.outward(slot).start()
            self.store(chunk, slot, self.whole, True)

    def last(self, chunk, slot):
        @pl.when(self.is_end)
        def _():
            self.inward(slot).wait_send()
            self.outward(slot).wait_recv()
            self.store(chunk, slot, self.line_three, True)

    def end(self, chunk, slot):
        @pl.when(self.is_end)
        def _():
            self.store(chunk, slot, self.line_three, False)
            self.repay(2, self.inner)

        @pl.when(self.is_middle)
        def _():
            self.store(chunk, slot, self.whole, False)
            self.outward(slot).wait_send()

    def store(self, chunk, slot, origin, begin):
        def one(target):
            copy = pltpu.make_async_copy(origin.at[slot], target, self.store_sem.at[slot])
            copy.start() if begin else copy.wait()

        self.targets(chunk, one)

    def drain(self):
        @pl.when(self.is_end)
        def _():
            pl.semaphore_wait(self.credit.at[self.first_stage], self.slots)

        @pl.when(self.is_middle)
        def _():
            pl.semaphore_wait(self.credit.at[self.first_stage + 1], self.slots)
            pl.semaphore_wait(self.credit.at[self.first_stage + 2], self.slots)


def pieces(lengths, chunk, body):
    low = 0
    for which, amount in enumerate(lengths):

        @pl.when((chunk >= low) & (chunk < low + amount))
        def _(low=low, which=which):
            body(which, chunk - low)

        low += amount


def tile_columns(at, width):
    return pl.ds(pl.multiple_of(at * width, width), width)


def sum_kernel(count, group, per, *refs):
    take = iter(refs)
    lefts = [next(take) for _ in range(count)]
    right_in = [next(take) for _ in range(count)]
    projection_in, residual_in, source_in, pick_in = [next(take) for _ in range(4)]
    parts = [next(take) for _ in range(2)]
    image_part, bias_part, scale_row = next(take), next(take), next(take)
    results = [next(take) for _ in range(count)]
    given, own_block = next(take), next(take)
    part_results = [next(take) for _ in range(2)]
    every_image, bias_total = next(take), next(take)
    units = next(take)
    rights = [next(take) for _ in range(count)]
    projection, residual, source, pick, both, spread, sums = [next(take) for _ in range(7)]
    grads, core_in, pair, upper_in, lower_in, upper_two, lower_two = [next(take) for _ in range(7)]
    main_buffers = [next(take) for _ in range(5)]
    tall_buffers = [next(take) for _ in range(5)]
    image_sum, image_in, bias_in, small_send, small_recv = [next(take) for _ in range(5)]
    send_sem, recv_sem, store_sem, load_sem, give_send, give_recv, in_sem, unit_sem, credit = take
    row = lax.axis_index("row")
    near_row, far_row = row + 1 - 2 * lax.rem(row, 2), lax.rem(row + 2, 4)
    main = Line(5, LINE_SLOTS, main_buffers, (send_sem, recv_sem, store_sem.at[0], credit))
    tall = Line(8, tall_buffers[0].shape[0], tall_buffers, (send_sem, recv_sem, store_sem.at[1], credit))
    tall.load_sem = load_sem
    across = [-(-right.shape[1] // TILE_COLUMNS) for right in rights]
    lengths = [left.shape[1] * amount for left, amount in zip(lefts, across)]
    chunks = sum(lengths)
    _, (core, x, y), (sibling, x_mate, y_mate) = mates()

    plan, low = [], 0
    for which, left in enumerate(lefts):
        for block in range(left.shape[1]):
            plan.append((low, which, block))
            low += across[which]

    def unit_copy(unit):
        _, which, block = plan[unit]
        origin = lefts[which].at[:, block]
        return pltpu.make_async_copy(origin, units.at[unit % 2], unit_sem.at[unit % 2])

    arrivals = [
        pltpu.make_async_copy(origin, target, in_sem.at[at])
        for at, (origin, target) in enumerate(
            [
                *zip(right_in, rights),
                (projection_in, projection),
                (residual_in, residual),
                (source_in, source),
                (pick_in, pick),
            ]
        )
    ]
    unit_copy(0).start()
    for at in (0, 3, 5, 6, 7, 8, 1, 2, 4):
        arrivals[at].start()

    def both_cuts(chunk, body):
        for parity, cut in enumerate(CUTS):

            @pl.when(lax.rem(chunk, 2) == parity)
            def _(cut=cut):
                body(pl.ds(0, cut), pl.ds(cut, TILE_ROWS - cut), cut)

    def main_targets(chunk, body):
        def one(which, at):
            result = results[which]
            columns = tile_columns(lax.rem(at, across[which]), TILE_COLUMNS)
            body(result.at[at // across[which], :, columns])

        pieces(lengths, chunk, one)

    main.targets = main_targets

    def side_tiles(line, origins, ends):
        amounts = [origin.shape[1] // LINE_TILE for origin in origins]

        def view(refs):
            def visit(chunk, body):
                def one(which, at):
                    body(refs[which].at[:, tile_columns(at, LINE_TILE)])

                pieces(amounts, chunk, one)

            return visit

        line.sources, line.targets = view(origins), view(ends)
        return sum(amounts)

    tall_tiles = side_tiles(tall, parts, part_results)

    def remote(stage, slot, source, target, where):
        return pltpu.make_async_remote_copy(
            src_ref=source,
            dst_ref=target,
            send_sem=send_sem.at[stage, slot],
            recv_sem=recv_sem.at[stage, slot],
            device_id={"img": where},
            device_id_type=MESH,
        )

    def to_sibling(slot):
        return remote(0, slot, grads.at[slot, :, :, 1 - core], core_in.at[slot], sibling)

    def upper_first(slot, rows):
        target = upper_in.at[slot, :, pl.ds(0, rows.size), :]
        return remote(1, slot, pair.at[slot, :, 1 - x, rows, :], target, x_mate)

    def lower_first(slot, rows):
        target = lower_in.at[slot, :, pl.ds(0, rows.size), :]
        return remote(2, slot, pair.at[slot, 1 - y, :, rows, :], target, y_mate)

    def upper_second(slot, rows):
        target = upper_two.at[slot, pl.ds(0, rows.size), :]
        return remote(3, slot, pair.at[slot, 1 - y, x, rows, :], target, y_mate)

    def lower_second(slot, rows):
        target = lower_two.at[slot, pl.ds(0, rows.size), :]
        return remote(4, slot, pair.at[slot, y, 1 - x, rows, :], target, x_mate)

    def spend(stage, chunk):
        @pl.when(chunk >= SLOTS)
        def _():
            pl.semaphore_wait(credit.at[stage], 1)

    def repay(stage, where):
        pl.semaphore_signal(
            credit.at[stage], inc=1, device_id={"img": where}, device_id_type=MESH
        )

    for mate in (sibling, x_mate, y_mate):
        greet({"img": mate})
    sender = Give(group, per, spread, given, give_send, give_recv)
    sender.greet()
    pl.semaphore_wait(pltpu.get_barrier_semaphore(), 6)

    def small(kind, source, target, where):
        return pltpu.make_async_remote_copy(
            src_ref=source,
            dst_ref=target,
            send_sem=small_send.at[kind],
            recv_sem=small_recv.at[kind],
            device_id=where,
            device_id_type=MESH,
        )

    own_half = pl.ds(2 * (row // 2), 2)
    image_hops = [
        (image_sum, image_in, {"img": sibling}),
        (every_image.at[row, y, x], every_image.at[row, y, x], {"img": y_mate}),
        (every_image.at[row, :, x], every_image.at[row, :, x], {"img": x_mate}),
        (every_image.at[row], every_image.at[row], {"row": near_row}),
        (every_image.at[own_half], every_image.at[own_half], {"row": far_row}),
    ]

    def small_hop(hop, begin):
        source, target, where = image_hops[hop]
        image = small(2 * hop, source, target, where)
        bias = small(2 * hop + 1, bias_total if hop else bias_part, bias_in.at[hop], where)
        if begin:
            image.start()
            bias.start()
            return
        image.wait()
        bias.wait()
        if hop == 0:
            summed = image_sum[...] + image_in[...]
            every_image[row, y, x] = summed.astype(jnp.bfloat16)
        bias_total[...] = (bias_total if hop else bias_part)[...] + bias_in[hop]

    def own_shard(chunk, slot):
        line_slot = lax.rem(chunk, LINE_SLOTS)

        def body(upper, lower, cut):
            upper_second(slot, upper).wait()
            main.shard[line_slot, upper, :] = add(
                pair[slot, y, x, upper, :], upper_two[slot, pl.ds(0, cut), :]
            )
            repay(3, y_mate)
            lower_second(slot, lower).wait()
            main.shard[line_slot, lower, :] = add(
                pair[slot, y, x, lower, :], lower_two[slot, pl.ds(0, TILE_ROWS - cut), :]
            )
            repay(4, x_mate)

        both_cuts(chunk, body)
        main.enter(chunk, line_slot)

    def second_axis(chunk, slot):
        def body(upper, lower, cut):
            upper_first(slot, upper).wait()
            for at in range(2):
                pair[slot, at, x, upper, :] = add(
                    pair[slot, at, x, upper, :], upper_in[slot, at, pl.ds(0, cut), :]
                )
            repay(1, x_mate)
            spend(3, chunk)
            upper_second(slot, upper).start()
            lower_first(slot, lower).wait()
            for at in range(2):
                pair[slot, y, at, lower, :] = add(
                    pair[slot, y, at, lower, :], lower_in[slot, at, pl.ds(0, TILE_ROWS - cut), :]
                )
            repay(2, y_mate)
            spend(4, chunk)
            lower_second(slot, lower).start()

        both_cuts(chunk, body)

    def first_axis(chunk, slot):
        to_sibling(slot).wait()
        for at_y in range(2):
            for at_x in range(2):
                pair[slot, at_y, at_x] = add(
                    grads[slot, at_y, at_x, core], core_in[slot, at_y, at_x]
                )
        repay(0, sibling)
        spend(1, chunk)
        spend(2, chunk)

        def body(upper, lower, cut):
            upper_first(slot, upper).start()
            lower_first(slot, lower).start()

        both_cuts(chunk, body)

    def multiply(chunk, slot):
        def one(which, at):
            right = rights[which]
            column, whole_tiles = lax.rem(at, across[which]), right.shape[1] // TILE_COLUMNS
            first_unit = [one_of for _, one_of, _ in plan].index(which)
            slot_of_unit = lax.rem(first_unit + at // across[which], 2)

            def times(values):
                for half in range(2):
                    rows = units[slot_of_unit, pl.ds(4 * half, 4)].reshape(4 * TILE_ROWS, -1)
                    product = jnp.dot(rows, values, preferred_element_type=jnp.float32)
                    grads[slot, half] = product.astype(jnp.bfloat16).reshape(
                        2, 2, TILE_ROWS, TILE_COLUMNS
                    )

            if whole_tiles == across[which]:
                times(right[:, tile_columns(column, TILE_COLUMNS)])
                return

            @pl.when(column < whole_tiles)
            def _():
                times(right[:, tile_columns(column, TILE_COLUMNS)])

            @pl.when(column == whole_tiles)
            def _():
                rest = right[:, whole_tiles * TILE_COLUMNS :]
                gap = jnp.zeros((rest.shape[0], TILE_COLUMNS - rest.shape[1]), rest.dtype)
                times(jnp.concatenate([rest, gap], axis=1))

        for unit, (begin, which, block) in enumerate(plan):

            @pl.when(chunk == begin)
            def _(unit=unit, which=which, block=block):
                unit_copy(unit).wait()
                if unit + 1 < len(plan):
                    unit_copy(unit + 1).start()
                if block == 0 and which != 3:
                    arrivals[which].wait()

        pieces(lengths, chunk, one)
        spend(0, chunk)
        to_sibling(slot).start()

    stages = [
        (LAST_LAG, LINE_SLOTS, main.end),
        (14, LINE_SLOTS, main.last),
        (11, LINE_SLOTS, main.third),
        (8, LINE_SLOTS, main.second),
        (5, SLOTS, own_shard),
        (3, SLOTS, second_axis),
        (1, SLOTS, first_axis),
        (0, SLOTS, multiply),
    ]

    def token_rows(at):
        rows = pl.ds(pl.multiple_of(at * TOKEN_ROWS, TOKEN_ROWS), TOKEN_ROWS)
        grad = lax.dot_general(
            rights[3][rows, :], projection[...], LAST, preferred_element_type=jnp.float32
        )
        tokens = source[rows, :].astype(jnp.float32)
        centre = tokens - jnp.mean(tokens, axis=-1, keepdims=True)
        spread_of = lax.rsqrt(jnp.mean(centre * centre, axis=-1, keepdims=True) + 1e-06)
        norm = centre * spread_of
        sums[0:1, :] += jnp.sum(grad, axis=0, keepdims=True)
        sums[1:2, :] += jnp.sum(grad * norm, axis=0, keepdims=True)
        grad = grad * (1.0 + scale_row[...])
        along = jnp.mean(grad * norm, axis=-1, keepdims=True)
        grad = spread_of * (grad - jnp.mean(grad, axis=-1, keepdims=True) - norm * along)
        both[core, rows, :] = (residual[rows, :] + grad).astype(jnp.bfloat16)

    token_blocks = source.shape[0] // TOKEN_ROWS // AT_ONCE
    lanes = source.shape[1] // 128
    swapped, handed = token_blocks + 2, token_blocks + 2 + 4 // AT_ONCE

    def token_swap():
        return small(10, both.at[core], both.at[core], {"img": sibling})

    def own_copy():
        return pltpu.make_async_copy(spread.at[0], own_block, in_sem.at[9])

    def tokens_step(at):
        @pl.when(at == 0)
        def _():
            for which in (3, 5, 6, 7):
                arrivals[which].wait()
            sums[...] = jnp.zeros_like(sums)

        @pl.when(at < token_blocks)
        def _():
            for which in range(AT_ONCE):
                token_rows(AT_ONCE * at + which)

        @pl.when(at == token_blocks)
        def _():
            token_swap().start()
            image_sum[...] = image_part[...]
            for which in range(2):
                for lane in range(lanes):
                    values = sums[which : which + 1, pl.ds(lane * 128, 128)]
                    image_sum[pl.ds(which * lanes + lane, 1), :] = values

        @pl.when(at == swapped)
        def _():
            token_swap().wait()
            arrivals[8].wait()

        @pl.when((at >= swapped) & (at < handed))
        def _():
            tokens = both[...].reshape(2 * both.shape[1], -1)
            for which in range(AT_ONCE):
                shift = AT_ONCE * (at - swapped) + which
                laid = jnp.dot(pick[shift], tokens, preferred_element_type=jnp.float32)
                spread[shift] = laid.astype(jnp.bfloat16)

        @pl.when(at == handed)
        def _():
            own_copy().start()

        @pl.when(at >= handed)
        def _():
            sender.trickle(at - handed, GIVE_ROWS)

    def step(at, carry):
        for hop in range(5):

            @pl.when(at == token_blocks + 1 + 4 * hop)
            def _(hop=hop):
                small_hop(hop, True)

            @pl.when(at == token_blocks + 4 + 4 * hop)
            def _(hop=hop):
                small_hop(hop, False)

        for lag, body in (
            (8, tall.end),
            (7, tall.last),
            (5, tall.third),
            (3, tall.second),
            (1, tall.loaded),
            (0, functools.partial(tall.load, begin=True)),
        ):
            for which in range(AT_ONCE):
                tile = AT_ONCE * (at - lag) + which

                @pl.when((at >= lag) & (tile < tall_tiles))
                def _(tile=tile, body=body):
                    body(tile, tile)

        for lag, slots, body in stages:
            chunk = at - lag

            @pl.when((chunk >= 0) & (chunk < chunks))
            def _(chunk=chunk, slots=slots, body=body):
                body(chunk, lax.rem(chunk, slots))

        tokens_step(at)
        return carry

    lax.fori_loop(0, chunks + LAST_LAG, step, 0)
    own_copy().wait()
    for stage in range(5):
        pl.semaphore_wait(credit.at[stage], SLOTS)
    for line in (main, tall):
        line.drain()
    sender.wait()


def turn(operand):
    blocks = operand.shape[1] // (8 * TILE_ROWS)
    return operand.T.reshape(8, blocks, TILE_ROWS, operand.shape[0])


def sum_gradients(lefts, rights, tokens_side, image_part, bias_part, scale_row, parts, group, per):
    bf16, f32 = jnp.bfloat16, jnp.float32
    projection, residual, source, pick = tokens_side
    length, width = source.shape
    image_rows, bias_rows = image_part.size // 128, bias_part.size // 128
    padded = -(-image_rows // 16) * 16
    image_part = jnp.pad(image_part.reshape(image_rows, 128), ((0, padded - image_rows), (0, 0)))
    bias_part = bias_part.reshape(bias_rows, 128)
    block = (pick.shape[1], width)
    shapes = [
        *[
            jax.ShapeDtypeStruct(
                (left.shape[1], TILE_ROWS, -(-right.shape[1] // TILE_COLUMNS) * TILE_COLUMNS), bf16
            )
            for left, right in zip(lefts, rights)
        ],
        jax.ShapeDtypeStruct((3, *block), bf16),
        jax.ShapeDtypeStruct(block, bf16),
        *[jax.ShapeDtypeStruct(part.shape, bf16) for part in parts],
        jax.ShapeDtypeStruct((4, 2, 2, padded, 128), bf16),
        jax.ShapeDtypeStruct((bias_rows, 128), f32),
    ]
    tile = (TILE_ROWS, TILE_COLUMNS)
    vmem, hbm = pl.BlockSpec(memory_space=pltpu.VMEM), pl.BlockSpec(memory_space=pl.ANY)
    flops = 2 * sum(left.size * right.shape[1] for left, right in zip(lefts, rights))
    tiles = sum(part.shape[1] // LINE_TILE for part in parts)
    most = max(LINE_SLOTS, tiles)
    results = pl.pallas_call(
        functools.partial(sum_kernel, len(lefts), group, per),
        in_specs=[hbm] * (2 * len(lefts) + 6) + [vmem] * 3,
        out_specs=[hbm] * (len(lefts) + 4) + [vmem] * 2,
        out_shape=shapes,
        scratch_shapes=[
            pltpu.VMEM((2, 8, TILE_ROWS, length), bf16),
            *[pltpu.VMEM(right.shape, bf16) for right in rights],
            pltpu.VMEM(projection.shape, bf16),
            pltpu.VMEM(residual.shape, f32),
            pltpu.VMEM(source.shape, bf16),
            pltpu.VMEM(pick.shape, bf16),
            pltpu.VMEM((2, length, width), bf16),
            pltpu.VMEM((4, *block), bf16),
            pltpu.VMEM((2, width), f32),
            pltpu.VMEM((SLOTS, 2, 2, 2, *tile), bf16),
            pltpu.VMEM((SLOTS, 2, 2, *tile), bf16),
            pltpu.VMEM((SLOTS, 2, 2, *tile), bf16),
            *[pltpu.VMEM((SLOTS, 2, max(CUTS), TILE_COLUMNS), bf16)] * 2,
            *[pltpu.VMEM((SLOTS, max(CUTS), TILE_COLUMNS), bf16)] * 2,
            *[pltpu.VMEM((LINE_SLOTS, *tile), bf16)] * 5,
            *[pltpu.VMEM((tiles, parts[0].shape[0], LINE_TILE), bf16)] * 5,
            pltpu.VMEM((padded, 128), f32),
            pltpu.VMEM((padded, 128), f32),
            pltpu.VMEM((5, bias_rows, 128), f32),
            pltpu.SemaphoreType.DMA((11,)),
            pltpu.SemaphoreType.DMA((11,)),
            pltpu.SemaphoreType.DMA((11, most)),
            pltpu.SemaphoreType.DMA((11, most)),
            pltpu.SemaphoreType.DMA((2, most)),
            pltpu.SemaphoreType.DMA((tiles,)),
            pltpu.SemaphoreType.DMA((3,)),
            pltpu.SemaphoreType.DMA((3,)),
            pltpu.SemaphoreType.DMA((10,)),
            pltpu.SemaphoreType.DMA((2,)),
            pltpu.SemaphoreType.REGULAR((11,)),
        ],
        compiler_params=pltpu.CompilerParams(
            collective_id=0, has_side_effects=True, vmem_limit_bytes=60 * 1024 * 1024
        ),
        cost_estimate=pl.CostEstimate(
            flops=flops, bytes_accessed=600000000, transcendentals=0
        ),
        name="sum_gradients",
    )(*lefts, *rights, *tokens_side, *parts, image_part, bias_part, scale_row)
    take = iter(results)
    summed = [next(take) for _ in lefts]
    summed = [
        result.reshape(-1, result.shape[2])[:, : right.shape[1]].astype(f32)
        for result, right in zip(summed, rights)
    ]
    given, own_block = next(take), next(take)
    parts = [next(take).astype(f32) for _ in parts]
    every_image, bias_total = take
    every_image = every_image[:, :, :, :image_rows].reshape(4, 4, -1).transpose(1, 0, 2)
    return summed, every_image.reshape(16, -1), bias_total.reshape(-1), [own_block, *given], parts


def local(
    n_img,
    n_row,
    tokens,
    cotangent,
    targets,
    time_table,
    ada_weight,
    ada_bias,
    qkv_weight,
    out_weight,
    up_weight,
    up_bias,
    down_weight,
    proj_first,
    proj_second,
    proj_third,
    time_bins,
    image_order,
    counts,
):
    f32, bf16 = jnp.float32, jnp.bfloat16
    per, slot_len, width = tokens.shape
    column = 2 * per
    group = n_row // column
    length = TOTAL // (2 * group)
    n_images = time_bins.shape[0]
    img_rank, row_rank = lax.axis_index("img"), lax.axis_index("row")
    core = img_rank % 2
    place = row_rank // group
    receives = place // per == core

    def swap(operand, axis, bit):
        size = n_img if axis == "img" else n_row
        return lax.ppermute(operand, axis, [(at, at ^ bit) for at in range(size)])

    def route(shift, back):
        pairs = [
            (img * n_row + (row + shift) % n_row, img * n_row + row)
            for img in range(n_img)
            for row in range(n_row)
            if (row // group) // per == img % 2
        ]
        return [(b, a) for a, b in pairs] if back else pairs

    own_counts = lax.dynamic_index_in_dim(counts, place % per, 0, keepdims=False)
    first_of = (jnp.cumsum(own_counts) - own_counts) * RW
    position = jnp.arange(slot_len)
    kept = (row_rank % group) * 2 * length + jnp.arange(2 * length)
    picks = []
    for shift in range(n_row):
        source_row = (row_rank + shift) % n_row
        begin = lax.dynamic_index_in_dim(first_of, source_row, 0, keepdims=False)
        limit = lax.dynamic_index_in_dim(own_counts, source_row, 0, keepdims=False) * RW
        hit = (kept[None, :] == begin + position[:, None]) & (position[:, None] < limit)
        picks.append(hit)
    pick = jnp.concatenate(picks, axis=0).astype(bf16)

    def image_of(shift):
        return (((row_rank - shift) % n_row) // group) % per

    def bring(operand):
        pieces = []
        for shift in range(n_row):
            piece = lax.dynamic_index_in_dim(operand, image_of(shift), 0, keepdims=False)
            if shift:
                piece = lax.ppermute(piece, ("img", "row"), route(shift, False))
            pieces.append(piece)
        packed = weight_grad(pick, jnp.concatenate(pieces, axis=0)).astype(bf16)
        own = lax.dynamic_slice_in_dim(packed, core * length, length, 0)
        other = lax.dynamic_slice_in_dim(packed, (1 - core) * length, length, 0)
        return jnp.where(receives, own, swap(other, "img", 1))

    def give_start(operand, other):
        both = jnp.where(
            core == 0,
            jnp.concatenate([operand, other], axis=0),
            jnp.concatenate([other, operand], axis=0),
        )
        return matmul(pick, both).astype(bf16).reshape(n_row, slot_len, -1)

    def give_send(spread):
        sent = [
            lax.ppermute(spread[shift], ("img", "row"), route(shift, True))
            for shift in range(1, n_row)
        ]
        return [spread[0], *sent]

    def give_merge(blocks):
        images = [jnp.zeros_like(blocks[0]) for _ in range(per)]
        for shift, block in enumerate(blocks):
            sender = ((row_rank - shift) % n_row) // group
            for at in range(per):
                wanted = (sender // per == core) & (sender % per == at)
                if group > 1:
                    images[at] = images[at] + jnp.where(wanted, block, jnp.zeros_like(block))
                else:
                    images[at] = jnp.where(wanted, block, images[at])
        return jnp.stack(images)

    def fetch(operand):
        return lax.all_gather(operand, "img", axis=0, tiled=True)

    chip_bits = [1 << at for at in range(1, n_img.bit_length() - 1)]
    forth, back = chip_bits, chip_bits[-1:] + chip_bits[:-1]

    def side(bit):
        return (img_rank // bit) % 2

    def together(operand, bit, axis):
        blocks = jnp.stack([operand, swap(operand, "img", bit)], axis=axis)
        return jnp.where(side(bit) == 0, blocks, jnp.flip(blocks, axis=axis))

    def scattered(grad):
        return lax.psum_scatter(grad, "img", scatter_dimension=0, tiled=True)

    def offload_shards(left, right):
        return scattered(weight_grad(left, right).astype(bf16))

    def row_sum(part, turn_by):
        ranks = [(at + turn_by) % n_row for at in range(n_row)]
        return lax.psum(part, "row", axis_index_groups=[ranks]).astype(f32)

    fold = n_row // 4
    line_rank = row_rank // fold

    def over_row(part):
        def hop(operand, pairs):
            routes = [(a * fold + low, b * fold + low) for a, b in pairs for low in range(fold)]
            return lax.ppermute(operand, "row", routes)

        for at in range(fold.bit_length() - 1):
            part = (part.astype(f32) + swap(part, "row", 1 << at).astype(f32)).astype(bf16)
        part = (part.astype(f32) + hop(part, [(0, 1), (3, 2)]).astype(f32)).astype(bf16)
        part = (part.astype(f32) + hop(part, [(1, 2), (2, 1)]).astype(f32)).astype(bf16)
        outer = hop(part, [(1, 0), (2, 3)])
        return jnp.where((line_rank == 0) | (line_rank == 3), outer, part).astype(f32)

    order = image_order
    for bit in [1] + chip_bits:
        order = together(order, bit, 0).reshape(-1)
    chosen = jnp.sum(
        jnp.where(order[:, None] == jnp.arange(n_images)[None, :], time_bins[None, :], 0), axis=1
    )
    select = (chosen[:, None] == jnp.arange(time_table.shape[0])[None, :]).astype(f32)
    condition = jnp.dot(select, time_table.astype(f32), precision=lax.Precision.HIGHEST)
    silu_cond = jax.nn.silu(condition).astype(bf16)
    row_cond = lax.dynamic_index_in_dim(
        silu_cond.reshape(n_img // 2, column, -1), place, 1, keepdims=False
    )
    mod_width = ada_weight.shape[1]
    ff_width = up_weight.shape[1]
    bias_part = lax.dynamic_update_slice(
        jnp.zeros((mod_width,), f32), ada_bias.astype(f32), (img_rank * ada_bias.shape[0],)
    )
    up_bias_part = lax.dynamic_update_slice(
        jnp.zeros((ff_width,), f32), up_bias.astype(f32), (img_rank * up_bias.shape[0],)
    )
    mod_part = matmul(row_cond, ada_weight) + bias_part[None, :]
    small_plane = n_img == 8 and n_row == 4
    early = [qkv_weight, out_weight, proj_third]
    summed_rows = jnp.concatenate([mod_part.reshape(-1), up_bias_part])
    if small_plane:
        early, arrived, summed_rows = gather_weights(
            early, [tokens, cotangent, targets], summed_rows, group, per
        )
    else:
        early = [fetch(one) for one in early]
        for bit in [1] + chip_bits:
            summed_rows = summed_rows + swap(summed_rows, "img", bit)
    qkv_full, out_full, third_full = early
    modulation = lax.dynamic_index_in_dim(
        summed_rows[: (n_img // 2) * mod_width].reshape(n_img // 2, mod_width),
        img_rank // 2,
        0,
        keepdims=True,
    )
    up_bias_full = summed_rows[(n_img // 2) * mod_width :]
    up_full = fetch(up_weight)
    down_full = fetch(down_weight)
    first_full = fetch(proj_first)
    second_full = fetch(proj_second)

    shift_att, scale_att, gate_att, shift_mlp, scale_mlp, gate_mlp = jnp.split(
        modulation, 6, axis=1
    )
    if small_plane:
        image_counts = lax.dynamic_index_in_dim(together(counts, 1, 0).reshape(column, n_row), place, 0)
        ends = jnp.cumsum(image_counts[0])
        units = core * (length // RW) + jnp.arange(length // RW)
        origin = jnp.sum((units[:, None] >= ends[None, :]).astype(jnp.int32), axis=1)
        before = jnp.sum(
            jnp.where(origin[:, None] == jnp.arange(n_row), ends - image_counts[0], 0), axis=1
        )
        places = origin * slot_len + (units - before) * RW
        source, own_cotangent, own_targets, h_att = compact(
            places.astype(jnp.int32), arrived, shift_att, scale_att
        )
        source_rows, source = source, source.astype(f32)
        own_cotangent, own_targets = own_cotangent.astype(f32), own_targets.astype(f32)
    else:
        source = bring(tokens).astype(f32)
        own_cotangent, own_targets = bring(cotangent).astype(f32), bring(targets).astype(f32)
        h_att = modulate(source, shift_att, scale_att).astype(bf16)
    qkv_rows = matmul(h_att, qkv_full).astype(bf16)
    rest = swap(qkv_rows[:, width:], "img", 1)
    bits = [1 << at for at in range(group.bit_length() - 1)]
    for bit in bits:
        near = jnp.concatenate([qkv_rows[:, width:], rest], axis=0)
        rest = jnp.concatenate([rest, swap(near, "row", bit)], axis=0)
    head_mix, log_total = attend(qkv_rows, rest, width)
    attn_out = matmul(head_mix, out_full)
    residual = source + gate_att * attn_out
    h_mlp = modulate(residual, shift_mlp, scale_mlp).astype(bf16)
    pre_act = matmul(h_mlp, up_full) + up_bias_full
    gelu_out = gelu_tanh(pre_act).astype(bf16)
    mlp_out = matmul(gelu_out, down_full)
    lefts = [gelu_out, h_mlp, head_mix, h_att]
    if small_plane:
        lefts = [turn(left) for left in lefts]
        lefts, mlp_out = lax.optimization_barrier((lefts, mlp_out))
    block_own = (residual + gate_mlp * mlp_out).astype(bf16)
    lin_one = matmul(block_own, first_full)
    hid_one = jax.nn.silu(lin_one).astype(bf16)
    left_first = turn(block_own) if small_plane else block_own
    block_spread = give_start(block_own, swap(block_own, "img", 1))
    tied = lax.optimization_barrier((block_spread, left_first, hid_one))
    block_spread, left_first, hid_one = tied
    lin_two = matmul(hid_one, second_full)
    hid_two = jax.nn.silu(lin_two).astype(bf16)
    projected = matmul(hid_two, third_full)

    def align_loss(operand):
        return -0.5 * jnp.sum(alignment(operand, own_targets))

    d_proj = jax.vjp(align_loss, projected)[1](jnp.ones((), f32))[0].astype(bf16)
    third_sum = weight_grad(hid_two, d_proj).astype(bf16)
    third_sum, d_proj = lax.optimization_barrier((third_sum, d_proj))
    third_part = scattered(third_sum)
    d_lin_two = silu_back(lin_two, transposed(d_proj, third_full)).astype(bf16)
    second_sum = weight_grad(hid_one, d_lin_two).astype(bf16)
    second_sum, d_lin_two = lax.optimization_barrier((second_sum, d_lin_two))
    second_part = scattered(second_sum)
    d_lin_one = silu_back(lin_one, transposed(d_lin_two, second_full)).astype(bf16)
    d_res = own_cotangent + transposed(d_lin_one, first_full)
    d_gate_mlp = jnp.sum(d_res * mlp_out, axis=0)
    d_mlp = (d_res * gate_mlp).astype(bf16)
    d_pre = gelu_back(pre_act, transposed(d_mlp, down_full)).astype(bf16)
    bias_sum = jnp.sum(d_pre.astype(f32), axis=0)
    d_resid_norm, d_shift_mlp, d_scale_mlp = jax.vjp(modulate, residual, shift_mlp, scale_mlp)[1](
        transposed(d_pre, up_full)
    )
    d_residual = d_res + d_resid_norm
    d_gate_att = jnp.sum(d_residual * attn_out, axis=0)
    d_attn = (d_residual * gate_att).astype(bf16)
    d_mixed = transposed(d_attn, out_full).astype(bf16)
    third_part, d_mixed = lax.optimization_barrier((third_part, d_mixed))
    d_qkv, d_other = attend_back(
        qkv_rows,
        rest,
        head_mix,
        d_mixed,
        log_total,
        block_spread,
        (group, per) if small_plane else None,
    )
    if small_plane:
        block_out = give_merge([block_spread[0], *d_other])
    else:
        block_out = give_merge(give_send(block_spread))
        d_own, d_rest = d_qkv[:, width:].astype(f32), d_other
        for bit in reversed(bits):
            full = jnp.concatenate([d_own, d_rest.astype(f32)], axis=0)
            half = full.shape[0] // 2
            full = full[:half] + swap(full[half:].astype(bf16), "row", bit).astype(f32)
            d_own, d_rest = full[:length], full[length:].astype(bf16)
        d_own = d_own + swap(d_rest, "img", 1).astype(f32)
        d_qkv = jnp.concatenate([d_qkv[:, :width], d_own.astype(bf16)], axis=1)
    second_part, d_qkv = lax.optimization_barrier((second_part, d_qkv))
    late_mod = jnp.concatenate([d_gate_att, d_shift_mlp[0], d_scale_mlp[0], d_gate_mlp])
    lefts.append(left_first)
    rights = [d_mlp, d_pre, d_attn, d_qkv, d_lin_one]
    proj_parts = [second_part, third_part]
    if small_plane:
        tied = (proj_parts, rights, d_residual, late_mod, bias_sum)
        proj_parts, rights, d_residual, late_mod, bias_sum = lax.optimization_barrier(tied)
        large, d_mod, bias_sum, blocks, proj_grads = sum_gradients(
            lefts,
            rights,
            (qkv_full, d_residual, source_rows, pick.reshape(n_row, slot_len, -1)),
            jnp.concatenate([jnp.zeros((2 * width,), f32), late_mod]),
            bias_sum,
            scale_att,
            proj_parts,
            group,
            per,
        )
        grad_tokens = give_merge(blocks)
    else:
        d_source, d_shift_att, d_scale_att = jax.vjp(modulate, source, shift_att, scale_att)[1](
            transposed(d_qkv, qkv_full)
        )
        tokens_own = (d_residual + d_source).astype(bf16)
        grad_tokens = give_merge(give_send(give_start(tokens_own, swap(tokens_own, "img", 1))))
        proj_grads = [row_sum(part, at) for at, part in enumerate(proj_parts)]
        large = [over_row(offload_shards(*pair)) for pair in zip(lefts, rights)]
        own_mod = jnp.concatenate([d_shift_att[0], d_scale_att[0], late_mod])
        slot_id = column * (img_rank // 2) + place
        placed = jnp.zeros((n_images, mod_width), f32)
        placed = lax.dynamic_update_slice(placed, own_mod[None, :], (slot_id, 0))
        d_mod, bias_sum = lax.psum((placed, bias_sum), ("img", "row"))
        d_mod = d_mod.astype(bf16)
    grad_second, grad_third = proj_grads
    grad_down, grad_up, grad_out, grad_qkv, grad_first = large

    grad_ada = weight_grad(silu_cond, d_mod)
    grad_ada_bias = jnp.sum(
        lax.dynamic_slice_in_dim(d_mod, img_rank * ada_bias.shape[0], ada_bias.shape[0], 1).astype(
            f32
        ),
        axis=0,
    )
    d_cond = silu_back(condition, transposed(d_mod, ada_weight))
    grad_table = jnp.dot(select.T, d_cond, precision=lax.Precision.HIGHEST)
    grad_up_bias = lax.dynamic_slice_in_dim(
        bias_sum, img_rank * up_bias.shape[0], up_bias.shape[0], 0
    )
    return (
        block_out,
        grad_tokens,
        grad_table,
        grad_ada,
        grad_ada_bias,
        grad_qkv,
        grad_out,
        grad_up,
        grad_up_bias,
        grad_down,
        grad_first,
        grad_second,
        grad_third,
    )


def solution(mesh):
    return jax.shard_map(
        functools.partial(local, mesh.shape["img"], mesh.shape["row"]),
        mesh=mesh,
        in_specs=(
            P("img", "row", None),
            P("img", "row", None),
            P("img", "row", None),
            P(None, "img"),
            P("img", None),
            P("img"),
            P("img", None),
            P("img", None),
            P("img", None),
            P("img"),
            P("img", None),
            P("img", None),
            P("img", None),
            P("img", None),
            P(),
            P("img"),
            P("img", None),
        ),
        out_specs=(
            P("img", "row", None),
            P("img", "row", None),
            P(None, "img"),
            P("img", None),
            P("img"),
            P("img", None),
            P("img", None),
            P("img", None),
            P("img"),
            P("img", None),
            P("img", None),
            P("img", None),
            P("img", None),
        ),
        check_vma=False,
    )
```

```python
import functools

import jax
import jax.numpy as jnp
from jax import lax
from jax.experimental import pallas as pl
from jax.experimental.pallas import tpu as pltpu
from jax.sharding import PartitionSpec as P

HEADS = 16
HDIM = 72
RW = 32
LROWS = 32
TOTAL = LROWS * RW
SCALE = HDIM ** (-0.5)
LOG2E = 1.4426950408889634
LAST = (((1,), (1,)), ((), ()))
FIRST = (((0,), (0,)), ((), ()))


def normalize(operand):
    centre = operand - jnp.mean(operand, axis=-1, keepdims=True)
    return centre * lax.rsqrt(jnp.mean(centre * centre, axis=-1, keepdims=True) + 1e-06)


def modulate(operand, shift_row, scale_row):
    return normalize(operand) * (1.0 + scale_row) + shift_row


def alignment(projected, targets):
    unit_proj = projected * lax.rsqrt(
        jnp.mean(projected * projected, axis=-1, keepdims=True) + 1e-06
    )
    unit_target = targets * lax.rsqrt(jnp.mean(targets * targets, axis=-1, keepdims=True) + 1e-06)
    return jnp.mean(unit_proj * unit_target, axis=-1)


def matmul(left_side, right_side):
    return jnp.dot(left_side, right_side, preferred_element_type=jnp.float32)


def transposed(left_side, right_side):
    return lax.dot_general(left_side, right_side, LAST, preferred_element_type=jnp.float32)


def weight_grad(left_side, right_side):
    return lax.dot_general(left_side, right_side, FIRST, preferred_element_type=jnp.float32)


def silu_back(operand, gradient):
    return jax.vjp(jax.nn.silu, operand)[1](gradient)[0]


def gelu_tanh(operand):
    return jax.nn.gelu(operand, approximate=True)


def gelu_back(operand, gradient):
    return jax.vjp(gelu_tanh, operand)[1](gradient)[0]


MESH = pl.DeviceIdType.MESH
def mates():
    me = lax.axis_index("img")
    core, x, y = lax.rem(me, 2), lax.rem(me // 2, 2), me // 4
    return me, (core, x, y), (me + 1 - 2 * core, me + 2 - 4 * x, me + 4 - 8 * y)


def greet(where):
    barrier = pltpu.get_barrier_semaphore()
    pl.semaphore_signal(barrier, inc=1, device_id=where, device_id_type=MESH)


def gather_copies(block, whole, send_sem, recv_sem):
    me, (_, _, y), (sibling, x_mate, y_mate) = mates()
    far = x_mate + 4 - 8 * y
    rows = block.shape[0]
    cut = (rows // 2 + 15) // 16 * 16
    upper, lower = pl.ds(0, cut), pl.ds(cut, rows - cut)

    def copy(kind, source, owner, rows, where):
        return pltpu.make_async_remote_copy(
            src_ref=source,
            dst_ref=whole.at[owner, rows, :],
            send_sem=send_sem.at[kind],
            recv_sem=recv_sem.at[kind],
            device_id={"img": where},
            device_id_type=MESH,
        )

    found = [
        copy(0, block.at[upper, :], me, upper, x_mate),
        copy(1, block.at[lower, :], me, lower, y_mate),
        copy(2, block.at[upper, :], me, upper, y_mate),
        copy(3, block.at[lower, :], me, lower, x_mate),
        copy(4, whole.at[x_mate, upper, :], x_mate, upper, y_mate),
        copy(5, whole.at[y_mate, lower, :], y_mate, lower, x_mate),
        copy(6, block.at[upper, :], me, upper, sibling),
        copy(7, block.at[lower, :], me, lower, sibling),
    ]
    come = [(x_mate, upper), (y_mate, lower), (y_mate, upper), (x_mate, lower)]
    come += [(far, upper), (far, lower)]
    for kind, (owner, rows) in enumerate(come):
        found.append(copy(8 + kind, whole.at[owner, rows, :], owner, rows, sibling))
    return found


def first_round(found):
    for kind in (0, 1, 6, 7):
        found[kind].start()


def second_round(found):
    found[0].wait_recv()
    for kind in (4, 2, 8):
        found[kind].start()
    found[1].wait_recv()
    for kind in (5, 3, 9):
        found[kind].start()


def third_round(found):
    for kind in (4, 5, 2, 3):
        found[kind].wait_recv()
        found[8 + kind].start()


def last_round(found):
    for kind, one in enumerate(found):
        if kind >= 6:
            one.wait_recv()
        one.wait_send()


HALF = HEADS // 2


def head_window(head, width, window):
    first = jnp.minimum(head * HDIM // 128, (width - window) // 128) * 128
    lane = lax.broadcasted_iota(jnp.int32, (1, window), 1) + first - head * HDIM
    return first, (lane >= 0) & (lane < HDIM)


def each_head(body):
    def narrow(at, carry):
        body(2 * at + at // (HALF // 2), 128)
        return carry

    def wide(at, carry):
        body(2 * at + 1 - at // (HALF // 2), 256)
        return carry

    lax.fori_loop(0, HALF, narrow, 0)
    lax.fori_loop(0, HALF, wide, 0)


def columns_at(first, part, width, window):
    return pl.ds(pl.multiple_of(first + part * width, 128), window)


def attend_kernel(remote, own_ref, *refs):
    mix_ref, lse_ref, rest_ref = refs[:3] if remote else (refs[1], refs[2], refs[0])
    length, width = mix_ref.shape
    block = min(256, length)
    if remote:
        me = lax.axis_index("img")
        sibling = {"img": me + 1 - 2 * lax.rem(me, 2)}
        greet(sibling)
        pl.semaphore_wait(pltpu.get_barrier_semaphore(), 1)
        swap = pltpu.make_async_remote_copy(
            src_ref=own_ref.at[:, pl.ds(width, 2 * width)],
            dst_ref=rest_ref,
            send_sem=refs[3],
            recv_sem=refs[4],
            device_id=sibling,
            device_id_type=MESH,
        )
        swap.start()

    def one_head(head, window):
        first, mine = head_window(head, width, window)
        mix_columns = columns_at(first, 0, width, window)
        key_refs = [own_ref.at[:, columns_at(first, 1, width, window)]]
        key_refs.append(rest_ref.at[:, columns_at(first, 0, width, window)])
        value_refs = [own_ref.at[:, columns_at(first, 2, width, window)]]
        value_refs.append(rest_ref.at[:, columns_at(first, 1, width, window)])
        keys, values = [ref[...] for ref in key_refs], [ref[...] for ref in value_refs]
        for at in range(0, length, block):
            rows = pl.ds(at, block)
            queries = jnp.where(mine, own_ref[rows, mix_columns], jnp.bfloat16(0))
            scores = [
                lax.dot_general(queries, part, LAST, preferred_element_type=jnp.float32)
                for part in keys
            ]
            tops = [jnp.max(part, axis=1, keepdims=True) for part in scores]
            top = jnp.maximum(tops[0], tops[1])
            top = top * (SCALE * LOG2E)
            weights = [jnp.exp2(part * (SCALE * LOG2E) - top) for part in scores]
            total = sum(jnp.sum(part, axis=1, keepdims=True) for part in weights)
            mixed = sum(
                jnp.dot(part.astype(jnp.bfloat16), value, preferred_element_type=jnp.float32)
                for part, value in zip(weights, values)
            )
            mixed = (mixed / total).astype(mix_ref.dtype)
            mix_ref[rows, mix_columns] = jnp.where(mine, mixed, mix_ref[rows, mix_columns])
            log_total = jnp.broadcast_to(top + jnp.log(total) * LOG2E, (block, 128))
            lse_ref[head, :, rows] = log_total.T[:1, :]

    mix_ref[...] = jnp.zeros_like(mix_ref)
    if remote:
        swap.wait()
    each_head(one_head)


def attend(own, rest, width):
    length, bf16 = own.shape[0], jnp.bfloat16
    vmem = pl.BlockSpec(memory_space=pltpu.VMEM)
    shapes = [
        jax.ShapeDtypeStruct((length, width), bf16),
        jax.ShapeDtypeStruct((HEADS, 1, length), jnp.float32),
    ]
    remote, operands, scratch, params = rest is None, [own], [], {}
    span = 2 * length
    if remote:
        shapes.append(jax.ShapeDtypeStruct((length, 2 * width), bf16))
        scratch = [pltpu.SemaphoreType.DMA] * 2
        params = dict(collective_id=3, has_side_effects=True)
    else:
        operands.append(rest)
        span = length + rest.shape[0]
    return pl.pallas_call(
        functools.partial(attend_kernel, remote),
        in_specs=[vmem] * len(operands),
        out_specs=[vmem] * len(shapes),
        out_shape=shapes,
        scratch_shapes=scratch,
        compiler_params=pltpu.CompilerParams(vmem_limit_bytes=40 * 1024 * 1024, **params),
        cost_estimate=pl.CostEstimate(
            flops=4 * HEADS * length * span * 256,
            bytes_accessed=4 * (length + span) * width * 2,
            transcendentals=HEADS * length * span,
        ),
        name="attend",
    )(*operands)


class Give:
    def __init__(self, group, per, spread, given, send_sem, recv_sem):
        self.group, self.per = group, per
        self.spread, self.given, self.send_sem, self.recv_sem = spread, given, send_sem, recv_sem
        self.row = lax.axis_index("row")
        self.slots = given.shape[1]

    def greet(self):
        for shift in range(1, 4):
            greet({"row": lax.rem(self.row + shift, 4)})

    def copy(self, shift, rows):
        return pltpu.make_async_remote_copy(
            src_ref=self.spread.at[shift, rows, :],
            dst_ref=self.given.at[shift - 1, rows, :],
            send_sem=self.send_sem.at[shift - 1],
            recv_sem=self.recv_sem.at[shift - 1],
            device_id={"row": lax.rem(self.row + shift, 4)},
            device_id_type=MESH,
        )

    def from_here(self, row):
        return (row // self.group) // self.per == lax.rem(lax.axis_index("img"), 2)

    def start(self, at, amount):
        @pl.when((at < self.slots // amount) & self.from_here(self.row))
        def _():
            for shift in range(1, 4):
                rows = pl.ds(pl.multiple_of(at * amount, amount), amount)
                self.copy(shift, rows).start()

    def trickle(self, at, amount):
        block = at // 2

        @pl.when((block < self.slots // amount) & self.from_here(self.row))
        def _():
            rows = pl.ds(pl.multiple_of(block * amount, amount), amount)

            @pl.when(lax.rem(at, 2) == 0)
            def _():
                self.copy(1, rows).start()
                self.copy(3, rows).start()

            @pl.when(lax.rem(at, 2) == 1)
            def _():
                self.copy(2, rows).start()

    def wait(self):
        for shift in range(1, 4):
            whole = self.copy(shift, pl.ds(0, self.slots))

            @pl.when(self.from_here(self.row))
            def _(whole=whole):
                whole.wait_send()

            @pl.when(self.from_here(lax.rem(self.row + 4 - shift, 4)))
            def _(whole=whole):
                whole.wait_recv()


def attend_back_kernel(give, own_ref, rest_ref, mix_ref, d_ref, lse_ref, spread, *refs):
    length, width = mix_ref.shape
    block = 256
    if give:
        d_own, given, d_rest, arrived, core_send, core_recv, *sems = refs
        me = lax.axis_index("img")
        sibling = {"img": me + 1 - 2 * lax.rem(me, 2)}
        sender = Give(*give, spread, given, *sems)
        sender.greet()
        greet(sibling)
        pl.semaphore_wait(pltpu.get_barrier_semaphore(), 4)
        sender.start(0, given.shape[1])
    else:
        d_own, d_rest = refs
    for ref in (d_own, d_rest):
        ref[...] = jnp.zeros_like(ref)

    def one_head(head, window):
        first, mine = head_window(head, width, window)
        here = columns_at(first, 0, width, window)
        queries = jnp.where(mine, own_ref[:, here], jnp.bfloat16(0))
        d_mix = jnp.where(mine, d_ref[:, here], jnp.bfloat16(0))
        product = d_mix.astype(jnp.float32) * mix_ref[:, here].astype(jnp.float32)
        delta = lax.dot_general(
            jnp.ones((8, window), jnp.float32),
            product,
            LAST,
            precision=lax.Precision.HIGHEST,
            preferred_element_type=jnp.float32,
        )[:1, :]
        log_total = lse_ref[head]
        d_query = jnp.zeros((length, window), jnp.float32)
        runs = [(own_ref, 1, d_own, at) for at in range(0, length, block)]
        runs += [(rest_ref, 0, d_rest, at) for at in range(0, rest_ref.shape[0], block)]
        for source, part, target, at in runs:
            rows = pl.ds(at, block)
            key_columns = columns_at(first, part, width, window)
            value_columns = columns_at(first, part + 1, width, window)
            keys, values = source[rows, key_columns], source[rows, value_columns]
            scores = lax.dot_general(keys, queries, LAST, preferred_element_type=jnp.float32)
            prob = jnp.exp2(scores * (SCALE * LOG2E) - log_total)
            d_prob = lax.dot_general(values, d_mix, LAST, preferred_element_type=jnp.float32)
            d_score = (prob * (d_prob - delta)).astype(jnp.bfloat16)
            d_key = jnp.dot(d_score, queries, preferred_element_type=jnp.float32) * SCALE
            d_value = jnp.dot(
                prob.astype(jnp.bfloat16), d_mix, preferred_element_type=jnp.float32
            )
            target[rows, key_columns] += d_key.astype(target.dtype)
            target[rows, value_columns] += d_value.astype(target.dtype)
            d_query += lax.dot_general(d_score, keys, FIRST, preferred_element_type=jnp.float32)
        d_query = jnp.where(mine, d_query * SCALE, 0.0)
        d_own[:, here] += d_query.astype(d_own.dtype)

    each_head(one_head)
    if give:
        swap = pltpu.make_async_remote_copy(
            src_ref=d_rest,
            dst_ref=arrived,
            send_sem=core_send,
            recv_sem=core_recv,
            device_id=sibling,
            device_id_type=MESH,
        )
        swap.start()
        swap.wait()
        d_own[:, pl.ds(width, 2 * width)] += arrived[...]
        sender.wait()


def attend_back(own, rest, mixed, d_mix, log_total, spread, give):
    length, width = mixed.shape
    span = length + rest.shape[0]
    vmem, bf16 = pl.BlockSpec(memory_space=pltpu.VMEM), jnp.bfloat16
    hbm = pl.BlockSpec(memory_space=pl.ANY)
    shapes = [jax.ShapeDtypeStruct(own.shape, bf16)]
    specs, scratch, remote = [vmem, vmem], [], {}
    if give:
        shapes.append(jax.ShapeDtypeStruct((spread.shape[0] - 1, *spread.shape[1:]), bf16))
        specs = [vmem, hbm]
        scratch = [pltpu.VMEM(rest.shape, bf16)] * 2
        scratch += [pltpu.SemaphoreType.DMA] * 2 + [pltpu.SemaphoreType.DMA((3,))] * 2
        remote = dict(collective_id=2, has_side_effects=True)
    else:
        shapes.append(jax.ShapeDtypeStruct(rest.shape, bf16))
    return pl.pallas_call(
        functools.partial(attend_back_kernel, give),
        in_specs=[vmem] * 5 + [hbm],
        out_specs=specs,
        out_shape=shapes,
        scratch_shapes=scratch,
        compiler_params=pltpu.CompilerParams(vmem_limit_bytes=60 * 1024 * 1024, **remote),
        cost_estimate=pl.CostEstimate(
            flops=10 * HEADS * length * span * 256,
            bytes_accessed=8 * (length + span) * width * 2,
            transcendentals=HEADS * length * span,
        ),
        name="attend_back",
    )(own, rest, mixed, d_mix, log_total, spread)


TILE_ROWS = 144
TILE_COLUMNS = 384
CUTS = (80, 64)
SLOTS = 4
LINE_SLOTS = 10
LAST_LAG = 15
LINE_TILE = 256
AT_ONCE = 2
GIVE_ROWS = 16
TOKEN_ROWS = 128


def add(one, other):
    return one + other


def gather_kernel(count, group, per, *refs):
    take = iter(refs)
    blocks = [next(take) for _ in range(count)]
    slots = [next(take) for _ in range(3)]
    part = next(take)
    wholes = [next(take) for _ in range(count)]
    arrivals = [next(take) for _ in range(3)]
    total = next(take)
    part_in, part_sum, send_sem, recv_sem, local_sem, slot_send, slot_recv, slot_local = [
        next(take) for _ in range(8)
    ]
    part_send, part_recv, *staged = take
    row = lax.axis_index("row")
    me, (core, x, y), (sibling, x_mate, y_mate) = mates()
    for mate in (sibling, x_mate, y_mate):
        greet({"img": mate})
    for shift in range(1, 4):
        greet({"row": lax.rem(row + shift, 4)})
    pl.semaphore_wait(pltpu.get_barrier_semaphore(), 6)

    def place_of(place):
        return (place // group) // per, lax.rem(place // group, per)

    takes_in = place_of(row)[0] == core

    def by_row(which, shift):
        where = lax.rem(row + 4 - shift, 4)
        return pltpu.make_async_remote_copy(
            src_ref=slots[which].at[place_of(where)[1]],
            dst_ref=arrivals[which].at[row],
            send_sem=slot_send.at[which, shift - 1],
            recv_sem=slot_recv.at[which, shift - 1],
            device_id={"row": where},
            device_id_type=MESH,
        )

    def own_slots(which, leaving):
        source = slots[which].at[place_of(row)[1]]
        stage = staged[count + which]
        if leaving:
            return pltpu.make_async_copy(stage, arrivals[which].at[row], slot_local.at[which])
        return pltpu.make_async_copy(source, stage, slot_local.at[which])

    def by_core(which, shift):
        origin = lax.rem(row + shift, 4)
        source = arrivals[which].at[origin] if shift else slots[which].at[place_of(row)[1]]
        return pltpu.make_async_remote_copy(
            src_ref=source,
            dst_ref=arrivals[which].at[origin],
            send_sem=slot_send.at[which, 3 + shift],
            recv_sem=slot_recv.at[which, 3 + shift],
            device_id={"img": sibling},
            device_id_type=MESH,
        )

    def start_slots(which):
        for shift in range(1, 4):

            @pl.when(place_of(lax.rem(row + 4 - shift, 4))[0] == core)
            def _(shift=shift):
                by_row(which, shift).start()

        @pl.when(takes_in)
        def _():
            own_slots(which, False).start()
            by_core(which, 0).start()

    def stage_slots(which):
        @pl.when(takes_in)
        def _():
            own_slots(which, False).wait()
            own_slots(which, True).start()

    def pass_slots(which):
        for shift in range(1, 4):

            @pl.when(takes_in)
            def _(shift=shift):
                by_row(which, shift).wait_recv()
                by_core(which, shift).start()

    def end_slots(which):
        for shift in range(1, 4):

            @pl.when(place_of(lax.rem(row + 4 - shift, 4))[0] == core)
            def _(shift=shift):
                by_row(which, shift).wait_send()

        @pl.when(takes_in)
        def _():
            own_slots(which, True).wait()
            for shift in range(4):
                by_core(which, shift).wait_send()

        @pl.when(jnp.logical_not(takes_in))
        def _():
            for shift in range(4):
                by_core(which, shift).wait_recv()

    part_mates = [sibling, x_mate, y_mate]

    def part_hop(hop):
        return pltpu.make_async_remote_copy(
            src_ref=part_sum.at[hop - 1] if hop else part,
            dst_ref=part_in.at[hop],
            send_sem=part_send.at[hop],
            recv_sem=part_recv.at[hop],
            device_id={"img": part_mates[hop]},
            device_id_type=MESH,
        )

    def take_part(hop):
        part_hop(hop).wait()
        summed = (part_sum[hop - 1] if hop else part[...]) + part_in[hop]
        if hop == 2:
            total[...] = summed
        else:
            part_sum[hop] = summed
            part_hop(hop + 1).start()

    every = [
        gather_copies(blocks[at], wholes[at], send_sem.at[at], recv_sem.at[at])
        for at in range(count)
    ]
    locals_ = [
        pltpu.make_async_copy(blocks[at], staged[at], local_sem.at[at]) for at in range(count)
    ]
    moved = [
        pltpu.make_async_copy(staged[at], wholes[at].at[me], local_sem.at[at])
        for at in range(count)
    ]
    part_hop(0).start()
    start_slots(0)
    for at in range(count):
        first_round(every[at])
        locals_[at].start()
    take_part(0)
    start_slots(1)
    start_slots(2)
    for found in every:
        second_round(found)
    take_part(1)
    for at in range(count):
        locals_[at].wait()
        moved[at].start()
    for which in range(3):
        stage_slots(which)
    pass_slots(0)
    for found in every:
        third_round(found)
    take_part(2)
    pass_slots(1)
    pass_slots(2)
    for at in range(count):
        last_round(every[at])
        moved[at].wait()
    for which in range(3):
        end_slots(which)


def gather_weights(blocks, slots, part, group, per):
    count = len(blocks)
    vmem, hbm = pl.BlockSpec(memory_space=pltpu.VMEM), pl.BlockSpec(memory_space=pl.ANY)
    part_rows = part.size // 128
    results = pl.pallas_call(
        functools.partial(gather_kernel, count, group, per),
        in_specs=[hbm] * (count + 3) + [vmem],
        out_specs=[hbm] * (count + 3) + [vmem],
        out_shape=[
            *[jax.ShapeDtypeStruct((8, *block.shape), block.dtype) for block in blocks],
            *[jax.ShapeDtypeStruct((4, *one.shape[1:]), one.dtype) for one in slots],
            jax.ShapeDtypeStruct((part_rows, 128), jnp.float32),
        ],
        scratch_shapes=[
            pltpu.VMEM((3, part_rows, 128), jnp.float32),
            pltpu.VMEM((2, part_rows, 128), jnp.float32),
            pltpu.SemaphoreType.DMA((count, 14)),
            pltpu.SemaphoreType.DMA((count, 14)),
            pltpu.SemaphoreType.DMA((count,)),
            pltpu.SemaphoreType.DMA((3, 7)),
            pltpu.SemaphoreType.DMA((3, 7)),
            pltpu.SemaphoreType.DMA((3,)),
            pltpu.SemaphoreType.DMA((3,)),
            pltpu.SemaphoreType.DMA((3,)),
            *[pltpu.VMEM(block.shape, block.dtype) for block in blocks],
            *[pltpu.VMEM(one.shape[1:], one.dtype) for one in slots],
        ],
        compiler_params=pltpu.CompilerParams(
            collective_id=1, has_side_effects=True, vmem_limit_bytes=60 * 1024 * 1024
        ),
        cost_estimate=pl.CostEstimate(flops=0, bytes_accessed=200000000, transcendentals=0),
        name="gather_weights",
    )(*blocks, *slots, part.reshape(part_rows, 128))
    wholes = [whole.reshape(-1, whole.shape[-1]) for whole in results[:count]]
    return wholes, results[count : count + 3], results[-1].reshape(-1)


def compact_kernel(places, *refs):
    sources, (shift, scale), targets, (h_att, sems) = refs[:3], refs[3:5], refs[5:8], refs[8:]
    amount = targets[0].shape[0] // RW

    def one(at, carry):
        begin = pl.multiple_of(places[at], RW)
        rows = pl.ds(pl.multiple_of(at * RW, RW), RW)
        for which in range(3):
            source = sources[which].at[pl.ds(begin, RW), :]
            pltpu.make_async_copy(source, targets[which].at[rows, :], sems.at[which]).start()
        return carry

    lax.fori_loop(0, amount, one, 0)

    def wait(which):
        rows = pl.ds(0, targets[which].shape[0])
        source = sources[which].at[rows, :]
        pltpu.make_async_copy(source, targets[which], sems.at[which]).wait()

    wait(0)

    def norm(at, carry):
        rows = pl.ds(pl.multiple_of(at * 64, 64), 64)
        block = targets[0][rows, :].astype(jnp.float32)
        block = modulate(block, shift[...], scale[...])
        h_att[rows, :] = block.astype(jnp.bfloat16)
        return carry

    lax.fori_loop(0, targets[0].shape[0] // 64, norm, 0)
    wait(1)
    wait(2)


def compact(places, slots, shift, scale):
    length = places.shape[0] * RW
    flat = [one.reshape(-1, one.shape[-1]) for one in slots]
    vmem, hbm = pl.BlockSpec(memory_space=pltpu.VMEM), pl.BlockSpec(memory_space=pl.ANY)
    shapes = [jax.ShapeDtypeStruct((length, one.shape[1]), one.dtype) for one in flat]
    return pl.pallas_call(
        compact_kernel,
        in_specs=[pl.BlockSpec(memory_space=pltpu.SMEM), *[hbm] * 3, vmem, vmem],
        out_specs=[vmem] * 4,
        out_shape=[*shapes, shapes[0]],
        scratch_shapes=[pltpu.SemaphoreType.DMA((3,))],
        compiler_params=pltpu.CompilerParams(vmem_limit_bytes=60 * 1024 * 1024),
        cost_estimate=pl.CostEstimate(flops=0, bytes_accessed=8000000, transcendentals=0),
        name="compact",
    )(places, *flat, shift, scale)


class Line:
    def __init__(self, first_stage, slots, buffers, sems):
        self.first_stage, self.slots = first_stage, slots
        self.shard, self.line_one, self.line_two, self.whole, self.line_three = buffers
        self.send_sem, self.recv_sem, self.store_sem, self.credit = sems
        row = lax.axis_index("row")
        self.is_end = (row == 0) | (row == 3)
        self.is_middle = (row == 1) | (row == 2)
        self.inner = {"row": jnp.where(row == 0, 1, 2)}
        self.outer = {"row": jnp.where(row == 1, 0, 3)}
        self.across = {"row": jnp.where(row == 1, 2, 1)}

    def remote(self, stage, slot, source, target, where):
        return pltpu.make_async_remote_copy(
            src_ref=source,
            dst_ref=target,
            send_sem=self.send_sem.at[self.first_stage + stage, slot],
            recv_sem=self.recv_sem.at[self.first_stage + stage, slot],
            device_id=where,
            device_id_type=MESH,
        )

    def inward(self, slot):
        return self.remote(0, slot, self.shard.at[slot], self.line_one.at[slot], self.inner)

    def crosswise(self, slot):
        return self.remote(1, slot, self.shard.at[slot], self.line_two.at[slot], self.across)

    def outward(self, slot):
        return self.remote(2, slot, self.whole.at[slot], self.line_three.at[slot], self.outer)

    def spend(self, stage, chunk):
        @pl.when(chunk >= self.slots)
        def _():
            pl.semaphore_wait(self.credit.at[self.first_stage + stage], 1)

    def repay(self, stage, where):
        pl.semaphore_signal(
            self.credit.at[self.first_stage + stage],
            inc=1,
            device_id=where,
            device_id_type=MESH,
        )

    def load(self, chunk, slot, begin):
        def one(source):
            copy = pltpu.make_async_copy(source, self.shard.at[slot], self.load_sem.at[slot])
            copy.start() if begin else copy.wait()

        self.sources(chunk, one)

    def loaded(self, chunk, slot):
        self.load(chunk, slot, False)
        self.enter(chunk, slot)

    def enter(self, chunk, slot):
        @pl.when(self.is_end)
        def _():
            self.spend(0, chunk)
            self.inward(slot).start()

    def second(self, chunk, slot):
        @pl.when(self.is_middle)
        def _():
            self.inward(slot).wait_recv()
            self.shard[slot] = add(self.shard[slot], self.line_one[slot])
            self.repay(0, self.outer)
            self.spend(1, chunk)
            self.crosswise(slot).start()

    def third(self, chunk, slot):
        @pl.when(self.is_middle)
        def _():
            self.crosswise(slot).wait()
            self.whole[slot] = add(self.shard[slot], self.line_two[slot])
            self.repay(1, self.across)
            self.spend(2, chunk)
            self.outward(slot).start()
            self.store(chunk, slot, self.whole, True)

    def last(self, chunk, slot):
        @pl.when(self.is_end)
        def _():
            self.inward(slot).wait_send()
            self.outward(slot).wait_recv()
            self.store(chunk, slot, self.line_three, True)

    def end(self, chunk, slot):
        @pl.when(self.is_end)
        def _():
            self.store(chunk, slot, self.line_three, False)
            self.repay(2, self.inner)

        @pl.when(self.is_middle)
        def _():
            self.store(chunk, slot, self.whole, False)
            self.outward(slot).wait_send()

    def store(self, chunk, slot, origin, begin):
        def one(target):
            copy = pltpu.make_async_copy(origin.at[slot], target, self.store_sem.at[slot])
            copy.start() if begin else copy.wait()

        self.targets(chunk, one)

    def drain(self):
        @pl.when(self.is_end)
        def _():
            pl.semaphore_wait(self.credit.at[self.first_stage], self.slots)

        @pl.when(self.is_middle)
        def _():
            pl.semaphore_wait(self.credit.at[self.first_stage + 1], self.slots)
            pl.semaphore_wait(self.credit.at[self.first_stage + 2], self.slots)


def pieces(lengths, chunk, body):
    low = 0
    for which, amount in enumerate(lengths):

        @pl.when((chunk >= low) & (chunk < low + amount))
        def _(low=low, which=which):
            body(which, chunk - low)

        low += amount


def tile_columns(at, width):
    return pl.ds(pl.multiple_of(at * width, width), width)


def sum_kernel(count, group, per, *refs):
    take = iter(refs)
    lefts = [next(take) for _ in range(count)]
    right_in = [next(take) for _ in range(count)]
    projection_in, residual_in, source_in, pick_in = [next(take) for _ in range(4)]
    parts = [next(take) for _ in range(2)]
    image_part, bias_part, scale_row = next(take), next(take), next(take)
    results = [next(take) for _ in range(count)]
    given, own_block = next(take), next(take)
    part_results = [next(take) for _ in range(2)]
    every_image, bias_total = next(take), next(take)
    units = next(take)
    rights = [next(take) for _ in range(count)]
    projection, residual, source, pick, both, spread, sums = [next(take) for _ in range(7)]
    grads, core_in, pair, upper_in, lower_in, upper_two, lower_two = [next(take) for _ in range(7)]
    main_buffers = [next(take) for _ in range(5)]
    tall_buffers = [next(take) for _ in range(5)]
    image_sum, image_in, bias_in, small_send, small_recv = [next(take) for _ in range(5)]
    send_sem, recv_sem, store_sem, load_sem, give_send, give_recv, in_sem, unit_sem, credit = take
    row = lax.axis_index("row")
    near_row, far_row = row + 1 - 2 * lax.rem(row, 2), lax.rem(row + 2, 4)
    main = Line(5, LINE_SLOTS, main_buffers, (send_sem, recv_sem, store_sem.at[0], credit))
    tall = Line(8, tall_buffers[0].shape[0], tall_buffers, (send_sem, recv_sem, store_sem.at[1], credit))
    tall.load_sem = load_sem
    across = [-(-right.shape[1] // TILE_COLUMNS) for right in rights]
    lengths = [left.shape[1] * amount for left, amount in zip(lefts, across)]
    chunks = sum(lengths)
    _, (core, x, y), (sibling, x_mate, y_mate) = mates()

    plan, low = [], 0
    for which, left in enumerate(lefts):
        for block in range(left.shape[1]):
            plan.append((low, which, block))
            low += across[which]

    def unit_copy(unit):
        _, which, block = plan[unit]
        origin = lefts[which].at[:, block]
        return pltpu.make_async_copy(origin, units.at[unit % 2], unit_sem.at[unit % 2])

    arrivals = [
        pltpu.make_async_copy(origin, target, in_sem.at[at])
        for at, (origin, target) in enumerate(
            [
                *zip(right_in, rights),
                (projection_in, projection),
                (residual_in, residual),
                (source_in, source),
                (pick_in, pick),
            ]
        )
    ]
    unit_copy(0).start()
    for at in (0, 3, 5, 6, 7, 8, 1, 2, 4):
        arrivals[at].start()

    def both_cuts(chunk, body):
        for parity, cut in enumerate(CUTS):

            @pl.when(lax.rem(chunk, 2) == parity)
            def _(cut=cut):
                body(pl.ds(0, cut), pl.ds(cut, TILE_ROWS - cut), cut)

    def main_targets(chunk, body):
        def one(which, at):
            result = results[which]
            columns = tile_columns(lax.rem(at, across[which]), TILE_COLUMNS)
            body(result.at[at // across[which], :, columns])

        pieces(lengths, chunk, one)

    main.targets = main_targets

    def side_tiles(line, origins, ends):
        amounts = [origin.shape[1] // LINE_TILE for origin in origins]

        def view(refs):
            def visit(chunk, body):
                def one(which, at):
                    body(refs[which].at[:, tile_columns(at, LINE_TILE)])

                pieces(amounts, chunk, one)

            return visit

        line.sources, line.targets = view(origins), view(ends)
        return sum(amounts)

    tall_tiles = side_tiles(tall, parts, part_results)

    def remote(stage, slot, source, target, where):
        return pltpu.make_async_remote_copy(
            src_ref=source,
            dst_ref=target,
            send_sem=send_sem.at[stage, slot],
            recv_sem=recv_sem.at[stage, slot],
            device_id={"img": where},
            device_id_type=MESH,
        )

    def to_sibling(slot):
        return remote(0, slot, grads.at[slot, :, :, 1 - core], core_in.at[slot], sibling)

    def upper_first(slot, rows):
        target = upper_in.at[slot, :, pl.ds(0, rows.size), :]
        return remote(1, slot, pair.at[slot, :, 1 - x, rows, :], target, x_mate)

    def lower_first(slot, rows):
        target = lower_in.at[slot, :, pl.ds(0, rows.size), :]
        return remote(2, slot, pair.at[slot, 1 - y, :, rows, :], target, y_mate)

    def upper_second(slot, rows):
        target = upper_two.at[slot, pl.ds(0, rows.size), :]
        return remote(3, slot, pair.at[slot, 1 - y, x, rows, :], target, y_mate)

    def lower_second(slot, rows):
        target = lower_two.at[slot, pl.ds(0, rows.size), :]
        return remote(4, slot, pair.at[slot, y, 1 - x, rows, :], target, x_mate)

    def spend(stage, chunk):
        @pl.when(chunk >= SLOTS)
        def _():
            pl.semaphore_wait(credit.at[stage], 1)

    def repay(stage, where):
        pl.semaphore_signal(
            credit.at[stage], inc=1, device_id={"img": where}, device_id_type=MESH
        )

    for mate in (sibling, x_mate, y_mate):
        greet({"img": mate})
    sender = Give(group, per, spread, given, give_send, give_recv)
    sender.greet()
    pl.semaphore_wait(pltpu.get_barrier_semaphore(), 6)

    def small(kind, source, target, where):
        return pltpu.make_async_remote_copy(
            src_ref=source,
            dst_ref=target,
            send_sem=small_send.at[kind],
            recv_sem=small_recv.at[kind],
            device_id=where,
            device_id_type=MESH,
        )

    own_half = pl.ds(2 * (row // 2), 2)
    image_hops = [
        (image_sum, image_in, {"img": sibling}),
        (every_image.at[row, y, x], every_image.at[row, y, x], {"img": y_mate}),
        (every_image.at[row, :, x], every_image.at[row, :, x], {"img": x_mate}),
        (every_image.at[row], every_image.at[row], {"row": near_row}),
        (every_image.at[own_half], every_image.at[own_half], {"row": far_row}),
    ]

    def small_hop(hop, begin):
        source, target, where = image_hops[hop]
        image = small(2 * hop, source, target, where)
        bias = small(2 * hop + 1, bias_total if hop else bias_part, bias_in.at[hop], where)
        if begin:
            image.start()
            bias.start()
            return
        image.wait()
        bias.wait()
        if hop == 0:
            summed = image_sum[...] + image_in[...]
            every_image[row, y, x] = summed.astype(jnp.bfloat16)
        bias_total[...] = (bias_total if hop else bias_part)[...] + bias_in[hop]

    def own_shard(chunk, slot):
        line_slot = lax.rem(chunk, LINE_SLOTS)

        def body(upper, lower, cut):
            upper_second(slot, upper).wait()
            main.shard[line_slot, upper, :] = add(
                pair[slot, y, x, upper, :], upper_two[slot, pl.ds(0, cut), :]
            )
            repay(3, y_mate)
            lower_second(slot, lower).wait()
            main.shard[line_slot, lower, :] = add(
                pair[slot, y, x, lower, :], lower_two[slot, pl.ds(0, TILE_ROWS - cut), :]
            )
            repay(4, x_mate)

        both_cuts(chunk, body)
        main.enter(chunk, line_slot)

    def second_axis(chunk, slot):
        def body(upper, lower, cut):
            upper_first(slot, upper).wait()
            for at in range(2):
                pair[slot, at, x, upper, :] = add(
                    pair[slot, at, x, upper, :], upper_in[slot, at, pl.ds(0, cut), :]
                )
            repay(1, x_mate)
            spend(3, chunk)
            upper_second(slot, upper).start()
            lower_first(slot, lower).wait()
            for at in range(2):
                pair[slot, y, at, lower, :] = add(
                    pair[slot, y, at, lower, :], lower_in[slot, at, pl.ds(0, TILE_ROWS - cut), :]
                )
            repay(2, y_mate)
            spend(4, chunk)
            lower_second(slot, lower).start()

        both_cuts(chunk, body)

    def first_axis(chunk, slot):
        to_sibling(slot).wait()
        for at_y in range(2):
            for at_x in range(2):
                pair[slot, at_y, at_x] = add(
                    grads[slot, at_y, at_x, core], core_in[slot, at_y, at_x]
                )
        repay(0, sibling)
        spend(1, chunk)
        spend(2, chunk)

        def body(upper, lower, cut):
            upper_first(slot, upper).start()
            lower_first(slot, lower).start()

        both_cuts(chunk, body)

    def multiply(chunk, slot):
        def one(which, at):
            right = rights[which]
            column, whole_tiles = lax.rem(at, across[which]), right.shape[1] // TILE_COLUMNS
            first_unit = [one_of for _, one_of, _ in plan].index(which)
            slot_of_unit = lax.rem(first_unit + at // across[which], 2)

            def times(values):
                for half in range(2):
                    rows = units[slot_of_unit, pl.ds(4 * half, 4)].reshape(4 * TILE_ROWS, -1)
                    product = jnp.dot(rows, values, preferred_element_type=jnp.float32)
                    grads[slot, half] = product.astype(jnp.bfloat16).reshape(
                        2, 2, TILE_ROWS, TILE_COLUMNS
                    )

            if whole_tiles == across[which]:
                times(right[:, tile_columns(column, TILE_COLUMNS)])
                return

            @pl.when(column < whole_tiles)
            def _():
                times(right[:, tile_columns(column, TILE_COLUMNS)])

            @pl.when(column == whole_tiles)
            def _():
                rest = right[:, whole_tiles * TILE_COLUMNS :]
                gap = jnp.zeros((rest.shape[0], TILE_COLUMNS - rest.shape[1]), rest.dtype)
                times(jnp.concatenate([rest, gap], axis=1))

        for unit, (begin, which, block) in enumerate(plan):

            @pl.when(chunk == begin)
            def _(unit=unit, which=which, block=block):
                unit_copy(unit).wait()
                if unit + 1 < len(plan):
                    unit_copy(unit + 1).start()
                if block == 0 and which != 3:
                    arrivals[which].wait()

        pieces(lengths, chunk, one)
        spend(0, chunk)
        to_sibling(slot).start()

    stages = [
        (LAST_LAG, LINE_SLOTS, main.end),
        (14, LINE_SLOTS, main.last),
        (11, LINE_SLOTS, main.third),
        (8, LINE_SLOTS, main.second),
        (5, SLOTS, own_shard),
        (3, SLOTS, second_axis),
        (1, SLOTS, first_axis),
        (0, SLOTS, multiply),
    ]

    def token_rows(at):
        rows = pl.ds(pl.multiple_of(at * TOKEN_ROWS, TOKEN_ROWS), TOKEN_ROWS)
        grad = lax.dot_general(
            rights[3][rows, :], projection[...], LAST, preferred_element_type=jnp.float32
        )
        tokens = source[rows, :].astype(jnp.float32)
        centre = tokens - jnp.mean(tokens, axis=-1, keepdims=True)
        spread_of = lax.rsqrt(jnp.mean(centre * centre, axis=-1, keepdims=True) + 1e-06)
        norm = centre * spread_of
        sums[0:1, :] += jnp.sum(grad, axis=0, keepdims=True)
        sums[1:2, :] += jnp.sum(grad * norm, axis=0, keepdims=True)
        grad = grad * (1.0 + scale_row[...])
        along = jnp.mean(grad * norm, axis=-1, keepdims=True)
        grad = spread_of * (grad - jnp.mean(grad, axis=-1, keepdims=True) - norm * along)
        both[core, rows, :] = (residual[rows, :] + grad).astype(jnp.bfloat16)

    token_blocks = 1 + source.shape[0] // TOKEN_ROWS
    lanes = source.shape[1] // 128
    swapped, handed = token_blocks + 2, token_blocks + 2 + 4 // AT_ONCE

    def token_swap():
        return small(10, both.at[core], both.at[core], {"img": sibling})

    def own_copy():
        return pltpu.make_async_copy(spread.at[0], own_block, in_sem.at[9])

    def tokens_step(at):
        @pl.when(at == 1)
        def _():
            for which in (3, 5, 6, 7):
                arrivals[which].wait()
            sums[...] = jnp.zeros_like(sums)

        @pl.when((at >= 1) & (at < token_blocks))
        def _():
            token_rows(at - 1)

        @pl.when(at == token_blocks)
        def _():
            token_swap().start()
            image_sum[...] = image_part[...]
            for which in range(2):
                for lane in range(lanes):
                    values = sums[which : which + 1, pl.ds(lane * 128, 128)]
                    image_sum[pl.ds(which * lanes + lane, 1), :] = values

        @pl.when(at == swapped)
        def _():
            token_swap().wait()
            arrivals[8].wait()

        @pl.when((at >= swapped) & (at < handed))
        def _():
            tokens = both[...].reshape(2 * both.shape[1], -1)
            for which in range(AT_ONCE):
                shift = AT_ONCE * (at - swapped) + which
                laid = jnp.dot(pick[shift], tokens, preferred_element_type=jnp.float32)
                spread[shift] = laid.astype(jnp.bfloat16)

        @pl.when(at == handed)
        def _():
            own_copy().start()

        @pl.when(at >= handed)
        def _():
            sender.trickle(at - handed, GIVE_ROWS)

    def step(at, carry):
        for hop in range(5):

            @pl.when(at == token_blocks + 1 + 4 * hop)
            def _(hop=hop):
                small_hop(hop, True)

            @pl.when(at == token_blocks + 4 + 4 * hop)
            def _(hop=hop):
                small_hop(hop, False)

        for lag, body in (
            (8, tall.end),
            (7, tall.last),
            (5, tall.third),
            (3, tall.second),
            (1, tall.loaded),
            (0, functools.partial(tall.load, begin=True)),
        ):
            for which in range(AT_ONCE):
                tile = AT_ONCE * (at - lag) + which

                @pl.when((at >= lag) & (tile < tall_tiles))
                def _(tile=tile, body=body):
                    body(tile, tile)

        for lag, slots, body in stages:
            chunk = at - lag

            @pl.when((chunk >= 0) & (chunk < chunks))
            def _(chunk=chunk, slots=slots, body=body):
                body(chunk, lax.rem(chunk, slots))

        tokens_step(at)
        return carry

    lax.fori_loop(0, chunks + LAST_LAG, step, 0)
    own_copy().wait()
    for stage in range(5):
        pl.semaphore_wait(credit.at[stage], SLOTS)
    for line in (main, tall):
        line.drain()
    sender.wait()


def turn(operand):
    blocks = operand.shape[1] // (8 * TILE_ROWS)
    return operand.T.reshape(8, blocks, TILE_ROWS, operand.shape[0])


def sum_gradients(lefts, rights, tokens_side, image_part, bias_part, scale_row, parts, group, per):
    bf16, f32 = jnp.bfloat16, jnp.float32
    projection, residual, source, pick = tokens_side
    length, width = source.shape
    image_rows, bias_rows = image_part.size // 128, bias_part.size // 128
    padded = -(-image_rows // 16) * 16
    image_part = jnp.pad(image_part.reshape(image_rows, 128), ((0, padded - image_rows), (0, 0)))
    bias_part = bias_part.reshape(bias_rows, 128)
    block = (pick.shape[1], width)
    shapes = [
        *[
            jax.ShapeDtypeStruct(
                (left.shape[1], TILE_ROWS, -(-right.shape[1] // TILE_COLUMNS) * TILE_COLUMNS), bf16
            )
            for left, right in zip(lefts, rights)
        ],
        jax.ShapeDtypeStruct((3, *block), bf16),
        jax.ShapeDtypeStruct(block, bf16),
        *[jax.ShapeDtypeStruct(part.shape, bf16) for part in parts],
        jax.ShapeDtypeStruct((4, 2, 2, padded, 128), bf16),
        jax.ShapeDtypeStruct((bias_rows, 128), f32),
    ]
    tile = (TILE_ROWS, TILE_COLUMNS)
    vmem, hbm = pl.BlockSpec(memory_space=pltpu.VMEM), pl.BlockSpec(memory_space=pl.ANY)
    flops = 2 * sum(left.size * right.shape[1] for left, right in zip(lefts, rights))
    tiles = sum(part.shape[1] // LINE_TILE for part in parts)
    most = max(LINE_SLOTS, tiles)
    results = pl.pallas_call(
        functools.partial(sum_kernel, len(lefts), group, per),
        in_specs=[hbm] * (2 * len(lefts) + 6) + [vmem] * 3,
        out_specs=[hbm] * (len(lefts) + 4) + [vmem] * 2,
        out_shape=shapes,
        scratch_shapes=[
            pltpu.VMEM((2, 8, TILE_ROWS, length), bf16),
            *[pltpu.VMEM(right.shape, bf16) for right in rights],
            pltpu.VMEM(projection.shape, bf16),
            pltpu.VMEM(residual.shape, f32),
            pltpu.VMEM(source.shape, bf16),
            pltpu.VMEM(pick.shape, bf16),
            pltpu.VMEM((2, length, width), bf16),
            pltpu.VMEM((4, *block), bf16),
            pltpu.VMEM((2, width), f32),
            pltpu.VMEM((SLOTS, 2, 2, 2, *tile), bf16),
            pltpu.VMEM((SLOTS, 2, 2, *tile), bf16),
            pltpu.VMEM((SLOTS, 2, 2, *tile), bf16),
            *[pltpu.VMEM((SLOTS, 2, max(CUTS), TILE_COLUMNS), bf16)] * 2,
            *[pltpu.VMEM((SLOTS, max(CUTS), TILE_COLUMNS), bf16)] * 2,
            *[pltpu.VMEM((LINE_SLOTS, *tile), bf16)] * 5,
            *[pltpu.VMEM((tiles, parts[0].shape[0], LINE_TILE), bf16)] * 5,
            pltpu.VMEM((padded, 128), f32),
            pltpu.VMEM((padded, 128), f32),
            pltpu.VMEM((5, bias_rows, 128), f32),
            pltpu.SemaphoreType.DMA((11,)),
            pltpu.SemaphoreType.DMA((11,)),
            pltpu.SemaphoreType.DMA((11, most)),
            pltpu.SemaphoreType.DMA((11, most)),
            pltpu.SemaphoreType.DMA((2, most)),
            pltpu.SemaphoreType.DMA((tiles,)),
            pltpu.SemaphoreType.DMA((3,)),
            pltpu.SemaphoreType.DMA((3,)),
            pltpu.SemaphoreType.DMA((10,)),
            pltpu.SemaphoreType.DMA((2,)),
            pltpu.SemaphoreType.REGULAR((11,)),
        ],
        compiler_params=pltpu.CompilerParams(
            collective_id=0, has_side_effects=True, vmem_limit_bytes=60 * 1024 * 1024
        ),
        cost_estimate=pl.CostEstimate(
            flops=flops, bytes_accessed=600000000, transcendentals=0
        ),
        name="sum_gradients",
    )(*lefts, *rights, *tokens_side, *parts, image_part, bias_part, scale_row)
    take = iter(results)
    summed = [next(take) for _ in lefts]
    summed = [
        result.reshape(-1, result.shape[2])[:, : right.shape[1]].astype(f32)
        for result, right in zip(summed, rights)
    ]
    given, own_block = next(take), next(take)
    parts = [next(take).astype(f32) for _ in parts]
    every_image, bias_total = take
    every_image = every_image[:, :, :, :image_rows].reshape(4, 4, -1).transpose(1, 0, 2)
    return summed, every_image.reshape(16, -1), bias_total.reshape(-1), [own_block, *given], parts


def local(
    n_img,
    n_row,
    tokens,
    cotangent,
    targets,
    time_table,
    ada_weight,
    ada_bias,
    qkv_weight,
    out_weight,
    up_weight,
    up_bias,
    down_weight,
    proj_first,
    proj_second,
    proj_third,
    time_bins,
    image_order,
    counts,
):
    f32, bf16 = jnp.float32, jnp.bfloat16
    per, slot_len, width = tokens.shape
    column = 2 * per
    group = n_row // column
    length = TOTAL // (2 * group)
    n_images = time_bins.shape[0]
    img_rank, row_rank = lax.axis_index("img"), lax.axis_index("row")
    core = img_rank % 2
    place = row_rank // group
    receives = place // per == core

    def swap(operand, axis, bit):
        size = n_img if axis == "img" else n_row
        return lax.ppermute(operand, axis, [(at, at ^ bit) for at in range(size)])

    def route(shift, back):
        pairs = [
            (img * n_row + (row + shift) % n_row, img * n_row + row)
            for img in range(n_img)
            for row in range(n_row)
            if (row // group) // per == img % 2
        ]
        return [(b, a) for a, b in pairs] if back else pairs

    own_counts = lax.dynamic_index_in_dim(counts, place % per, 0, keepdims=False)
    position = jnp.arange(slot_len)
    kept = (row_rank % group) * 2 * length + jnp.arange(2 * length)
    def make_pick(own_counts):
        first_of = (jnp.cumsum(own_counts) - own_counts) * RW
        picks = []
        for shift in range(n_row):
            source_row = (row_rank + shift) % n_row
            begin = lax.dynamic_index_in_dim(first_of, source_row, 0, keepdims=False)
            limit = lax.dynamic_index_in_dim(own_counts, source_row, 0, keepdims=False) * RW
            hit = (kept[None, :] == begin + position[:, None]) & (position[:, None] < limit)
            picks.append(hit)
        return jnp.concatenate(picks, axis=0).astype(bf16)

    def image_of(shift):
        return (((row_rank - shift) % n_row) // group) % per

    def bring(operand):
        pieces = []
        for shift in range(n_row):
            piece = lax.dynamic_index_in_dim(operand, image_of(shift), 0, keepdims=False)
            if shift:
                piece = lax.ppermute(piece, ("img", "row"), route(shift, False))
            pieces.append(piece)
        packed = weight_grad(pick, jnp.concatenate(pieces, axis=0)).astype(bf16)
        own = lax.dynamic_slice_in_dim(packed, core * length, length, 0)
        other = lax.dynamic_slice_in_dim(packed, (1 - core) * length, length, 0)
        return jnp.where(receives, own, swap(other, "img", 1))

    def give_start(operand, other):
        both = jnp.where(
            core == 0,
            jnp.concatenate([operand, other], axis=0),
            jnp.concatenate([other, operand], axis=0),
        )
        return matmul(pick, both).astype(bf16).reshape(n_row, slot_len, -1)

    def give_send(spread):
        sent = [
            lax.ppermute(spread[shift], ("img", "row"), route(shift, True))
            for shift in range(1, n_row)
        ]
        return [spread[0], *sent]

    def give_merge(blocks):
        images = [jnp.zeros_like(blocks[0]) for _ in range(per)]
        for shift, block in enumerate(blocks):
            sender = ((row_rank - shift) % n_row) // group
            for at in range(per):
                wanted = (sender // per == core) & (sender % per == at)
                if group > 1:
                    images[at] = images[at] + jnp.where(wanted, block, jnp.zeros_like(block))
                else:
                    images[at] = jnp.where(wanted, block, images[at])
        return jnp.stack(images)

    def fetch(operand):
        return lax.all_gather(operand, "img", axis=0, tiled=True)

    chip_bits = [1 << at for at in range(1, n_img.bit_length() - 1)]
    forth, back = chip_bits, chip_bits[-1:] + chip_bits[:-1]

    def side(bit):
        return (img_rank // bit) % 2

    def together(operand, bit, axis):
        blocks = jnp.stack([operand, swap(operand, "img", bit)], axis=axis)
        return jnp.where(side(bit) == 0, blocks, jnp.flip(blocks, axis=axis))

    def scattered(grad):
        return lax.psum_scatter(grad, "img", scatter_dimension=0, tiled=True)

    def offload_shards(left, right):
        return scattered(weight_grad(left, right).astype(bf16))

    def row_sum(part, turn_by):
        ranks = [(at + turn_by) % n_row for at in range(n_row)]
        return lax.psum(part, "row", axis_index_groups=[ranks]).astype(f32)

    fold = n_row // 4
    line_rank = row_rank // fold

    def over_row(part):
        def hop(operand, pairs):
            routes = [(a * fold + low, b * fold + low) for a, b in pairs for low in range(fold)]
            return lax.ppermute(operand, "row", routes)

        for at in range(fold.bit_length() - 1):
            part = (part.astype(f32) + swap(part, "row", 1 << at).astype(f32)).astype(bf16)
        part = (part.astype(f32) + hop(part, [(0, 1), (3, 2)]).astype(f32)).astype(bf16)
        part = (part.astype(f32) + hop(part, [(1, 2), (2, 1)]).astype(f32)).astype(bf16)
        outer = hop(part, [(1, 0), (2, 3)])
        return jnp.where((line_rank == 0) | (line_rank == 3), outer, part).astype(f32)

    order = image_order
    for bit in [1] + chip_bits:
        order = together(order, bit, 0).reshape(-1)
    chosen = jnp.sum(
        jnp.where(order[:, None] == jnp.arange(n_images)[None, :], time_bins[None, :], 0), axis=1
    )
    select = (chosen[:, None] == jnp.arange(time_table.shape[0])[None, :]).astype(f32)
    condition = jnp.dot(select, time_table.astype(f32), precision=lax.Precision.HIGHEST)
    silu_cond = jax.nn.silu(condition).astype(bf16)
    row_cond = lax.dynamic_index_in_dim(
        silu_cond.reshape(n_img // 2, column, -1), place, 1, keepdims=False
    )
    mod_width = ada_weight.shape[1]
    ff_width = up_weight.shape[1]
    bias_part = lax.dynamic_update_slice(
        jnp.zeros((mod_width,), f32), ada_bias.astype(f32), (img_rank * ada_bias.shape[0],)
    )
    up_bias_part = lax.dynamic_update_slice(
        jnp.zeros((ff_width,), f32), up_bias.astype(f32), (img_rank * up_bias.shape[0],)
    )
    mod_part = matmul(row_cond, ada_weight) + bias_part[None, :]
    small_plane = n_img == 8 and n_row == 4
    pick = None if small_plane else make_pick(own_counts)
    early = [qkv_weight, out_weight, proj_first]
    summed_rows = jnp.concatenate([mod_part.reshape(-1), up_bias_part])
    if small_plane:
        early, arrived, summed_rows = gather_weights(
            early, [tokens, cotangent, targets], summed_rows, group, per
        )
    else:
        early = [fetch(one) for one in early]
        for bit in [1] + chip_bits:
            summed_rows = summed_rows + swap(summed_rows, "img", bit)
    qkv_full, out_full, first_full = early
    modulation = lax.dynamic_index_in_dim(
        summed_rows[: (n_img // 2) * mod_width].reshape(n_img // 2, mod_width),
        img_rank // 2,
        0,
        keepdims=True,
    )
    up_bias_full = summed_rows[(n_img // 2) * mod_width :]
    up_full = fetch(up_weight)
    down_full = fetch(down_weight)
    second_full = fetch(proj_second)
    third_full = fetch(proj_third)

    shift_att, scale_att, gate_att, shift_mlp, scale_mlp, gate_mlp = jnp.split(
        modulation, 6, axis=1
    )
    if small_plane:
        image_counts = lax.dynamic_index_in_dim(together(counts, 1, 0).reshape(column, n_row), place, 0)
        ends = jnp.cumsum(image_counts[0])
        units = core * (length // RW) + jnp.arange(length // RW)
        origin = jnp.sum((units[:, None] >= ends[None, :]).astype(jnp.int32), axis=1)
        before = jnp.sum(
            jnp.where(origin[:, None] == jnp.arange(n_row), ends - image_counts[0], 0), axis=1
        )
        places = origin * slot_len + (units - before) * RW
        source, own_cotangent, own_targets, h_att = compact(
            places.astype(jnp.int32), arrived, shift_att, scale_att
        )
        source_rows, source = source, source.astype(f32)
        own_cotangent, own_targets = own_cotangent.astype(f32), own_targets.astype(f32)
    else:
        source = bring(tokens).astype(f32)
        own_cotangent, own_targets = bring(cotangent).astype(f32), bring(targets).astype(f32)
        h_att = modulate(source, shift_att, scale_att).astype(bf16)
    qkv_rows = matmul(h_att, qkv_full).astype(bf16)
    bits = [1 << at for at in range(group.bit_length() - 1)]
    if small_plane:
        head_mix, log_total, rest = attend(qkv_rows, None, width)
    else:
        rest = swap(qkv_rows[:, width:], "img", 1)
        for bit in bits:
            near = jnp.concatenate([qkv_rows[:, width:], rest], axis=0)
            rest = jnp.concatenate([rest, swap(near, "row", bit)], axis=0)
        head_mix, log_total = attend(qkv_rows, rest, width)
    attn_out = matmul(head_mix, out_full)
    residual = source + gate_att * attn_out
    h_mlp = modulate(residual, shift_mlp, scale_mlp).astype(bf16)
    pre_act = matmul(h_mlp, up_full) + up_bias_full
    gelu_out = gelu_tanh(pre_act).astype(bf16)
    mlp_out = matmul(gelu_out, down_full)
    lefts = [gelu_out, h_mlp, head_mix, h_att]
    if small_plane:
        lefts = [turn(left) for left in lefts]
        lefts, mlp_out = lax.optimization_barrier((lefts, mlp_out))
    block_own = (residual + gate_mlp * mlp_out).astype(bf16)
    lin_one = matmul(block_own, first_full)
    hid_one = jax.nn.silu(lin_one).astype(bf16)
    left_first = turn(block_own) if small_plane else block_own
    if small_plane:
        own_counts, block_own = lax.optimization_barrier((own_counts, block_own))
        pick = make_pick(own_counts)
    block_spread = give_start(block_own, swap(block_own, "img", 1))
    tied = lax.optimization_barrier((block_spread, left_first, hid_one))
    block_spread, left_first, hid_one = tied
    lin_two = matmul(hid_one, second_full)
    hid_two = jax.nn.silu(lin_two).astype(bf16)
    projected = matmul(hid_two, third_full)

    def align_loss(operand):
        return -0.5 * jnp.sum(alignment(operand, own_targets))

    d_proj = jax.vjp(align_loss, projected)[1](jnp.ones((), f32))[0].astype(bf16)
    third_sum = weight_grad(hid_two, d_proj).astype(bf16)
    third_sum, d_proj = lax.optimization_barrier((third_sum, d_proj))
    third_part = scattered(third_sum)
    d_lin_two = silu_back(lin_two, transposed(d_proj, third_full)).astype(bf16)
    second_sum = weight_grad(hid_one, d_lin_two).astype(bf16)
    second_sum, d_lin_two = lax.optimization_barrier((second_sum, d_lin_two))
    second_part = scattered(second_sum)
    d_lin_one = silu_back(lin_one, transposed(d_lin_two, second_full)).astype(bf16)
    d_res = own_cotangent + transposed(d_lin_one, first_full)
    d_gate_mlp = jnp.sum(d_res * mlp_out, axis=0)
    d_mlp = (d_res * gate_mlp).astype(bf16)
    d_pre = gelu_back(pre_act, transposed(d_mlp, down_full)).astype(bf16)
    bias_sum = jnp.sum(d_pre.astype(f32), axis=0)
    d_resid_norm, d_shift_mlp, d_scale_mlp = jax.vjp(modulate, residual, shift_mlp, scale_mlp)[1](
        transposed(d_pre, up_full)
    )
    d_residual = d_res + d_resid_norm
    d_gate_att = jnp.sum(d_residual * attn_out, axis=0)
    d_attn = (d_residual * gate_att).astype(bf16)
    d_mixed = transposed(d_attn, out_full).astype(bf16)
    third_part, d_mixed = lax.optimization_barrier((third_part, d_mixed))
    d_qkv, d_other = attend_back(
        qkv_rows,
        rest,
        head_mix,
        d_mixed,
        log_total,
        block_spread,
        (group, per) if small_plane else None,
    )
    if small_plane:
        block_out = give_merge([block_spread[0], *d_other])
    else:
        block_out = give_merge(give_send(block_spread))
        d_own, d_rest = d_qkv[:, width:].astype(f32), d_other
        for bit in reversed(bits):
            full = jnp.concatenate([d_own, d_rest.astype(f32)], axis=0)
            half = full.shape[0] // 2
            full = full[:half] + swap(full[half:].astype(bf16), "row", bit).astype(f32)
            d_own, d_rest = full[:length], full[length:].astype(bf16)
        d_own = d_own + swap(d_rest, "img", 1).astype(f32)
        d_qkv = jnp.concatenate([d_qkv[:, :width], d_own.astype(bf16)], axis=1)
    second_part, d_qkv = lax.optimization_barrier((second_part, d_qkv))
    late_mod = jnp.concatenate([d_gate_att, d_shift_mlp[0], d_scale_mlp[0], d_gate_mlp])
    lefts.append(left_first)
    rights = [d_mlp, d_pre, d_attn, d_qkv, d_lin_one]
    proj_parts = [second_part, third_part]
    if small_plane:
        tied = (proj_parts, rights, d_residual, late_mod, bias_sum)
        proj_parts, rights, d_residual, late_mod, bias_sum = lax.optimization_barrier(tied)
        large, d_mod, bias_sum, blocks, proj_grads = sum_gradients(
            lefts,
            rights,
            (qkv_full, d_residual, source_rows, pick.reshape(n_row, slot_len, -1)),
            jnp.concatenate([jnp.zeros((2 * width,), f32), late_mod]),
            bias_sum,
            scale_att,
            proj_parts,
            group,
            per,
        )
        grad_tokens = give_merge(blocks)
    else:
        d_source, d_shift_att, d_scale_att = jax.vjp(modulate, source, shift_att, scale_att)[1](
            transposed(d_qkv, qkv_full)
        )
        tokens_own = (d_residual + d_source).astype(bf16)
        grad_tokens = give_merge(give_send(give_start(tokens_own, swap(tokens_own, "img", 1))))
        proj_grads = [row_sum(part, at) for at, part in enumerate(proj_parts)]
        large = [over_row(offload_shards(*pair)) for pair in zip(lefts, rights)]
        own_mod = jnp.concatenate([d_shift_att[0], d_scale_att[0], late_mod])
        slot_id = column * (img_rank // 2) + place
        placed = jnp.zeros((n_images, mod_width), f32)
        placed = lax.dynamic_update_slice(placed, own_mod[None, :], (slot_id, 0))
        d_mod, bias_sum = lax.psum((placed, bias_sum), ("img", "row"))
        d_mod = d_mod.astype(bf16)
    grad_second, grad_third = proj_grads
    grad_down, grad_up, grad_out, grad_qkv, grad_first = large

    grad_ada = weight_grad(silu_cond, d_mod)
    grad_ada_bias = jnp.sum(
        lax.dynamic_slice_in_dim(d_mod, img_rank * ada_bias.shape[0], ada_bias.shape[0], 1).astype(
            f32
        ),
        axis=0,
    )
    d_cond = silu_back(condition, transposed(d_mod, ada_weight))
    grad_table = jnp.dot(select.T, d_cond, precision=lax.Precision.HIGHEST)
    grad_up_bias = lax.dynamic_index_in_dim(
        bias_sum.reshape(n_img, -1), img_rank, 0, keepdims=False
    )
    return (
        block_out,
        grad_tokens,
        grad_table,
        grad_ada,
        grad_ada_bias,
        grad_qkv,
        grad_out,
        grad_up,
        grad_up_bias,
        grad_down,
        grad_first,
        grad_second,
        grad_third,
    )


def solution(mesh):
    return jax.shard_map(
        functools.partial(local, mesh.shape["img"], mesh.shape["row"]),
        mesh=mesh,
        in_specs=(
            P("img", "row", None),
            P("img", "row", None),
            P("img", "row", None),
            P(None, "img"),
            P("img", None),
            P("img"),
            P("img", None),
            P("img", None),
            P("img", None),
            P("img"),
            P("img", None),
            P("img", None),
            P("img", None),
            P("img", None),
            P(),
            P("img"),
            P("img", None),
        ),
        out_specs=(
            P("img", "row", None),
            P("img", "row", None),
            P(None, "img"),
            P("img", None),
            P("img"),
            P("img", None),
            P("img", None),
            P("img", None),
            P("img"),
            P("img", None),
            P("img", None),
            P("img", None),
            P("img", None),
        ),
        check_vma=False,
    )
```

```python
import functools

import jax
import jax.numpy as jnp
from jax import lax
from jax.experimental import pallas as pl
from jax.experimental.pallas import tpu as pltpu
from jax.sharding import PartitionSpec as P

HEADS = 16
HDIM = 72
RW = 32
LROWS = 32
TOTAL = LROWS * RW
SCALE = HDIM ** (-0.5)
LOG2E = 1.4426950408889634
LAST = (((1,), (1,)), ((), ()))
FIRST = (((0,), (0,)), ((), ()))


def normalize(operand):
    centre = operand - jnp.mean(operand, axis=-1, keepdims=True)
    return centre * lax.rsqrt(jnp.mean(centre * centre, axis=-1, keepdims=True) + 1e-06)


def modulate(operand, shift_row, scale_row):
    return normalize(operand) * (1.0 + scale_row) + shift_row


def alignment(projected, targets):
    unit_proj = projected * lax.rsqrt(
        jnp.mean(projected * projected, axis=-1, keepdims=True) + 1e-06
    )
    unit_target = targets * lax.rsqrt(jnp.mean(targets * targets, axis=-1, keepdims=True) + 1e-06)
    return jnp.mean(unit_proj * unit_target, axis=-1)


def matmul(left_side, right_side):
    return jnp.dot(left_side, right_side, preferred_element_type=jnp.float32)


def transposed(left_side, right_side):
    return lax.dot_general(left_side, right_side, LAST, preferred_element_type=jnp.float32)


def weight_grad(left_side, right_side):
    return lax.dot_general(left_side, right_side, FIRST, preferred_element_type=jnp.float32)


def silu_back(operand, gradient):
    return jax.vjp(jax.nn.silu, operand)[1](gradient)[0]


def gelu_tanh(operand):
    return jax.nn.gelu(operand, approximate=True)


def gelu_back(operand, gradient):
    return jax.vjp(gelu_tanh, operand)[1](gradient)[0]


MESH = pl.DeviceIdType.MESH
def mates():
    me = lax.axis_index("img")
    core, x, y = lax.rem(me, 2), lax.rem(me // 2, 2), me // 4
    return me, (core, x, y), (me + 1 - 2 * core, me + 2 - 4 * x, me + 4 - 8 * y)


def greet(where):
    barrier = pltpu.get_barrier_semaphore()
    pl.semaphore_signal(barrier, inc=1, device_id=where, device_id_type=MESH)


def gather_copies(block, whole, send_sem, recv_sem):
    me, (_, _, y), (sibling, x_mate, y_mate) = mates()
    far = x_mate + 4 - 8 * y
    rows = block.shape[0]
    cut = (rows // 2 + 15) // 16 * 16
    upper, lower = pl.ds(0, cut), pl.ds(cut, rows - cut)

    def copy(kind, source, owner, rows, where):
        return pltpu.make_async_remote_copy(
            src_ref=source,
            dst_ref=whole.at[owner, rows, :],
            send_sem=send_sem.at[kind],
            recv_sem=recv_sem.at[kind],
            device_id={"img": where},
            device_id_type=MESH,
        )

    found = [
        copy(0, block.at[upper, :], me, upper, x_mate),
        copy(1, block.at[lower, :], me, lower, y_mate),
        copy(2, block.at[upper, :], me, upper, y_mate),
        copy(3, block.at[lower, :], me, lower, x_mate),
        copy(4, whole.at[x_mate, upper, :], x_mate, upper, y_mate),
        copy(5, whole.at[y_mate, lower, :], y_mate, lower, x_mate),
        copy(6, block.at[upper, :], me, upper, sibling),
        copy(7, block.at[lower, :], me, lower, sibling),
    ]
    come = [(x_mate, upper), (y_mate, lower), (y_mate, upper), (x_mate, lower)]
    come += [(far, upper), (far, lower)]
    for kind, (owner, rows) in enumerate(come):
        found.append(copy(8 + kind, whole.at[owner, rows, :], owner, rows, sibling))
    return found


def first_round(found):
    for kind in (0, 1, 6, 7):
        found[kind].start()


def second_round(found):
    found[0].wait_recv()
    for kind in (4, 2, 8):
        found[kind].start()
    found[1].wait_recv()
    for kind in (5, 3, 9):
        found[kind].start()


def third_round(found):
    for kind in (4, 5, 2, 3):
        found[kind].wait_recv()
        found[8 + kind].start()


def last_round(found):
    for kind, one in enumerate(found):
        if kind >= 6:
            one.wait_recv()
        one.wait_send()


HALF = HEADS // 2


def head_window(head, width, window):
    first = jnp.minimum(head * HDIM // 128, (width - window) // 128) * 128
    lane = lax.broadcasted_iota(jnp.int32, (1, window), 1) + first - head * HDIM
    return first, (lane >= 0) & (lane < HDIM)


def each_head(body):
    def narrow(at, carry):
        body(2 * at + at // (HALF // 2), 128)
        return carry

    def wide(at, carry):
        body(2 * at + 1 - at // (HALF // 2), 256)
        return carry

    lax.fori_loop(0, HALF, narrow, 0)
    lax.fori_loop(0, HALF, wide, 0)


def columns_at(first, part, width, window):
    return pl.ds(pl.multiple_of(first + part * width, 128), window)


def attend_kernel(remote, own_ref, *refs):
    mix_ref, lse_ref, rest_ref = refs[:3] if remote else (refs[1], refs[2], refs[0])
    length, width = mix_ref.shape
    block = min(256, length)
    if remote:
        me = lax.axis_index("img")
        sibling = {"img": me + 1 - 2 * lax.rem(me, 2)}
        greet(sibling)
        pl.semaphore_wait(pltpu.get_barrier_semaphore(), 1)
        swap = pltpu.make_async_remote_copy(
            src_ref=own_ref.at[:, pl.ds(width, 2 * width)],
            dst_ref=rest_ref,
            send_sem=refs[3],
            recv_sem=refs[4],
            device_id=sibling,
            device_id_type=MESH,
        )
        swap.start()

    def one_head(head, window):
        first, mine = head_window(head, width, window)
        mix_columns = columns_at(first, 0, width, window)
        key_refs = [own_ref.at[:, columns_at(first, 1, width, window)]]
        key_refs.append(rest_ref.at[:, columns_at(first, 0, width, window)])
        value_refs = [own_ref.at[:, columns_at(first, 2, width, window)]]
        value_refs.append(rest_ref.at[:, columns_at(first, 1, width, window)])
        keys, values = [ref[...] for ref in key_refs], [ref[...] for ref in value_refs]
        for at in range(0, length, block):
            rows = pl.ds(at, block)
            queries = jnp.where(mine, own_ref[rows, mix_columns], jnp.bfloat16(0))
            scores = [
                lax.dot_general(queries, part, LAST, preferred_element_type=jnp.float32)
                for part in keys
            ]
            tops = [jnp.max(part, axis=1, keepdims=True) for part in scores]
            top = jnp.maximum(tops[0], tops[1])
            top = top * (SCALE * LOG2E)
            weights = [jnp.exp2(part * (SCALE * LOG2E) - top) for part in scores]
            total = sum(jnp.sum(part, axis=1, keepdims=True) for part in weights)
            mixed = sum(
                jnp.dot(part.astype(jnp.bfloat16), value, preferred_element_type=jnp.float32)
                for part, value in zip(weights, values)
            )
            mixed = (mixed / total).astype(mix_ref.dtype)
            mix_ref[rows, mix_columns] = jnp.where(mine, mixed, mix_ref[rows, mix_columns])
            log_total = jnp.broadcast_to(top + jnp.log(total) * LOG2E, (block, 128))
            lse_ref[head, :, rows] = log_total.T[:1, :]

    mix_ref[...] = jnp.zeros_like(mix_ref)
    if remote:
        swap.wait()
    each_head(one_head)


def attend(own, rest, width):
    length, bf16 = own.shape[0], jnp.bfloat16
    vmem = pl.BlockSpec(memory_space=pltpu.VMEM)
    shapes = [
        jax.ShapeDtypeStruct((length, width), bf16),
        jax.ShapeDtypeStruct((HEADS, 1, length), jnp.float32),
    ]
    remote, operands, scratch, params = rest is None, [own], [], {}
    span = 2 * length
    if remote:
        shapes.append(jax.ShapeDtypeStruct((length, 2 * width), bf16))
        scratch = [pltpu.SemaphoreType.DMA] * 2
        params = dict(collective_id=3, has_side_effects=True)
    else:
        operands.append(rest)
        span = length + rest.shape[0]
    return pl.pallas_call(
        functools.partial(attend_kernel, remote),
        in_specs=[vmem] * len(operands),
        out_specs=[vmem] * len(shapes),
        out_shape=shapes,
        scratch_shapes=scratch,
        compiler_params=pltpu.CompilerParams(vmem_limit_bytes=28 * 1024 * 1024, **params),
        cost_estimate=pl.CostEstimate(
            flops=4 * HEADS * length * span * 256,
            bytes_accessed=4 * (length + span) * width * 2,
            transcendentals=HEADS * length * span,
        ),
        name="attend",
    )(*operands)


class Give:
    def __init__(self, group, per, spread, given, send_sem, recv_sem):
        self.group, self.per = group, per
        self.spread, self.given, self.send_sem, self.recv_sem = spread, given, send_sem, recv_sem
        self.row = lax.axis_index("row")
        self.slots = given.shape[1]

    def greet(self):
        for shift in range(1, 4):
            greet({"row": lax.rem(self.row + shift, 4)})

    def copy(self, shift, rows):
        return pltpu.make_async_remote_copy(
            src_ref=self.spread.at[shift, rows, :],
            dst_ref=self.given.at[shift - 1, rows, :],
            send_sem=self.send_sem.at[shift - 1],
            recv_sem=self.recv_sem.at[shift - 1],
            device_id={"row": lax.rem(self.row + shift, 4)},
            device_id_type=MESH,
        )

    def from_here(self, row):
        return (row // self.group) // self.per == lax.rem(lax.axis_index("img"), 2)

    def start(self, at, amount):
        @pl.when((at < self.slots // amount) & self.from_here(self.row))
        def _():
            for shift in range(1, 4):
                rows = pl.ds(pl.multiple_of(at * amount, amount), amount)
                self.copy(shift, rows).start()

    def trickle(self, at, amount):
        block = at // 2

        @pl.when((block < self.slots // amount) & self.from_here(self.row))
        def _():
            rows = pl.ds(pl.multiple_of(block * amount, amount), amount)

            @pl.when(lax.rem(at, 2) == 0)
            def _():
                self.copy(1, rows).start()
                self.copy(3, rows).start()

            @pl.when(lax.rem(at, 2) == 1)
            def _():
                self.copy(2, rows).start()

    def wait(self):
        for shift in range(1, 4):
            whole = self.copy(shift, pl.ds(0, self.slots))

            @pl.when(self.from_here(self.row))
            def _(whole=whole):
                whole.wait_send()

            @pl.when(self.from_here(lax.rem(self.row + 4 - shift, 4)))
            def _(whole=whole):
                whole.wait_recv()


def attend_back_kernel(give, own_in, rest_in, mix_in, d_ref, lse_ref, spread, *refs):
    *refs, own_ref, rest_ref, mix_ref, load_sem = refs
    length, width = mix_ref.shape
    loads = [
        pltpu.make_async_copy(source, target, load_sem.at[at])
        for at, (source, target) in enumerate(
            [(own_in, own_ref), (rest_in, rest_ref), (mix_in, mix_ref)]
        )
    ]
    for one in loads:
        one.start()
    block = 256
    if give:
        d_own, given, d_rest, arrived, core_send, core_recv, *sems = refs
        me = lax.axis_index("img")
        sibling = {"img": me + 1 - 2 * lax.rem(me, 2)}
        sender = Give(*give, spread, given, *sems)
        sender.greet()
        greet(sibling)
        pl.semaphore_wait(pltpu.get_barrier_semaphore(), 4)
        sender.start(0, given.shape[1])
    else:
        d_own, d_rest = refs
    for ref in (d_own, d_rest):
        ref[...] = jnp.zeros_like(ref)
    for one in loads:
        one.wait()

    def one_head(head, window):
        first, mine = head_window(head, width, window)
        here = columns_at(first, 0, width, window)
        queries = jnp.where(mine, own_ref[:, here], jnp.bfloat16(0))
        d_mix = jnp.where(mine, d_ref[:, here], jnp.bfloat16(0))
        product = d_mix.astype(jnp.float32) * mix_ref[:, here].astype(jnp.float32)
        delta = lax.dot_general(
            jnp.ones((8, window), jnp.float32),
            product,
            LAST,
            precision=lax.Precision.HIGHEST,
            preferred_element_type=jnp.float32,
        )[:1, :]
        log_total = lse_ref[head]
        d_query = jnp.zeros((length, window), jnp.float32)
        runs = [(own_ref, 1, d_own, at) for at in range(0, length, block)]
        runs += [(rest_ref, 0, d_rest, at) for at in range(0, rest_ref.shape[0], block)]
        for source, part, target, at in runs:
            rows = pl.ds(at, block)
            key_columns = columns_at(first, part, width, window)
            value_columns = columns_at(first, part + 1, width, window)
            keys, values = source[rows, key_columns], source[rows, value_columns]
            scores = lax.dot_general(keys, queries, LAST, preferred_element_type=jnp.float32)
            prob = jnp.exp2(scores * (SCALE * LOG2E) - log_total)
            d_prob = lax.dot_general(values, d_mix, LAST, preferred_element_type=jnp.float32)
            d_score = (prob * (d_prob - delta)).astype(jnp.bfloat16)
            d_key = jnp.dot(d_score, queries, preferred_element_type=jnp.float32) * SCALE
            d_value = jnp.dot(
                prob.astype(jnp.bfloat16), d_mix, preferred_element_type=jnp.float32
            )
            target[rows, key_columns] += d_key.astype(target.dtype)
            target[rows, value_columns] += d_value.astype(target.dtype)
            d_query += lax.dot_general(d_score, keys, FIRST, preferred_element_type=jnp.float32)
        d_query = jnp.where(mine, d_query * SCALE, 0.0)
        d_own[:, here] += d_query.astype(d_own.dtype)

    each_head(one_head)
    if give:
        swap = pltpu.make_async_remote_copy(
            src_ref=d_rest,
            dst_ref=arrived,
            send_sem=core_send,
            recv_sem=core_recv,
            device_id=sibling,
            device_id_type=MESH,
        )
        swap.start()
        swap.wait()
        d_own[:, pl.ds(width, 2 * width)] += arrived[...]
        sender.wait()


def attend_back(own, rest, mixed, d_mix, log_total, spread, give):
    length, width = mixed.shape
    span = length + rest.shape[0]
    vmem, bf16 = pl.BlockSpec(memory_space=pltpu.VMEM), jnp.bfloat16
    hbm = pl.BlockSpec(memory_space=pl.ANY)
    shapes = [jax.ShapeDtypeStruct(own.shape, bf16)]
    specs, scratch, remote = [vmem, vmem], [], {}
    if give:
        shapes.append(jax.ShapeDtypeStruct((spread.shape[0] - 1, *spread.shape[1:]), bf16))
        specs = [vmem, hbm]
        scratch = [pltpu.VMEM(rest.shape, bf16)] * 2
        scratch += [pltpu.SemaphoreType.DMA] * 2 + [pltpu.SemaphoreType.DMA((3,))] * 2
        remote = dict(collective_id=2, has_side_effects=True)
    else:
        shapes.append(jax.ShapeDtypeStruct(rest.shape, bf16))
    return pl.pallas_call(
        functools.partial(attend_back_kernel, give),
        in_specs=[hbm] * 3 + [vmem] * 2 + [hbm],
        out_specs=specs,
        out_shape=shapes,
        scratch_shapes=[
            *scratch,
            *[pltpu.VMEM(one.shape, bf16) for one in (own, rest, mixed)],
            pltpu.SemaphoreType.DMA((3,)),
        ],
        compiler_params=pltpu.CompilerParams(vmem_limit_bytes=60 * 1024 * 1024, **remote),
        cost_estimate=pl.CostEstimate(
            flops=10 * HEADS * length * span * 256,
            bytes_accessed=8 * (length + span) * width * 2,
            transcendentals=HEADS * length * span,
        ),
        name="attend_back",
    )(own, rest, mixed, d_mix, log_total, spread)


TILE_ROWS = 144
TILE_COLUMNS = 384
CUTS = (80, 64)
SLOTS = 4
LINE_SLOTS = 10
LAST_LAG = 15
LINE_TILE = 256
AT_ONCE = 2
GIVE_ROWS = 16
TOKEN_ROWS = 128


def add(one, other):
    return one + other


def gather_kernel(count, group, per, *refs):
    take = iter(refs)
    blocks = [next(take) for _ in range(count)]
    slots = [next(take) for _ in range(3)]
    part = next(take)
    wholes = [next(take) for _ in range(count)]
    arrivals = [next(take) for _ in range(3)]
    total = next(take)
    part_in, part_sum, send_sem, recv_sem, local_sem, slot_send, slot_recv, slot_local = [
        next(take) for _ in range(8)
    ]
    part_send, part_recv, *staged = take
    row = lax.axis_index("row")
    me, (core, x, y), (sibling, x_mate, y_mate) = mates()
    for mate in (sibling, x_mate, y_mate):
        greet({"img": mate})
    for shift in range(1, 4):
        greet({"row": lax.rem(row + shift, 4)})
    pl.semaphore_wait(pltpu.get_barrier_semaphore(), 6)

    def place_of(place):
        return (place // group) // per, lax.rem(place // group, per)

    takes_in = place_of(row)[0] == core

    def by_row(which, shift):
        where = lax.rem(row + 4 - shift, 4)
        return pltpu.make_async_remote_copy(
            src_ref=slots[which].at[place_of(where)[1]],
            dst_ref=arrivals[which].at[row],
            send_sem=slot_send.at[which, shift - 1],
            recv_sem=slot_recv.at[which, shift - 1],
            device_id={"row": where},
            device_id_type=MESH,
        )

    def own_slots(which, leaving):
        source = slots[which].at[place_of(row)[1]]
        stage = staged[count + which]
        if leaving:
            return pltpu.make_async_copy(stage, arrivals[which].at[row], slot_local.at[which])
        return pltpu.make_async_copy(source, stage, slot_local.at[which])

    def by_core(which, shift):
        origin = lax.rem(row + shift, 4)
        source = arrivals[which].at[origin] if shift else slots[which].at[place_of(row)[1]]
        return pltpu.make_async_remote_copy(
            src_ref=source,
            dst_ref=arrivals[which].at[origin],
            send_sem=slot_send.at[which, 3 + shift],
            recv_sem=slot_recv.at[which, 3 + shift],
            device_id={"img": sibling},
            device_id_type=MESH,
        )

    def start_slots(which):
        for shift in range(1, 4):

            @pl.when(place_of(lax.rem(row + 4 - shift, 4))[0] == core)
            def _(shift=shift):
                by_row(which, shift).start()

        @pl.when(takes_in)
        def _():
            own_slots(which, False).start()
            by_core(which, 0).start()

    def stage_slots(which):
        @pl.when(takes_in)
        def _():
            own_slots(which, False).wait()
            own_slots(which, True).start()

    def pass_slots(which):
        for shift in range(1, 4):

            @pl.when(takes_in)
            def _(shift=shift):
                by_row(which, shift).wait_recv()
                by_core(which, shift).start()

    def end_slots(which):
        for shift in range(1, 4):

            @pl.when(place_of(lax.rem(row + 4 - shift, 4))[0] == core)
            def _(shift=shift):
                by_row(which, shift).wait_send()

        @pl.when(takes_in)
        def _():
            own_slots(which, True).wait()
            for shift in range(4):
                by_core(which, shift).wait_send()

        @pl.when(jnp.logical_not(takes_in))
        def _():
            for shift in range(4):
                by_core(which, shift).wait_recv()

    part_mates = [sibling, x_mate, y_mate]

    def part_hop(hop):
        return pltpu.make_async_remote_copy(
            src_ref=part_sum.at[hop - 1] if hop else part,
            dst_ref=part_in.at[hop],
            send_sem=part_send.at[hop],
            recv_sem=part_recv.at[hop],
            device_id={"img": part_mates[hop]},
            device_id_type=MESH,
        )

    def take_part(hop):
        part_hop(hop).wait()
        summed = (part_sum[hop - 1] if hop else part[...]) + part_in[hop]
        if hop == 2:
            total[...] = summed
        else:
            part_sum[hop] = summed
            part_hop(hop + 1).start()

    every = [
        gather_copies(blocks[at], wholes[at], send_sem.at[at], recv_sem.at[at])
        for at in range(count)
    ]
    locals_ = [
        pltpu.make_async_copy(blocks[at], staged[at], local_sem.at[at]) for at in range(count)
    ]
    moved = [
        pltpu.make_async_copy(staged[at], wholes[at].at[me], local_sem.at[at])
        for at in range(count)
    ]
    part_hop(0).start()
    start_slots(0)
    for at in range(count):
        first_round(every[at])
        locals_[at].start()
    take_part(0)
    start_slots(1)
    start_slots(2)
    for found in every:
        second_round(found)
    take_part(1)
    for at in range(count):
        locals_[at].wait()
        moved[at].start()
    for which in range(3):
        stage_slots(which)
    pass_slots(0)
    for found in every:
        third_round(found)
    take_part(2)
    pass_slots(1)
    pass_slots(2)
    for at in range(count):
        last_round(every[at])
        moved[at].wait()
    for which in range(3):
        end_slots(which)


def gather_weights(blocks, slots, part, group, per):
    count = len(blocks)
    vmem, hbm = pl.BlockSpec(memory_space=pltpu.VMEM), pl.BlockSpec(memory_space=pl.ANY)
    part_rows = part.size // 128
    results = pl.pallas_call(
        functools.partial(gather_kernel, count, group, per),
        in_specs=[hbm] * (count + 3) + [vmem],
        out_specs=[hbm] * (count + 3) + [vmem],
        out_shape=[
            *[jax.ShapeDtypeStruct((8, *block.shape), block.dtype) for block in blocks],
            *[jax.ShapeDtypeStruct((4, *one.shape[1:]), one.dtype) for one in slots],
            jax.ShapeDtypeStruct((part_rows, 128), jnp.float32),
        ],
        scratch_shapes=[
            pltpu.VMEM((3, part_rows, 128), jnp.float32),
            pltpu.VMEM((2, part_rows, 128), jnp.float32),
            pltpu.SemaphoreType.DMA((count, 14)),
            pltpu.SemaphoreType.DMA((count, 14)),
            pltpu.SemaphoreType.DMA((count,)),
            pltpu.SemaphoreType.DMA((3, 7)),
            pltpu.SemaphoreType.DMA((3, 7)),
            pltpu.SemaphoreType.DMA((3,)),
            pltpu.SemaphoreType.DMA((3,)),
            pltpu.SemaphoreType.DMA((3,)),
            *[pltpu.VMEM(block.shape, block.dtype) for block in blocks],
            *[pltpu.VMEM(one.shape[1:], one.dtype) for one in slots],
        ],
        compiler_params=pltpu.CompilerParams(
            collective_id=1, has_side_effects=True, vmem_limit_bytes=60 * 1024 * 1024
        ),
        cost_estimate=pl.CostEstimate(flops=0, bytes_accessed=200000000, transcendentals=0),
        name="gather_weights",
    )(*blocks, *slots, part.reshape(part_rows, 128))
    wholes = [whole.reshape(-1, whole.shape[-1]) for whole in results[:count]]
    return wholes, results[count : count + 3], results[-1].reshape(-1)


def compact_kernel(places, *refs):
    sources, (shift, scale), targets, (h_att, sems) = refs[:3], refs[3:5], refs[5:8], refs[8:]
    amount = targets[0].shape[0] // RW

    def one(at, carry):
        begin = pl.multiple_of(places[at], RW)
        rows = pl.ds(pl.multiple_of(at * RW, RW), RW)
        for which in range(3):
            source = sources[which].at[pl.ds(begin, RW), :]
            pltpu.make_async_copy(source, targets[which].at[rows, :], sems.at[which]).start()
        return carry

    lax.fori_loop(0, amount, one, 0)

    def wait(which):
        rows = pl.ds(0, targets[which].shape[0])
        source = sources[which].at[rows, :]
        pltpu.make_async_copy(source, targets[which], sems.at[which]).wait()

    wait(0)

    def norm(at, carry):
        rows = pl.ds(pl.multiple_of(at * 64, 64), 64)
        block = targets[0][rows, :].astype(jnp.float32)
        block = modulate(block, shift[...], scale[...])
        h_att[rows, :] = block.astype(jnp.bfloat16)
        return carry

    lax.fori_loop(0, targets[0].shape[0] // 64, norm, 0)
    wait(1)
    wait(2)


def compact(places, slots, shift, scale):
    length = places.shape[0] * RW
    flat = [one.reshape(-1, one.shape[-1]) for one in slots]
    vmem, hbm = pl.BlockSpec(memory_space=pltpu.VMEM), pl.BlockSpec(memory_space=pl.ANY)
    shapes = [jax.ShapeDtypeStruct((length, one.shape[1]), one.dtype) for one in flat]
    return pl.pallas_call(
        compact_kernel,
        in_specs=[pl.BlockSpec(memory_space=pltpu.SMEM), *[hbm] * 3, vmem, vmem],
        out_specs=[vmem] * 4,
        out_shape=[*shapes, shapes[0]],
        scratch_shapes=[pltpu.SemaphoreType.DMA((3,))],
        compiler_params=pltpu.CompilerParams(vmem_limit_bytes=60 * 1024 * 1024),
        cost_estimate=pl.CostEstimate(flops=0, bytes_accessed=8000000, transcendentals=0),
        name="compact",
    )(places, *flat, shift, scale)


class Line:
    def __init__(self, first_stage, slots, buffers, sems):
        self.first_stage, self.slots = first_stage, slots
        self.shard, self.line_one, self.line_two, self.whole, self.line_three = buffers
        self.send_sem, self.recv_sem, self.store_sem, self.credit = sems
        row = lax.axis_index("row")
        self.is_end = (row == 0) | (row == 3)
        self.is_middle = (row == 1) | (row == 2)
        self.inner = {"row": jnp.where(row == 0, 1, 2)}
        self.outer = {"row": jnp.where(row == 1, 0, 3)}
        self.across = {"row": jnp.where(row == 1, 2, 1)}

    def remote(self, stage, slot, source, target, where):
        return pltpu.make_async_remote_copy(
            src_ref=source,
            dst_ref=target,
            send_sem=self.send_sem.at[self.first_stage + stage, slot],
            recv_sem=self.recv_sem.at[self.first_stage + stage, slot],
            device_id=where,
            device_id_type=MESH,
        )

    def inward(self, slot):
        return self.remote(0, slot, self.shard.at[slot], self.line_one.at[slot], self.inner)

    def crosswise(self, slot):
        return self.remote(1, slot, self.shard.at[slot], self.line_two.at[slot], self.across)

    def outward(self, slot):
        return self.remote(2, slot, self.whole.at[slot], self.line_three.at[slot], self.outer)

    def spend(self, stage, chunk):
        @pl.when(chunk >= self.slots)
        def _():
            pl.semaphore_wait(self.credit.at[self.first_stage + stage], 1)

    def repay(self, stage, where):
        pl.semaphore_signal(
            self.credit.at[self.first_stage + stage],
            inc=1,
            device_id=where,
            device_id_type=MESH,
        )

    def load(self, chunk, slot, begin):
        def one(source):
            copy = pltpu.make_async_copy(source, self.shard.at[slot], self.load_sem.at[slot])
            copy.start() if begin else copy.wait()

        self.sources(chunk, one)

    def loaded(self, chunk, slot):
        self.load(chunk, slot, False)
        self.enter(chunk, slot)

    def enter(self, chunk, slot):
        @pl.when(self.is_end)
        def _():
            self.spend(0, chunk)
            self.inward(slot).start()

    def second(self, chunk, slot):
        @pl.when(self.is_middle)
        def _():
            self.inward(slot).wait_recv()
            self.shard[slot] = add(self.shard[slot], self.line_one[slot])
            self.repay(0, self.outer)
            self.spend(1, chunk)
            self.crosswise(slot).start()

    def third(self, chunk, slot):
        @pl.when(self.is_middle)
        def _():
            self.crosswise(slot).wait()
            self.whole[slot] = add(self.shard[slot], self.line_two[slot])
            self.repay(1, self.across)
            self.spend(2, chunk)
            self.outward(slot).start()
            self.store(chunk, slot, self.whole, True)

    def last(self, chunk, slot):
        @pl.when(self.is_end)
        def _():
            self.inward(slot).wait_send()
            self.outward(slot).wait_recv()
            self.store(chunk, slot, self.line_three, True)

    def end(self, chunk, slot):
        @pl.when(self.is_end)
        def _():
            self.store(chunk, slot, self.line_three, False)
            self.repay(2, self.inner)

        @pl.when(self.is_middle)
        def _():
            self.store(chunk, slot, self.whole, False)
            self.outward(slot).wait_send()

    def store(self, chunk, slot, origin, begin):
        def one(target):
            copy = pltpu.make_async_copy(origin.at[slot], target, self.store_sem.at[slot])
            copy.start() if begin else copy.wait()

        self.targets(chunk, one)

    def drain(self):
        @pl.when(self.is_end)
        def _():
            pl.semaphore_wait(self.credit.at[self.first_stage], self.slots)

        @pl.when(self.is_middle)
        def _():
            pl.semaphore_wait(self.credit.at[self.first_stage + 1], self.slots)
            pl.semaphore_wait(self.credit.at[self.first_stage + 2], self.slots)


def pieces(lengths, chunk, body):
    low = 0
    for which, amount in enumerate(lengths):

        @pl.when((chunk >= low) & (chunk < low + amount))
        def _(low=low, which=which):
            body(which, chunk - low)

        low += amount


def tile_columns(at, width):
    return pl.ds(pl.multiple_of(at * width, width), width)


def sum_kernel(count, group, per, *refs):
    take = iter(refs)
    lefts = [next(take) for _ in range(count)]
    right_in = [next(take) for _ in range(count)]
    projection_in, residual_in, source_in, pick_in = [next(take) for _ in range(4)]
    parts = [next(take) for _ in range(2)]
    image_part, bias_part, scale_row = next(take), next(take), next(take)
    results = [next(take) for _ in range(count)]
    given, own_block = next(take), next(take)
    part_results = [next(take) for _ in range(2)]
    every_image, bias_total = next(take), next(take)
    units = next(take)
    rights = [next(take) for _ in range(count)]
    projection, residual, source, pick, both, spread, sums = [next(take) for _ in range(7)]
    grads, core_in, pair, upper_in, lower_in, upper_two, lower_two = [next(take) for _ in range(7)]
    main_buffers = [next(take) for _ in range(5)]
    tall_buffers = [next(take) for _ in range(5)]
    image_sum, image_in, bias_in, small_send, small_recv = [next(take) for _ in range(5)]
    send_sem, recv_sem, store_sem, load_sem, give_send, give_recv, in_sem, unit_sem, credit = take
    row = lax.axis_index("row")
    near_row, far_row = row + 1 - 2 * lax.rem(row, 2), lax.rem(row + 2, 4)
    main = Line(5, LINE_SLOTS, main_buffers, (send_sem, recv_sem, store_sem.at[0], credit))
    tall = Line(8, tall_buffers[0].shape[0], tall_buffers, (send_sem, recv_sem, store_sem.at[1], credit))
    tall.load_sem = load_sem
    across = [-(-right.shape[1] // TILE_COLUMNS) for right in rights]
    lengths = [left.shape[1] * amount for left, amount in zip(lefts, across)]
    chunks = sum(lengths)
    _, (core, x, y), (sibling, x_mate, y_mate) = mates()

    plan, low = [], 0
    for which, left in enumerate(lefts):
        for block in range(left.shape[1]):
            plan.append((low, which, block))
            low += across[which]

    def unit_copy(unit):
        _, which, block = plan[unit]
        origin = lefts[which].at[:, block]
        return pltpu.make_async_copy(origin, units.at[unit % 2], unit_sem.at[unit % 2])

    arrivals = [
        pltpu.make_async_copy(origin, target, in_sem.at[at])
        for at, (origin, target) in enumerate(
            [
                *zip(right_in, rights),
                (projection_in, projection),
                (residual_in, residual),
                (source_in, source),
                (pick_in, pick),
            ]
        )
    ]
    unit_copy(0).start()
    for at in (0, 3, 5, 6, 7, 8, 1, 2, 4):
        arrivals[at].start()

    def both_cuts(chunk, body):
        for parity, cut in enumerate(CUTS):

            @pl.when(lax.rem(chunk, 2) == parity)
            def _(cut=cut):
                body(pl.ds(0, cut), pl.ds(cut, TILE_ROWS - cut), cut)

    def main_targets(chunk, body):
        def one(which, at):
            result = results[which]
            columns = tile_columns(lax.rem(at, across[which]), TILE_COLUMNS)
            body(result.at[at // across[which], :, columns])

        pieces(lengths, chunk, one)

    main.targets = main_targets

    def side_tiles(line, origins, ends):
        amounts = [origin.shape[1] // LINE_TILE for origin in origins]

        def view(refs):
            def visit(chunk, body):
                def one(which, at):
                    body(refs[which].at[:, tile_columns(at, LINE_TILE)])

                pieces(amounts, chunk, one)

            return visit

        line.sources, line.targets = view(origins), view(ends)
        return sum(amounts)

    tall_tiles = side_tiles(tall, parts, part_results)

    def remote(stage, slot, source, target, where):
        return pltpu.make_async_remote_copy(
            src_ref=source,
            dst_ref=target,
            send_sem=send_sem.at[stage, slot],
            recv_sem=recv_sem.at[stage, slot],
            device_id={"img": where},
            device_id_type=MESH,
        )

    def to_sibling(slot):
        return remote(0, slot, grads.at[slot, :, :, 1 - core], core_in.at[slot], sibling)

    def upper_first(slot, rows):
        target = upper_in.at[slot, :, pl.ds(0, rows.size), :]
        return remote(1, slot, pair.at[slot, :, 1 - x, rows, :], target, x_mate)

    def lower_first(slot, rows):
        target = lower_in.at[slot, :, pl.ds(0, rows.size), :]
        return remote(2, slot, pair.at[slot, 1 - y, :, rows, :], target, y_mate)

    def upper_second(slot, rows):
        target = upper_two.at[slot, pl.ds(0, rows.size), :]
        return remote(3, slot, pair.at[slot, 1 - y, x, rows, :], target, y_mate)

    def lower_second(slot, rows):
        target = lower_two.at[slot, pl.ds(0, rows.size), :]
        return remote(4, slot, pair.at[slot, y, 1 - x, rows, :], target, x_mate)

    def spend(stage, chunk):
        @pl.when(chunk >= SLOTS)
        def _():
            pl.semaphore_wait(credit.at[stage], 1)

    def repay(stage, where):
        pl.semaphore_signal(
            credit.at[stage], inc=1, device_id={"img": where}, device_id_type=MESH
        )

    for mate in (sibling, x_mate, y_mate):
        greet({"img": mate})
    sender = Give(group, per, spread, given, give_send, give_recv)
    sender.greet()
    pl.semaphore_wait(pltpu.get_barrier_semaphore(), 6)

    def small(kind, source, target, where):
        return pltpu.make_async_remote_copy(
            src_ref=source,
            dst_ref=target,
            send_sem=small_send.at[kind],
            recv_sem=small_recv.at[kind],
            device_id=where,
            device_id_type=MESH,
        )

    own_half = pl.ds(2 * (row // 2), 2)
    image_hops = [
        (image_sum, image_in, {"img": sibling}),
        (every_image.at[row, y, x], every_image.at[row, y, x], {"img": y_mate}),
        (every_image.at[row, :, x], every_image.at[row, :, x], {"img": x_mate}),
        (every_image.at[row], every_image.at[row], {"row": near_row}),
        (every_image.at[own_half], every_image.at[own_half], {"row": far_row}),
    ]

    def small_hop(hop, begin):
        source, target, where = image_hops[hop]
        image = small(2 * hop, source, target, where)
        bias = small(2 * hop + 1, bias_total if hop else bias_part, bias_in.at[hop], where)
        if begin:
            image.start()
            bias.start()
            return
        image.wait()
        bias.wait()
        if hop == 0:
            summed = image_sum[...] + image_in[...]
            every_image[row, y, x] = summed.astype(jnp.bfloat16)
        bias_total[...] = (bias_total if hop else bias_part)[...] + bias_in[hop]

    def own_shard(chunk, slot):
        line_slot = lax.rem(chunk, LINE_SLOTS)

        def body(upper, lower, cut):
            upper_second(slot, upper).wait()
            main.shard[line_slot, upper, :] = add(
                pair[slot, y, x, upper, :], upper_two[slot, pl.ds(0, cut), :]
            )
            repay(3, y_mate)
            lower_second(slot, lower).wait()
            main.shard[line_slot, lower, :] = add(
                pair[slot, y, x, lower, :], lower_two[slot, pl.ds(0, TILE_ROWS - cut), :]
            )
            repay(4, x_mate)

        both_cuts(chunk, body)
        main.enter(chunk, line_slot)

    def second_axis(chunk, slot):
        def body(upper, lower, cut):
            upper_first(slot, upper).wait()
            for at in range(2):
                pair[slot, at, x, upper, :] = add(
                    pair[slot, at, x, upper, :], upper_in[slot, at, pl.ds(0, cut), :]
                )
            repay(1, x_mate)
            spend(3, chunk)
            upper_second(slot, upper).start()
            lower_first(slot, lower).wait()
            for at in range(2):
                pair[slot, y, at, lower, :] = add(
                    pair[slot, y, at, lower, :], lower_in[slot, at, pl.ds(0, TILE_ROWS - cut), :]
                )
            repay(2, y_mate)
            spend(4, chunk)
            lower_second(slot, lower).start()

        both_cuts(chunk, body)

    def first_axis(chunk, slot):
        to_sibling(slot).wait()
        for at_y in range(2):
            for at_x in range(2):
                pair[slot, at_y, at_x] = add(
                    grads[slot, at_y, at_x, core], core_in[slot, at_y, at_x]
                )
        repay(0, sibling)
        spend(1, chunk)
        spend(2, chunk)

        def body(upper, lower, cut):
            upper_first(slot, upper).start()
            lower_first(slot, lower).start()

        both_cuts(chunk, body)

    def multiply(chunk, slot):
        def one(which, at):
            right = rights[which]
            column, whole_tiles = lax.rem(at, across[which]), right.shape[1] // TILE_COLUMNS
            first_unit = [one_of for _, one_of, _ in plan].index(which)
            slot_of_unit = lax.rem(first_unit + at // across[which], 2)

            def times(values):
                for half in range(2):
                    rows = units[slot_of_unit, pl.ds(4 * half, 4)].reshape(4 * TILE_ROWS, -1)
                    product = jnp.dot(rows, values, preferred_element_type=jnp.float32)
                    grads[slot, half] = product.astype(jnp.bfloat16).reshape(
                        2, 2, TILE_ROWS, TILE_COLUMNS
                    )

            if whole_tiles == across[which]:
                times(right[:, tile_columns(column, TILE_COLUMNS)])
                return

            @pl.when(column < whole_tiles)
            def _():
                times(right[:, tile_columns(column, TILE_COLUMNS)])

            @pl.when(column == whole_tiles)
            def _():
                rest = right[:, whole_tiles * TILE_COLUMNS :]
                gap = jnp.zeros((rest.shape[0], TILE_COLUMNS - rest.shape[1]), rest.dtype)
                times(jnp.concatenate([rest, gap], axis=1))

        for unit, (begin, which, block) in enumerate(plan):

            @pl.when(chunk == begin)
            def _(unit=unit, which=which, block=block):
                unit_copy(unit).wait()
                if unit + 1 < len(plan):
                    unit_copy(unit + 1).start()
                if block == 0 and which != 3:
                    arrivals[which].wait()

        pieces(lengths, chunk, one)
        spend(0, chunk)
        to_sibling(slot).start()

    stages = [
        (LAST_LAG, LINE_SLOTS, main.end),
        (14, LINE_SLOTS, main.last),
        (11, LINE_SLOTS, main.third),
        (8, LINE_SLOTS, main.second),
        (5, SLOTS, own_shard),
        (3, SLOTS, second_axis),
        (1, SLOTS, first_axis),
        (0, SLOTS, multiply),
    ]

    def token_rows(at):
        rows = pl.ds(pl.multiple_of(at * TOKEN_ROWS, TOKEN_ROWS), TOKEN_ROWS)
        grad = lax.dot_general(
            rights[3][rows, :], projection[...], LAST, preferred_element_type=jnp.float32
        )
        tokens = source[rows, :].astype(jnp.float32)
        centre = tokens - jnp.mean(tokens, axis=-1, keepdims=True)
        spread_of = lax.rsqrt(jnp.mean(centre * centre, axis=-1, keepdims=True) + 1e-06)
        norm = centre * spread_of
        sums[0:1, :] += jnp.sum(grad, axis=0, keepdims=True)
        sums[1:2, :] += jnp.sum(grad * norm, axis=0, keepdims=True)
        grad = grad * (1.0 + scale_row[...])
        along = jnp.mean(grad * norm, axis=-1, keepdims=True)
        grad = spread_of * (grad - jnp.mean(grad, axis=-1, keepdims=True) - norm * along)
        both[core, rows, :] = (residual[rows, :] + grad).astype(jnp.bfloat16)

    token_blocks = 1 + source.shape[0] // TOKEN_ROWS
    lanes = source.shape[1] // 128
    swapped, handed = token_blocks + 2, token_blocks + 2 + 4 // AT_ONCE

    def token_swap():
        return small(10, both.at[core], both.at[core], {"img": sibling})

    def own_copy():
        return pltpu.make_async_copy(spread.at[0], own_block, in_sem.at[9])

    def tokens_step(at):
        @pl.when(at == 1)
        def _():
            for which in (3, 5, 6, 7):
                arrivals[which].wait()
            sums[...] = jnp.zeros_like(sums)

        @pl.when((at >= 1) & (at < token_blocks))
        def _():
            token_rows(at - 1)

        @pl.when(at == token_blocks)
        def _():
            token_swap().start()
            image_sum[...] = image_part[...]
            for which in range(2):
                for lane in range(lanes):
                    values = sums[which : which + 1, pl.ds(lane * 128, 128)]
                    image_sum[pl.ds(which * lanes + lane, 1), :] = values

        @pl.when(at == swapped)
        def _():
            token_swap().wait()
            arrivals[8].wait()

        @pl.when((at >= swapped) & (at < handed))
        def _():
            tokens = both[...].reshape(2 * both.shape[1], -1)
            for which in range(AT_ONCE):
                shift = AT_ONCE * (at - swapped) + which
                laid = jnp.dot(pick[shift], tokens, preferred_element_type=jnp.float32)
                spread[shift] = laid.astype(jnp.bfloat16)

        @pl.when(at == handed)
        def _():
            own_copy().start()

        @pl.when(at >= handed)
        def _():
            sender.trickle(at - handed, GIVE_ROWS)

    def step(at, carry):
        for hop in range(5):

            @pl.when(at == token_blocks + 1 + 4 * hop)
            def _(hop=hop):
                small_hop(hop, True)

            @pl.when(at == token_blocks + 4 + 4 * hop)
            def _(hop=hop):
                small_hop(hop, False)

        for lag, body in (
            (8, tall.end),
            (7, tall.last),
            (5, tall.third),
            (3, tall.second),
            (1, tall.loaded),
            (0, functools.partial(tall.load, begin=True)),
        ):
            for which in range(AT_ONCE):
                tile = AT_ONCE * (at - lag) + which

                @pl.when((at >= lag) & (tile < tall_tiles))
                def _(tile=tile, body=body):
                    body(tile, tile)

        for lag, slots, body in stages:
            chunk = at - lag

            @pl.when((chunk >= 0) & (chunk < chunks))
            def _(chunk=chunk, slots=slots, body=body):
                body(chunk, lax.rem(chunk, slots))

        tokens_step(at)
        return carry

    lax.fori_loop(0, chunks + LAST_LAG, step, 0)
    own_copy().wait()
    for stage in range(5):
        pl.semaphore_wait(credit.at[stage], SLOTS)
    for line in (main, tall):
        line.drain()
    sender.wait()


def turn(operand):
    blocks = operand.shape[1] // (8 * TILE_ROWS)
    return operand.T.reshape(8, blocks, TILE_ROWS, operand.shape[0])


def sum_gradients(lefts, rights, tokens_side, image_part, bias_part, scale_row, parts, group, per):
    bf16, f32 = jnp.bfloat16, jnp.float32
    projection, residual, source, pick = tokens_side
    length, width = source.shape
    image_rows, bias_rows = image_part.size // 128, bias_part.size // 128
    padded = -(-image_rows // 16) * 16
    image_part = jnp.pad(image_part.reshape(image_rows, 128), ((0, padded - image_rows), (0, 0)))
    bias_part = bias_part.reshape(bias_rows, 128)
    block = (pick.shape[1], width)
    shapes = [
        *[
            jax.ShapeDtypeStruct(
                (left.shape[1], TILE_ROWS, -(-right.shape[1] // TILE_COLUMNS) * TILE_COLUMNS), bf16
            )
            for left, right in zip(lefts, rights)
        ],
        jax.ShapeDtypeStruct((3, *block), bf16),
        jax.ShapeDtypeStruct(block, bf16),
        *[jax.ShapeDtypeStruct(part.shape, bf16) for part in parts],
        jax.ShapeDtypeStruct((4, 2, 2, padded, 128), bf16),
        jax.ShapeDtypeStruct((bias_rows, 128), f32),
    ]
    tile = (TILE_ROWS, TILE_COLUMNS)
    vmem, hbm = pl.BlockSpec(memory_space=pltpu.VMEM), pl.BlockSpec(memory_space=pl.ANY)
    flops = 2 * sum(left.size * right.shape[1] for left, right in zip(lefts, rights))
    tiles = sum(part.shape[1] // LINE_TILE for part in parts)
    most = max(LINE_SLOTS, tiles)
    results = pl.pallas_call(
        functools.partial(sum_kernel, len(lefts), group, per),
        in_specs=[hbm] * (2 * len(lefts) + 6) + [vmem] * 3,
        out_specs=[hbm] * (len(lefts) + 4) + [vmem] * 2,
        out_shape=shapes,
        scratch_shapes=[
            pltpu.VMEM((2, 8, TILE_ROWS, length), bf16),
            *[pltpu.VMEM(right.shape, bf16) for right in rights],
            pltpu.VMEM(projection.shape, bf16),
            pltpu.VMEM(residual.shape, f32),
            pltpu.VMEM(source.shape, bf16),
            pltpu.VMEM(pick.shape, bf16),
            pltpu.VMEM((2, length, width), bf16),
            pltpu.VMEM((4, *block), bf16),
            pltpu.VMEM((2, width), f32),
            pltpu.VMEM((SLOTS, 2, 2, 2, *tile), bf16),
            pltpu.VMEM((SLOTS, 2, 2, *tile), bf16),
            pltpu.VMEM((SLOTS, 2, 2, *tile), bf16),
            *[pltpu.VMEM((SLOTS, 2, max(CUTS), TILE_COLUMNS), bf16)] * 2,
            *[pltpu.VMEM((SLOTS, max(CUTS), TILE_COLUMNS), bf16)] * 2,
            *[pltpu.VMEM((LINE_SLOTS, *tile), bf16)] * 5,
            *[pltpu.VMEM((tiles, parts[0].shape[0], LINE_TILE), bf16)] * 5,
            pltpu.VMEM((padded, 128), f32),
            pltpu.VMEM((padded, 128), f32),
            pltpu.VMEM((5, bias_rows, 128), f32),
            pltpu.SemaphoreType.DMA((11,)),
            pltpu.SemaphoreType.DMA((11,)),
            pltpu.SemaphoreType.DMA((11, most)),
            pltpu.SemaphoreType.DMA((11, most)),
            pltpu.SemaphoreType.DMA((2, most)),
            pltpu.SemaphoreType.DMA((tiles,)),
            pltpu.SemaphoreType.DMA((3,)),
            pltpu.SemaphoreType.DMA((3,)),
            pltpu.SemaphoreType.DMA((10,)),
            pltpu.SemaphoreType.DMA((2,)),
            pltpu.SemaphoreType.REGULAR((11,)),
        ],
        compiler_params=pltpu.CompilerParams(
            collective_id=0, has_side_effects=True, vmem_limit_bytes=60 * 1024 * 1024
        ),
        cost_estimate=pl.CostEstimate(
            flops=flops, bytes_accessed=600000000, transcendentals=0
        ),
        name="sum_gradients",
    )(*lefts, *rights, *tokens_side, *parts, image_part, bias_part, scale_row)
    take = iter(results)
    summed = [next(take) for _ in lefts]
    summed = [
        result.reshape(-1, result.shape[2])[:, : right.shape[1]].astype(f32)
        for result, right in zip(summed, rights)
    ]
    given, own_block = next(take), next(take)
    parts = [next(take).astype(f32) for _ in parts]
    every_image, bias_total = take
    every_image = every_image[:, :, :, :image_rows].reshape(4, 4, -1).transpose(1, 0, 2)
    return summed, every_image.reshape(16, -1), bias_total.reshape(-1), [own_block, *given], parts


def local(
    n_img,
    n_row,
    tokens,
    cotangent,
    targets,
    time_table,
    ada_weight,
    ada_bias,
    qkv_weight,
    out_weight,
    up_weight,
    up_bias,
    down_weight,
    proj_first,
    proj_second,
    proj_third,
    time_bins,
    image_order,
    counts,
):
    f32, bf16 = jnp.float32, jnp.bfloat16
    per, slot_len, width = tokens.shape
    column = 2 * per
    group = n_row // column
    length = TOTAL // (2 * group)
    n_images = time_bins.shape[0]
    img_rank, row_rank = lax.axis_index("img"), lax.axis_index("row")
    core = img_rank % 2
    place = row_rank // group
    receives = place // per == core

    def swap(operand, axis, bit):
        size = n_img if axis == "img" else n_row
        return lax.ppermute(operand, axis, [(at, at ^ bit) for at in range(size)])

    def route(shift, back):
        pairs = [
            (img * n_row + (row + shift) % n_row, img * n_row + row)
            for img in range(n_img)
            for row in range(n_row)
            if (row // group) // per == img % 2
        ]
        return [(b, a) for a, b in pairs] if back else pairs

    own_counts = lax.dynamic_index_in_dim(counts, place % per, 0, keepdims=False)
    position = jnp.arange(slot_len)
    kept = (row_rank % group) * 2 * length + jnp.arange(2 * length)
    def make_pick(own_counts):
        first_of = (jnp.cumsum(own_counts) - own_counts) * RW
        picks = []
        for shift in range(n_row):
            source_row = (row_rank + shift) % n_row
            begin = lax.dynamic_index_in_dim(first_of, source_row, 0, keepdims=False)
            limit = lax.dynamic_index_in_dim(own_counts, source_row, 0, keepdims=False) * RW
            hit = (kept[None, :] == begin + position[:, None]) & (position[:, None] < limit)
            picks.append(hit)
        return jnp.concatenate(picks, axis=0).astype(bf16)

    def image_of(shift):
        return (((row_rank - shift) % n_row) // group) % per

    def bring(operand):
        pieces = []
        for shift in range(n_row):
            piece = lax.dynamic_index_in_dim(operand, image_of(shift), 0, keepdims=False)
            if shift:
                piece = lax.ppermute(piece, ("img", "row"), route(shift, False))
            pieces.append(piece)
        packed = weight_grad(pick, jnp.concatenate(pieces, axis=0)).astype(bf16)
        own = lax.dynamic_slice_in_dim(packed, core * length, length, 0)
        other = lax.dynamic_slice_in_dim(packed, (1 - core) * length, length, 0)
        return jnp.where(receives, own, swap(other, "img", 1))

    def give_start(operand, other):
        both = jnp.where(
            core == 0,
            jnp.concatenate([operand, other], axis=0),
            jnp.concatenate([other, operand], axis=0),
        )
        return matmul(pick, both).astype(bf16).reshape(n_row, slot_len, -1)

    def give_send(spread):
        sent = [
            lax.ppermute(spread[shift], ("img", "row"), route(shift, True))
            for shift in range(1, n_row)
        ]
        return [spread[0], *sent]

    def give_merge(blocks):
        images = [jnp.zeros_like(blocks[0]) for _ in range(per)]
        for shift, block in enumerate(blocks):
            sender = ((row_rank - shift) % n_row) // group
            for at in range(per):
                wanted = (sender // per == core) & (sender % per == at)
                if group > 1:
                    images[at] = images[at] + jnp.where(wanted, block, jnp.zeros_like(block))
                else:
                    images[at] = jnp.where(wanted, block, images[at])
        return jnp.stack(images)

    def fetch(operand):
        return lax.all_gather(operand, "img", axis=0, tiled=True)

    chip_bits = [1 << at for at in range(1, n_img.bit_length() - 1)]
    forth, back = chip_bits, chip_bits[-1:] + chip_bits[:-1]

    def side(bit):
        return (img_rank // bit) % 2

    def together(operand, bit, axis):
        blocks = jnp.stack([operand, swap(operand, "img", bit)], axis=axis)
        return jnp.where(side(bit) == 0, blocks, jnp.flip(blocks, axis=axis))

    def scattered(grad):
        return lax.psum_scatter(grad, "img", scatter_dimension=0, tiled=True)

    def offload_shards(left, right):
        return scattered(weight_grad(left, right).astype(bf16))

    def row_sum(part, turn_by):
        ranks = [(at + turn_by) % n_row for at in range(n_row)]
        return lax.psum(part, "row", axis_index_groups=[ranks]).astype(f32)

    fold = n_row // 4
    line_rank = row_rank // fold

    def over_row(part):
        def hop(operand, pairs):
            routes = [(a * fold + low, b * fold + low) for a, b in pairs for low in range(fold)]
            return lax.ppermute(operand, "row", routes)

        for at in range(fold.bit_length() - 1):
            part = (part.astype(f32) + swap(part, "row", 1 << at).astype(f32)).astype(bf16)
        part = (part.astype(f32) + hop(part, [(0, 1), (3, 2)]).astype(f32)).astype(bf16)
        part = (part.astype(f32) + hop(part, [(1, 2), (2, 1)]).astype(f32)).astype(bf16)
        outer = hop(part, [(1, 0), (2, 3)])
        return jnp.where((line_rank == 0) | (line_rank == 3), outer, part).astype(f32)

    order = image_order
    for bit in [1] + chip_bits:
        order = together(order, bit, 0).reshape(-1)
    chosen = jnp.sum(
        jnp.where(order[:, None] == jnp.arange(n_images)[None, :], time_bins[None, :], 0), axis=1
    )
    select = (chosen[:, None] == jnp.arange(time_table.shape[0])[None, :]).astype(f32)
    condition = jnp.dot(select, time_table.astype(f32), precision=lax.Precision.HIGHEST)
    silu_cond = jax.nn.silu(condition).astype(bf16)
    row_cond = lax.dynamic_index_in_dim(
        silu_cond.reshape(n_img // 2, column, -1), place, 1, keepdims=False
    )
    mod_width = ada_weight.shape[1]
    ff_width = up_weight.shape[1]
    bias_part = lax.dynamic_update_slice(
        jnp.zeros((mod_width,), f32), ada_bias.astype(f32), (img_rank * ada_bias.shape[0],)
    )
    up_bias_part = lax.dynamic_update_slice(
        jnp.zeros((ff_width,), f32), up_bias.astype(f32), (img_rank * up_bias.shape[0],)
    )
    mod_part = matmul(row_cond, ada_weight) + bias_part[None, :]
    small_plane = n_img == 8 and n_row == 4
    pick = None if small_plane else make_pick(own_counts)
    early = [qkv_weight, out_weight, proj_first]
    summed_rows = jnp.concatenate([mod_part.reshape(-1), up_bias_part])
    if small_plane:
        early, arrived, summed_rows = gather_weights(
            early, [tokens, cotangent, targets], summed_rows, group, per
        )
    else:
        early = [fetch(one) for one in early]
        for bit in [1] + chip_bits:
            summed_rows = summed_rows + swap(summed_rows, "img", bit)
    qkv_full, out_full, first_full = early
    modulation = lax.dynamic_index_in_dim(
        summed_rows[: (n_img // 2) * mod_width].reshape(n_img // 2, mod_width),
        img_rank // 2,
        0,
        keepdims=True,
    )
    up_bias_full = summed_rows[(n_img // 2) * mod_width :]
    up_full = fetch(up_weight)
    down_full = fetch(down_weight)
    second_full = fetch(proj_second)
    third_full = fetch(proj_third)

    shift_att, scale_att, gate_att, shift_mlp, scale_mlp, gate_mlp = jnp.split(
        modulation, 6, axis=1
    )
    if small_plane:
        image_counts = lax.dynamic_index_in_dim(together(counts, 1, 0).reshape(column, n_row), place, 0)
        ends = jnp.cumsum(image_counts[0])
        units = core * (length // RW) + jnp.arange(length // RW)
        origin = jnp.sum((units[:, None] >= ends[None, :]).astype(jnp.int32), axis=1)
        before = jnp.sum(
            jnp.where(origin[:, None] == jnp.arange(n_row), ends - image_counts[0], 0), axis=1
        )
        places = origin * slot_len + (units - before) * RW
        source, own_cotangent, own_targets, h_att = compact(
            places.astype(jnp.int32), arrived, shift_att, scale_att
        )
        source_rows, source = source, source.astype(f32)
        own_cotangent, own_targets = own_cotangent.astype(f32), own_targets.astype(f32)
    else:
        source = bring(tokens).astype(f32)
        own_cotangent, own_targets = bring(cotangent).astype(f32), bring(targets).astype(f32)
        h_att = modulate(source, shift_att, scale_att).astype(bf16)
    qkv_rows = matmul(h_att, qkv_full).astype(bf16)
    bits = [1 << at for at in range(group.bit_length() - 1)]
    if small_plane:
        head_mix, log_total, rest = attend(qkv_rows, None, width)
    else:
        rest = swap(qkv_rows[:, width:], "img", 1)
        for bit in bits:
            near = jnp.concatenate([qkv_rows[:, width:], rest], axis=0)
            rest = jnp.concatenate([rest, swap(near, "row", bit)], axis=0)
        head_mix, log_total = attend(qkv_rows, rest, width)
    attn_out = matmul(head_mix, out_full)
    residual = source + gate_att * attn_out
    h_mlp = modulate(residual, shift_mlp, scale_mlp).astype(bf16)
    pre_act = matmul(h_mlp, up_full) + up_bias_full
    gelu_out = gelu_tanh(pre_act).astype(bf16)
    mlp_out = matmul(gelu_out, down_full)
    lefts = [gelu_out, h_mlp, head_mix, h_att]
    if small_plane:
        lefts = [turn(left) for left in lefts]
        lefts, mlp_out = lax.optimization_barrier((lefts, mlp_out))
    block_own = (residual + gate_mlp * mlp_out).astype(bf16)
    lin_one = matmul(block_own, first_full)
    hid_one = jax.nn.silu(lin_one).astype(bf16)
    left_first = turn(block_own) if small_plane else block_own
    if small_plane:
        own_counts, block_own = lax.optimization_barrier((own_counts, block_own))
        pick = make_pick(own_counts)
    block_spread = give_start(block_own, swap(block_own, "img", 1))
    tied = lax.optimization_barrier((block_spread, left_first, hid_one))
    block_spread, left_first, hid_one = tied
    lin_two = matmul(hid_one, second_full)
    hid_two = jax.nn.silu(lin_two).astype(bf16)
    projected = matmul(hid_two, third_full)

    def align_loss(operand):
        return -0.5 * jnp.sum(alignment(operand, own_targets))

    d_proj = jax.vjp(align_loss, projected)[1](jnp.ones((), f32))[0].astype(bf16)
    third_sum = weight_grad(hid_two, d_proj).astype(bf16)
    third_sum, d_proj = lax.optimization_barrier((third_sum, d_proj))
    third_part = scattered(third_sum)
    d_lin_two = silu_back(lin_two, transposed(d_proj, third_full)).astype(bf16)
    second_sum = weight_grad(hid_one, d_lin_two).astype(bf16)
    second_sum, d_lin_two = lax.optimization_barrier((second_sum, d_lin_two))
    second_part = scattered(second_sum)
    d_lin_one = silu_back(lin_one, transposed(d_lin_two, second_full)).astype(bf16)
    d_res = own_cotangent + transposed(d_lin_one, first_full)
    d_gate_mlp = jnp.sum(d_res * mlp_out, axis=0)
    d_mlp = (d_res * gate_mlp).astype(bf16)
    d_pre = gelu_back(pre_act, transposed(d_mlp, down_full)).astype(bf16)
    bias_sum = jnp.sum(d_pre.astype(f32), axis=0)
    d_resid_norm, d_shift_mlp, d_scale_mlp = jax.vjp(modulate, residual, shift_mlp, scale_mlp)[1](
        transposed(d_pre, up_full)
    )
    d_residual = d_res + d_resid_norm
    d_gate_att = jnp.sum(d_residual * attn_out, axis=0)
    d_attn = (d_residual * gate_att).astype(bf16)
    d_mixed = transposed(d_attn, out_full).astype(bf16)
    third_part, d_mixed = lax.optimization_barrier((third_part, d_mixed))
    d_qkv, d_other = attend_back(
        qkv_rows,
        rest,
        head_mix,
        d_mixed,
        log_total,
        block_spread,
        (group, per) if small_plane else None,
    )
    if small_plane:
        block_out = give_merge([block_spread[0], *d_other])
    else:
        block_out = give_merge(give_send(block_spread))
        d_own, d_rest = d_qkv[:, width:].astype(f32), d_other
        for bit in reversed(bits):
            full = jnp.concatenate([d_own, d_rest.astype(f32)], axis=0)
            half = full.shape[0] // 2
            full = full[:half] + swap(full[half:].astype(bf16), "row", bit).astype(f32)
            d_own, d_rest = full[:length], full[length:].astype(bf16)
        d_own = d_own + swap(d_rest, "img", 1).astype(f32)
        d_qkv = jnp.concatenate([d_qkv[:, :width], d_own.astype(bf16)], axis=1)
    second_part, d_qkv = lax.optimization_barrier((second_part, d_qkv))
    late_mod = jnp.concatenate([d_gate_att, d_shift_mlp[0], d_scale_mlp[0], d_gate_mlp])
    lefts.append(left_first)
    rights = [d_mlp, d_pre, d_attn, d_qkv, d_lin_one]
    proj_parts = [second_part, third_part]
    if small_plane:
        tied = (proj_parts, rights, d_residual, late_mod, bias_sum)
        proj_parts, rights, d_residual, late_mod, bias_sum = lax.optimization_barrier(tied)
        large, d_mod, bias_sum, blocks, proj_grads = sum_gradients(
            lefts,
            rights,
            (qkv_full, d_residual, source_rows, pick.reshape(n_row, slot_len, -1)),
            jnp.concatenate([jnp.zeros((2 * width,), f32), late_mod]),
            bias_sum,
            scale_att,
            proj_parts,
            group,
            per,
        )
        grad_tokens = give_merge(blocks)
    else:
        d_source, d_shift_att, d_scale_att = jax.vjp(modulate, source, shift_att, scale_att)[1](
            transposed(d_qkv, qkv_full)
        )
        tokens_own = (d_residual + d_source).astype(bf16)
        grad_tokens = give_merge(give_send(give_start(tokens_own, swap(tokens_own, "img", 1))))
        proj_grads = [row_sum(part, at) for at, part in enumerate(proj_parts)]
        large = [over_row(offload_shards(*pair)) for pair in zip(lefts, rights)]
        own_mod = jnp.concatenate([d_shift_att[0], d_scale_att[0], late_mod])
        slot_id = column * (img_rank // 2) + place
        placed = jnp.zeros((n_images, mod_width), f32)
        placed = lax.dynamic_update_slice(placed, own_mod[None, :], (slot_id, 0))
        d_mod, bias_sum = lax.psum((placed, bias_sum), ("img", "row"))
        d_mod = d_mod.astype(bf16)
    grad_second, grad_third = proj_grads
    grad_down, grad_up, grad_out, grad_qkv, grad_first = large

    grad_ada = weight_grad(silu_cond, d_mod)
    grad_ada_bias = jnp.sum(
        lax.dynamic_slice_in_dim(d_mod, img_rank * ada_bias.shape[0], ada_bias.shape[0], 1).astype(
            f32
        ),
        axis=0,
    )
    d_cond = silu_back(condition, transposed(d_mod, ada_weight))
    grad_table = jnp.dot(select.T, d_cond, precision=lax.Precision.HIGHEST)
    grad_up_bias = lax.dynamic_index_in_dim(
        bias_sum.reshape(n_img, -1), img_rank, 0, keepdims=False
    )
    return (
        block_out,
        grad_tokens,
        grad_table,
        grad_ada,
        grad_ada_bias,
        grad_qkv,
        grad_out,
        grad_up,
        grad_up_bias,
        grad_down,
        grad_first,
        grad_second,
        grad_third,
    )


def solution(mesh):
    return jax.shard_map(
        functools.partial(local, mesh.shape["img"], mesh.shape["row"]),
        mesh=mesh,
        in_specs=(
            P("img", "row", None),
            P("img", "row", None),
            P("img", "row", None),
            P(None, "img"),
            P("img", None),
            P("img"),
            P("img", None),
            P("img", None),
            P("img", None),
            P("img"),
            P("img", None),
            P("img", None),
            P("img", None),
            P("img", None),
            P(),
            P("img"),
            P("img", None),
        ),
        out_specs=(
            P("img", "row", None),
            P("img", "row", None),
            P(None, "img"),
            P("img", None),
            P("img"),
            P("img", None),
            P("img", None),
            P("img", None),
            P("img"),
            P("img", None),
            P("img", None),
            P("img", None),
            P("img", None),
        ),
        check_vma=False,
    )
```
